128 devices in a mesh: lat: 8 (over x, y_lo), lon: 16 (over z, y_hi, core).
Axes of the slice: x: 4, y: 4 (y_hi: 2, y_lo: 2; y = y_hi * 2 + y_lo), z: 4, core: 2. Of those that a mesh axis runs over, the one named last changes fastest.
Arguments:
- tokens: bfloat16 [2, 96, 384, 512], P(None, 'lat', 'lon'), may hold values from -6 to 6
- land_sea: int32 [96, 384], P('lat', 'lon'), may hold values 0 or 1
- land_vec: bfloat16 [512], replicated, may hold values from -4 to 4
- fine_gain: bfloat16 [512], replicated, may hold values from 0.5 to 1.5
- fine_qkv: bfloat16 [512, 1536], replicated, may hold values from -2 to 2
- fine_proj: bfloat16 [512, 512], replicated, may hold values from -0.25 to 0.25
- merge_gain: bfloat16 [2048], replicated, may hold values from 0.5 to 1.5
- merge_weight: bfloat16 [2048, 1024], replicated, may hold values from -0.125 to 0.125
- coarse_gain: bfloat16 [1024], replicated, may hold values from 0.5 to 1.5
- coarse_qkv: bfloat16 [1024, 3072], replicated, may hold values from -2 to 2
- coarse_proj: bfloat16 [1024, 1024], replicated, may hold values from -0.1875 to 0.1875
- cotangent: bfloat16 [2, 48, 192, 1024], P(None, 'lat', 'lon'), may hold values from -6 to 6
Outputs:
- coarse_out: bfloat16 [2, 48, 192, 1024], P(None, 'lat', 'lon')
- grad_tokens: bfloat16 [2, 96, 384, 512], P(None, 'lat', 'lon')
- fine_grads: float32 [512, 2048], P('lat', 'lon')
The draws below stay inside these ranges and needn't reach their ends.
All inputs are finite; a program needn't handle non-finite values. No bound on the sum of `land_sea` on one device may be relied on, other than what follows from the above.
Results may differ from the reference program's by a relative error of at most 0.03.
Values may be sent and summed in bfloat16 or wider, within the bound.
No kernel may reach another device: no remote copies, remote signals or barrier semaphores. Data moves between devices by JAX's collectives and lax.ppermute only.
A program may use at most 128 MiB of HBM per device.

```python
import math
import jax
import jax.numpy as jnp
from jax import lax

D = 512
DC = 1024
HEADS = 8
HEADS_C = 16
LEV = 2
WLAT = 6
WLON = 12
NLAT = 96
NLON = 384


def projection_draw(key, width, heads, strength):
    base_key, common_key, head_key = jax.random.split(key, 3)
    base = jax.random.truncated_normal(base_key, -3.0, 3.0, (width, 3 * width), jnp.float32)
    common = jax.random.truncated_normal(common_key, -3.0, 3.0, (width, width), jnp.float32)
    level = jax.random.uniform(head_key, (heads,), jnp.float32, 0.2, 1.0) * strength
    level = jnp.repeat(level, width // heads)
    shared = common * level[None, :]
    extra = jnp.concatenate([shared, shared, jnp.zeros((width, width), jnp.float32)], axis=1)
    return ((base + extra) * width ** (-0.5)).astype(jnp.bfloat16)


def draw_fine_qkv(key, part):
    key = jax.random.fold_in(key, 11)
    return projection_draw(key, D, HEADS, 0.0)


def draw_coarse_qkv(key, part):
    key = jax.random.fold_in(key, 23)
    return projection_draw(key, DC, HEADS_C, 0.0)


def touch_ends(drawn, own_key, low, top_value):
    extent = drawn.shape
    place = [jax.random.randint(jax.random.fold_in(own_key, axis), (), 0, extent[axis]) for axis in range(len(extent))]
    drawn = drawn.at[tuple(place)].set(low)
    longest = extent.index(max(extent))
    place[longest] = (place[longest] + 1) % extent[longest]
    return drawn.at[tuple(place)].set(top_value)


def shard_levels(rng, shape, cuts, low, largest):
    loudness, own = 1.0, jax.random.fold_in(rng, 6)
    for dim, blocks in cuts:
        steps = jnp.exp(jax.random.uniform(jax.random.fold_in(own, dim), (blocks,), jnp.float32, low / len(cuts), largest / len(cuts)))
        loudness = loudness * jnp.repeat(steps, shape[dim] // blocks).reshape([-1 if axis == dim else 1 for axis in range(len(shape))])
    return loudness


def gaussian(stream_key, extent, scale, most, cuts=(), held_as=jnp.bfloat16):
    values = jax.random.normal(stream_key, extent, jnp.float32) * scale
    if len(cuts) > 0:
        values = shard_levels(stream_key, extent, cuts, -0.22, 0.18) * values
    return jnp.clip(values, min=-most, max=most).astype(held_as)


def setup_inputs(seed: int = 0) -> dict:
    key_of = jax.random.split(jax.random.key(seed), 13)
    return {
        "tokens": gaussian(key_of[0], (LEV, NLAT, NLON, D), 1.0, 6.0, ((1, 8), (2, 16))),
        "land_sea": touch_ends((jax.random.randint(key_of[1], (NLAT, NLON), 0, 3) < 1).astype(jnp.int32), jax.random.fold_in(key_of[1], 1), 0, 1),
        "land_vec": gaussian(key_of[2], (D,), 1.0, 4.0),
        "fine_gain": jnp.clip(jax.random.uniform(key_of[3], (D,), jnp.float32, 0.5, 1.5), 0.5, 1.5).astype(jnp.bfloat16),
        "fine_qkv": draw_fine_qkv(jax.random.fold_in(key_of[12], 71), 0),
        "fine_proj": gaussian(key_of[5], (D, D), D ** -0.5, 0.25),
        "merge_gain": jnp.clip(jax.random.uniform(key_of[6], (4 * D,), jnp.float32, 0.5, 1.5), 0.5, 1.5).astype(jnp.bfloat16),
        "merge_weight": gaussian(key_of[7], (4 * D, DC), (4 * D) ** -0.5, 0.125),
        "coarse_gain": jnp.clip(jax.random.uniform(key_of[8], (DC,), jnp.float32, 0.5, 1.5), 0.5, 1.5).astype(jnp.bfloat16),
        "coarse_qkv": draw_coarse_qkv(jax.random.fold_in(key_of[12], 71), 0),
        "coarse_proj": gaussian(key_of[10], (DC, DC), DC ** -0.5, 0.1875),
        "cotangent": gaussian(key_of[11], (LEV, NLAT // 2, NLON // 2, DC), 1.0, 6.0, ((1, 8), (2, 16))),
    }


EPSILON = 1e-05

def normalize(values, gain):
    wide = values.astype(jnp.float32)
    centre = lax.optimization_barrier(jnp.mean(wide, axis=-1, keepdims=True))
    spread = lax.optimization_barrier(jnp.mean(jnp.square(wide - centre), axis=-1, keepdims=True))
    return ((wide - centre) * lax.rsqrt(spread + EPSILON) * gain.astype(jnp.float32)).astype(jnp.bfloat16)

def times_transposed(left, weight):
    return lax.dot_general(left, weight, (((left.ndim - 1,), (1,)), ((), ())), preferred_element_type=jnp.float32)

def to_windows(values):
    levels, rows, cols, feat = values.shape
    blocks = values.reshape(levels, rows // WLAT, WLAT, cols // WLON, WLON, feat)
    return blocks.transpose(1, 3, 0, 2, 4, 5).reshape(-1, levels * WLAT * WLON, feat)

def from_windows(values, levels, rows, cols):
    feat = values.shape[-1]
    blocks = values.reshape(rows // WLAT, cols // WLON, levels, WLAT, WLON, feat)
    return blocks.transpose(2, 0, 3, 1, 4, 5).reshape(levels, rows, cols, feat)

def attend(qkv, region, heads):
    count, length, triple = qkv.shape
    width = triple // 3
    parts = qkv.astype(jnp.float32).reshape(count, length, 3, heads, width // heads)
    query, keys, vals = (parts[:, :, 0], parts[:, :, 1], parts[:, :, 2])
    scores = jnp.einsum('wqhd,wkhd->whqk', query, keys) * (width // heads) ** (-0.5)
    same = (region[:, :, None] == region[:, None, :])[:, None]
    scores = jnp.where(same, scores, -1e+30)
    top = lax.optimization_barrier(jnp.max(scores, axis=-1, keepdims=True))
    raised = jnp.exp(scores - top)
    probs = (raised / lax.optimization_barrier(jnp.sum(raised, axis=-1, keepdims=True))).astype(jnp.bfloat16)
    mixed = jnp.einsum('whqk,wkhd->wqhd', probs.astype(jnp.float32), vals)
    return mixed.reshape(count, length, width).astype(jnp.bfloat16)

def attend_mapped(qkv_win, region_win, heads, groups):
    shaped = qkv_win.reshape(groups, -1, qkv_win.shape[1], qkv_win.shape[2])
    marks = region_win.reshape(groups, -1, region_win.shape[1])
    result = lax.map(lambda pair: attend(pair[0], pair[1], heads), (shaped, marks))
    return result.reshape(qkv_win.shape[0], qkv_win.shape[1], -1)

def attend_grad_mapped(qkv_win, region_win, d_win, heads, groups):
    shaped = qkv_win.reshape(groups, -1, qkv_win.shape[1], qkv_win.shape[2])
    marks = region_win.reshape(groups, -1, region_win.shape[1])
    d_shaped = d_win.reshape(groups, -1, d_win.shape[1], d_win.shape[2])

    def one_group(triple):
        return jax.vjp(lambda t: attend(t, triple[1], heads), triple[0])[1](triple[2])[0]
    result = lax.map(one_group, (shaped, marks, d_shaped))
    return result.reshape(qkv_win.shape)

def shift_grid(values, sign):
    return jnp.roll(values, (sign * (WLAT // 2), sign * (WLON // 2)), axis=(1, 2))

def region_full(levels, rows, cols):
    flag = (jnp.arange(rows) >= rows - WLAT // 2).astype(jnp.int32)
    return jnp.broadcast_to(flag[None, :, None], (levels, rows, cols))

def layer_forward(inside, gain, w_qkv, w_proj, heads):
    levels, rows, cols, width = inside.shape
    normed = normalize(inside, gain)
    qkv = jnp.dot(normed, w_qkv, preferred_element_type=jnp.float32).astype(jnp.bfloat16)
    qkv_win = to_windows(qkv)
    region_win = to_windows(region_full(levels, rows, cols)[..., None])[..., 0]
    mixed = from_windows(attend_mapped(qkv_win, region_win, heads, rows // WLAT), levels, rows, cols)
    result = (inside.astype(jnp.float32) + jnp.dot(mixed, w_proj, preferred_element_type=jnp.float32)).astype(jnp.bfloat16)
    return (result, (normed, qkv_win, region_win, mixed))

def layer_backward(d_result, inside, gain, w_qkv, w_proj, saved, heads):
    normed, qkv_win, region_win, mixed = saved
    levels, rows, cols, width = inside.shape
    d_mixed = times_transposed(d_result, w_proj).astype(jnp.bfloat16)
    d_qkv_win = attend_grad_mapped(qkv_win, region_win, to_windows(d_mixed), heads, rows // WLAT)
    d_qkv = from_windows(d_qkv_win, levels, rows, cols)
    d_normed = times_transposed(d_qkv, w_qkv).astype(jnp.bfloat16)
    d_norm_in = jax.vjp(lambda t: normalize(t, gain), inside)[1](d_normed)[0]
    d_inside = (d_result.astype(jnp.float32) + d_norm_in.astype(jnp.float32)).astype(jnp.bfloat16)
    return (d_inside, d_qkv)

def merge_patches(values):
    levels, rows, cols, width = values.shape
    blocks = values.reshape(levels, rows // 2, 2, cols // 2, 2, width).transpose(0, 1, 3, 4, 2, 5)
    return blocks.reshape(levels, rows // 2, cols // 2, 4 * width)

def split_patches(values):
    levels, rows, cols, wide = values.shape
    width = wide // 4
    blocks = values.reshape(levels, rows, cols, 2, 2, width).transpose(0, 1, 4, 2, 3, 5)
    return blocks.reshape(levels, 2 * rows, 2 * cols, width)

def contract_tokens(left, right):
    flat_left = left.reshape(-1, left.shape[-1])
    flat_right = right.reshape(-1, right.shape[-1])
    return jnp.dot(flat_left.T, flat_right, preferred_element_type=jnp.float32)

def reference(tokens, land_sea, land_vec, fine_gain, fine_qkv, fine_proj, merge_gain, merge_weight, coarse_gain, coarse_qkv, coarse_proj, cotangent):
    land = land_sea.astype(jnp.float32)[None, :, :, None]
    stream = (tokens.astype(jnp.float32) + land * land_vec.astype(jnp.float32)).astype(jnp.bfloat16)
    fine_in = shift_grid(stream, -1)
    fine_mid, fine_saved = layer_forward(fine_in, fine_gain, fine_qkv, fine_proj, HEADS)
    fine_out = shift_grid(fine_mid, 1)
    merged = merge_patches(fine_out)
    merge_normed = normalize(merged, merge_gain)
    coarse_in = jnp.dot(merge_normed, merge_weight, preferred_element_type=jnp.float32).astype(jnp.bfloat16)
    coarse_inside = shift_grid(coarse_in, -1)
    coarse_mid, coarse_saved = layer_forward(coarse_inside, coarse_gain, coarse_qkv, coarse_proj, HEADS_C)
    coarse_out = shift_grid(coarse_mid, 1)
    d_coarse_mid = shift_grid(cotangent, -1)
    d_coarse_inside, unused = layer_backward(d_coarse_mid, coarse_inside, coarse_gain, coarse_qkv, coarse_proj, coarse_saved, HEADS_C)
    d_coarse_in = shift_grid(d_coarse_inside, 1)
    d_merge_normed = times_transposed(d_coarse_in, merge_weight).astype(jnp.bfloat16)
    d_merged = jax.vjp(lambda t: normalize(t, merge_gain), merged)[1](d_merge_normed)[0]
    d_fine_mid = shift_grid(split_patches(d_merged), -1)
    d_fine_in, d_qkv = layer_backward(d_fine_mid, fine_in, fine_gain, fine_qkv, fine_proj, fine_saved, HEADS)
    grad_tokens = shift_grid(d_fine_in, 1)
    scale = 1.0 / math.sqrt(LEV * NLAT * NLON)
    grad_qkv = contract_tokens(fine_saved[0], d_qkv)
    grad_proj = contract_tokens(fine_saved[3], d_fine_mid)
    fine_grads = jnp.concatenate([grad_qkv, grad_proj], axis=1) * scale
    return (coarse_out, grad_tokens, fine_grads)
```

```python
import math

import jax
import jax.numpy as jnp
import numpy as np
from jax import lax
from jax.experimental import pallas as pl
from jax.experimental.pallas import tpu as pltpu
from jax.sharding import PartitionSpec as P

F32 = jnp.float32
BF16 = jnp.bfloat16
EPSILON = 1e-05
NEG = -1e30

QUADS = ((0, 0), (1, 0), (0, 1), (1, 1))
QROWS = 352
SROWS = QROWS + 96
PIECES = ((0, 144), (144, 80), (224, 80), (304, 48))
EXT = 1408
QRY = 768
CRS = 192

E_OFF = {
    0: (0, 576, 896, 1216),
    1: (144, 736, 976, 1312),
    2: (288, 656, 1056, 1264),
    3: (432, 816, 1136, 1360),
}
Q_OFF = {
    0: (0, 192, 384, 576),
    1: (48, 288, 432, 672),
    2: (96, 240, 480, 624),
    3: (144, 336, 528, 720),
}
CORDER = (0, 2, 1, 3)
C_OFF = {quad: 48 * place for place, quad in enumerate(CORDER)}

WINDOWS = (
    (0, 144, 0, 48, 0),
    (144, 144, 48, 48, 0),
    (288, 144, 96, 48, 0),
    (432, 144, 144, 48, 0),
    (576, 160, 192, 96, 1),
    (736, 160, 288, 96, 1),
    (896, 160, 384, 96, 2),
    (1056, 160, 480, 96, 2),
    (1216, 192, 576, 192, 3),
)


def piece_cells(quad):
    qr, qc = QUADS[quad]
    near_r, far_r, mid_r = ((1, 0, 2), (4, 5, 3))[qr]
    near_c, far_c, mid_c = ((1, 0, 2), (4, 5, 3))[qc]
    return (
        ((near_r, near_c), (near_r, far_c), (far_r, near_c), (far_r, far_c)),
        ((near_r, mid_c), (far_r, mid_c)),
        ((mid_r, near_c), (mid_r, far_c)),
        ((mid_r, mid_c),),
    )


def build_tables():
    pick = np.zeros((4, QROWS, 576), np.float32)
    cell_query = {}
    for quad in range(4):
        qr, qc = QUADS[quad]
        for (start, _), cells, q_off in zip(PIECES, piece_cells(quad), Q_OFF[quad]):
            cell_query[cells[0]] = q_off
            for number, (cr, cc) in enumerate(cells):
                for lev in range(2):
                    for i in range(3):
                        for j in range(6):
                            row = 3 * cr + i + 3 - 12 * qr
                            col = 6 * cc + j + 6 - 24 * qc
                            place = start + 36 * number + lev * 18 + i * 6 + j
                            pick[quad, place, lev * 288 + row * 24 + col] = 1
    cpick = np.zeros((4, 48, CRS), np.float32)
    merge = np.zeros((4, CRS, QRY), np.float32)
    for quad in range(4):
        qr, qc = QUADS[quad]
        for lev in range(2):
            for i in range(3):
                for j in range(6):
                    place = lev * 18 + i * 6 + j
                    row = i + 3 * (1 - qr)
                    col = j + 6 * (1 - qc)
                    cpick[quad, place, (lev * 6 + row) * 16 + col] = 1
                    for k, (di, dj) in enumerate(((0, 0), (1, 0), (0, 1), (1, 1))):
                        er = 3 + 2 * (3 * qr + i) + di
                        ec = 6 + 2 * (6 * qc + j) + dj
                        spot = cell_query[(er // 3, ec // 6)] + lev * 18 + (er % 3) * 6 + ec % 6
                        merge[k, C_OFF[quad] + place, spot] = 1
    return pick, cpick, merge


PICK, CPICK, MERGE = build_tables()


def nn(left, right):
    return jnp.dot(left, right, preferred_element_type=F32)


def nt(left, right):
    return lax.dot_general(left, right, (((1,), (1,)), ((), ())), preferred_element_type=F32)


def tn(left, right):
    return lax.dot_general(left, right, (((0,), (0,)), ((), ())), preferred_element_type=F32)


def prep_kernel(tok_ref, land_ref, vec_ref, cot_ref, pick_ref, cpick_ref, out_ref, slab):
    land = land_ref[...]
    stream = (tok_ref[...].astype(F32) + land * vec_ref[...].astype(F32)).astype(BF16)
    slab[...] = jnp.zeros_like(slab)
    for lev in range(2):
        for row in range(6):
            slab[lev * 6 + row, 0:12, :] = cot_ref[lev, row]
    cot = slab[...].reshape(CRS, 1024)
    for quad in range(4):
        out_ref[quad, 0:QROWS, :] = nn(pick_ref[quad], stream).astype(BF16)
        picked = nn(cpick_ref[quad], cot).astype(BF16)
        out_ref[quad, QROWS : QROWS + 48, :] = picked[:, 0:512]
        out_ref[quad, QROWS + 48 : SROWS, :] = picked[:, 512:1024]


def prep(tokens, land, vec, cot, pick, cpick):
    return pl.pallas_call(
        prep_kernel,
        out_shape=jax.ShapeDtypeStruct((4, SROWS, 512), BF16),
        scratch_shapes=[pltpu.VMEM((12, 16, 1024), BF16)],
        compiler_params=pltpu.CompilerParams(vmem_limit_bytes=48 * 2**20),
    )(tokens, land, vec, cot, pick, cpick)


def finish_kernel(own_ref, one_ref, two_ref, three_ref, pick_ref, cpick_ref, grad_ref, coarse_ref):
    total = None
    crs = None
    for quad, ref in enumerate((own_ref, one_ref, two_ref, three_ref)):
        term = nn(pick_ref[quad], ref[0:QROWS, :])
        total = term if total is None else total + term
        wide = jnp.concatenate([ref[QROWS : QROWS + 48, :], ref[QROWS + 48 : SROWS, :]], axis=1)
        cterm = nn(cpick_ref[quad], wide)
        crs = cterm if crs is None else crs + cterm
    grad_ref[...] = total.astype(BF16)
    slabs = crs.astype(BF16).reshape(12, 16, 1024)
    for lev in range(2):
        for row in range(6):
            coarse_ref[lev, row] = slabs[lev * 6 + row, 0:12, :]


def finish(own, one, two, three, pick_t, cpick_t):
    return pl.pallas_call(
        finish_kernel,
        out_shape=(
            jax.ShapeDtypeStruct((576, 512), BF16),
            jax.ShapeDtypeStruct((2, 6, 12, 1024), BF16),
        ),
        compiler_params=pltpu.CompilerParams(vmem_limit_bytes=48 * 2**20),
    )(own, one, two, three, pick_t, cpick_t)


def norm_rows(values, gain):
    wide = values.astype(F32)
    centre = jnp.mean(wide, axis=-1, keepdims=True)
    moved = wide - centre
    scale = lax.rsqrt(jnp.mean(moved * moved, axis=-1, keepdims=True) + EPSILON)
    return (moved * scale * gain).astype(BF16), centre, scale


def norm_back(values, gain, centre, scale, d_normed):
    hat = (values.astype(F32) - centre) * scale
    weighted = d_normed * gain
    first = jnp.mean(weighted, axis=-1, keepdims=True)
    second = jnp.mean(weighted * hat, axis=-1, keepdims=True)
    return scale * (weighted - first - hat * second)


def lane_masks(rows):
    lane = lax.broadcasted_iota(jnp.int32, (rows, 128), 1)
    return lane < 64


def stacked(values):
    low = lane_masks(values.shape[0])
    zero = jnp.zeros_like(values)
    return jnp.concatenate([jnp.where(low, values, zero), jnp.where(low, zero, values)], axis=0)


def unstacked(values):
    half = values.shape[0] // 2
    return jnp.where(lane_masks(half), values[:half], values[half:])


def attend_pair(query, keys, vals, bias):
    scores = nt(stacked(query), keys)
    if bias is not None:
        scores = scores + bias
    raised = jnp.exp(scores - jnp.max(scores, axis=-1, keepdims=True)).astype(BF16)
    wide = nn(raised, jnp.concatenate([vals, jnp.ones_like(vals)], axis=1))
    inverse = 1.0 / wide[:, 128:]
    return raised, inverse, unstacked(wide[:, :128] * inverse)


def attend_back(query, keys, vals, raised, inverse, mixed, d_mixed):
    d_scaled = stacked(d_mixed).astype(F32) * inverse
    d_short = d_scaled.astype(BF16)
    twice = jnp.concatenate([mixed, mixed], axis=0).astype(F32)
    delta = jnp.sum(d_scaled * twice, axis=-1, keepdims=True)
    d_probs = nt(d_short, vals)
    d_scores = (raised.astype(F32) * (d_probs - delta)).astype(BF16)
    d_query = unstacked(nn(d_scores, keys)) * 0.125
    d_keys = tn(d_scores, stacked(query))
    d_vals = tn(raised, d_short)
    return d_query, d_keys, d_vals


def pair_slice(start, pair):
    return pl.ds(pl.multiple_of(start + pair * 128, 128), 128)


def main_kernel(
    place_ref,
    q0_ref,
    q1_ref,
    q2_ref,
    q3_ref,
    fgain_ref,
    mgain_ref,
    cgain_ref,
    fqkv_hbm,
    fproj_hbm,
    merge_hbm,
    merge_t_hbm,
    mw_hbm,
    cqkv_hbm,
    cproj_hbm,
    out_ref,
    keep_ref,
    send_ref,
    x,
    cot,
    fqkv,
    fproj,
    mrg,
    mrg_t,
    mw,
    cqkv,
    cproj,
    sems,
    stat,
    normed,
    kv,
    qry,
    att,
    raised_a,
    raised_b,
    raised_c,
    inverse,
    bias_b,
    bias_c,
    mid,
    merged,
    mstat,
    mnormed,
    c_in,
    cstat,
    cnormed,
    cq,
    catt,
    craised,
    cinverse,
    dmid,
    datt,
    dq,
    dkv,
    dnorm,
    cdnorm,
    grads,
):
    last = place_ref[0]
    core = place_ref[1]
    weights = (
        (fqkv_hbm, fqkv),
        (fproj_hbm, fproj),
        (merge_hbm, mrg),
        (mw_hbm, mw),
        (cqkv_hbm, cqkv),
        (cproj_hbm, cproj),
        (merge_t_hbm, mrg_t),
    )
    loads = [pltpu.make_async_copy(src, dst, sems.at[n]) for n, (src, dst) in enumerate(weights)]
    pulls = []
    cpulls = []
    number = len(loads)
    for quad, ref in enumerate((q0_ref, q1_ref, q2_ref, q3_ref)):
        for (start, rows), off in zip(PIECES, E_OFF[quad]):
            pulls.append(
                pltpu.make_async_copy(
                    ref.at[pl.ds(start, rows)], x.at[pl.ds(off, rows)], sems.at[number]
                )
            )
            number += 1
        for half in range(2):
            cpulls.append(
                pltpu.make_async_copy(
                    ref.at[pl.ds(QROWS + 48 * half, 48)],
                    cot.at[half, pl.ds(C_OFF[quad], 48)],
                    sems.at[number],
                )
            )
            number += 1
    for copy in pulls:
        copy.start()
    for copy in loads:
        copy.start()
    for copy in cpulls:
        copy.start()

    def bias_of(shape, q_rows, piece, valid, q_half, k_half, split):
        q_at = lax.broadcasted_iota(jnp.int32, shape, 0) % q_rows
        k_at = lax.broadcasted_iota(jnp.int32, shape, 1)
        bad = (k_at % piece) >= valid
        if split:
            other = (q_at >= q_half) != (k_at >= k_half)
            bad = jnp.logical_or(bad, jnp.logical_and(other, last == 1))
        return jnp.where(bad, NEG, 0.0)

    bias_b[0] = bias_of((192, 160), 96, 80, 72, 48, 80, False)
    bias_b[1] = bias_of((192, 160), 96, 80, 72, 48, 80, True)
    bias_c[...] = bias_of((384, 192), 192, 48, 36, 96, 96, True)

    for copy in pulls:
        copy.wait()
    fgain = fgain_ref[...].astype(F32)

    @pl.loop(0, 8)
    def _(step):
        rows = pl.ds(pl.multiple_of(step * 176, 16), 176)
        result, centre, scale = norm_rows(x[rows, :], fgain)
        normed[rows, :] = result
        stat[0, rows, :] = jnp.broadcast_to(centre, (176, 128))
        stat[1, rows, :] = jnp.broadcast_to(scale, (176, 128))

    def cells(read):
        parts = []
        for q_start in range(0, QRY, 48):
            for quad in range(4):
                for e_off, q_off in zip(E_OFF[quad], Q_OFF[quad]):
                    if q_off == q_start:
                        parts.append(read(e_off))
        return jnp.concatenate(parts, axis=0)

    loads[0].wait()

    @pl.loop(0, 4)
    def _(step):
        kv[:, pl.ds(pl.multiple_of(step * 256, 256), 256)] = nn(
            normed[...], fqkv[:, pl.ds(pl.multiple_of(512 + step * 256, 256), 256)]
        ).astype(BF16)

    @pl.loop(0, 2)
    def _(step):
        cols = pl.ds(pl.multiple_of(step * 256, 256), 256)
        left = cells(lambda off: normed[pl.ds(off, 48), :])
        qry[:, cols] = (nn(left, fqkv[:, cols]).astype(BF16) * 0.125).astype(BF16)

    def raised_at(index, pair):
        kind = WINDOWS[index][4]
        if kind == 0:
            return raised_a.at[pair, index]
        if kind == 3:
            return raised_c.at[pair]
        return raised_b.at[pair, index - 4]

    def bias_at(kind):
        if kind == 0:
            return None
        return bias_c[...] if kind == 3 else bias_b[kind - 1]

    @pl.loop(0, 4)
    def _(pair):
        for index, (e_off, rows, q_off, q_rows, kind) in enumerate(WINDOWS):
            query = qry[pl.ds(q_off, q_rows), pair_slice(0, pair)]
            keys = kv[pl.ds(e_off, rows), pair_slice(0, pair)]
            vals = kv[pl.ds(e_off, rows), pair_slice(512, pair)]
            raised, inv, mixed = attend_pair(query, keys, vals, bias_at(kind))
            raised_at(index, pair)[...] = raised
            inverse[pair, pl.ds(2 * q_off, 2 * q_rows), :] = inv
            att[pl.ds(q_off, q_rows), pair_slice(0, pair)] = mixed.astype(BF16)

    loads[1].wait()

    @pl.loop(0, 2)
    def _(step):
        cols = pl.ds(pl.multiple_of(step * 256, 256), 256)
        left = cells(lambda off: x[pl.ds(off, 48), cols])
        mid[:, cols] = (left.astype(F32) + nn(att[...], fproj[:, cols])).astype(BF16)

    loads[2].wait()
    for k in range(4):
        merged[:, 512 * k : 512 * k + 512] = nn(mrg[k], mid[...]).astype(BF16)
    mgain = mgain_ref[...].astype(F32)
    result, centre, scale = norm_rows(merged[...], mgain)
    mnormed[...] = result
    mstat[0] = jnp.broadcast_to(centre, (CRS, 128))
    mstat[1] = jnp.broadcast_to(scale, (CRS, 128))
    loads[3].wait()

    @pl.loop(0, 4)
    def _(step):
        cols = pl.ds(pl.multiple_of(step * 256, 256), 256)
        c_in[:, cols] = nn(mnormed[...], mw[:, cols]).astype(BF16)

    cgain = cgain_ref[...].astype(F32)
    result, centre, scale = norm_rows(c_in[...], cgain)
    cnormed[...] = result
    cstat[0] = jnp.broadcast_to(centre, (CRS, 128))
    cstat[1] = jnp.broadcast_to(scale, (CRS, 128))
    loads[4].wait()

    @pl.loop(0, 6)
    def _(step):
        cols = pl.ds(pl.multiple_of(step * 512, 512), 512)
        value = nn(cnormed[...], cqkv[:, cols]).astype(BF16)
        cq[:, cols] = jnp.where(step < 2, value * 0.125, value).astype(BF16)

    @pl.loop(0, 8)
    def _(pair):
        raised, inv, mixed = attend_pair(
            cq[:, pair_slice(0, pair)],
            cq[:, pair_slice(1024, pair)],
            cq[:, pair_slice(2048, pair)],
            bias_c[...],
        )
        craised[pair] = raised
        cinverse[pair] = inv
        catt[:, pair_slice(0, pair)] = mixed.astype(BF16)

    loads[5].wait()
    for half in range(2):
        cols = slice(512 * half, 512 * half + 512)
        c_mid = (c_in[:, cols].astype(F32) + nn(catt[...], cproj[:, cols])).astype(BF16)
        for quad in range(4):
            off = C_OFF[quad]
            out_ref[quad, QROWS + 48 * half : QROWS + 48 * half + 48, :] = c_mid[off : off + 48]

    for copy in cpulls:
        copy.wait()
    dcot = jnp.concatenate([cot[0], cot[1]], axis=1)
    dcatt = nt(dcot, cproj[...]).astype(BF16)
    mnormed[:, 0:1024] = dcatt
    dcq = cq

    @pl.loop(0, 8)
    def _(pair):
        d_query, d_keys, d_vals = attend_back(
            cq[:, pair_slice(0, pair)],
            cq[:, pair_slice(1024, pair)],
            cq[:, pair_slice(2048, pair)],
            craised[pair],
            cinverse[pair],
            catt[:, pair_slice(0, pair)],
            mnormed[:, pair_slice(0, pair)],
        )
        dcq[:, pair_slice(0, pair)] = d_query.astype(BF16)
        dcq[:, pair_slice(1024, pair)] = d_keys.astype(BF16)
        dcq[:, pair_slice(2048, pair)] = d_vals.astype(BF16)

    @pl.loop(0, 4)
    def _(step):
        rows = pl.ds(pl.multiple_of(step * 256, 256), 256)
        cdnorm[:, rows] = nt(dcq[...], cqkv[rows, :])

    d_norm = norm_back(
        c_in[...], cgain, cstat[0][:, 0:1], cstat[1][:, 0:1], cdnorm[:, 0:1024].astype(BF16).astype(F32)
    )
    d_c = (dcot.astype(F32) + d_norm.astype(BF16).astype(F32)).astype(BF16)
    cnormed[...] = d_c

    @pl.loop(0, 4)
    def _(step):
        rows = pl.ds(pl.multiple_of(step * 512, 512), 512)
        cdnorm[:, rows] = nt(cnormed[...], mw[rows, :])

    d_merged = norm_back(
        merged[...], mgain, mstat[0][:, 0:1], mstat[1][:, 0:1], cdnorm[...].astype(BF16).astype(F32)
    ).astype(BF16)
    merged[...] = d_merged
    loads[6].wait()
    total = nn(mrg_t[0], merged[:, 0:512])
    for k in range(1, 4):
        total = total + nn(mrg_t[k], merged[:, 512 * k : 512 * k + 512])
    dmid[...] = total.astype(BF16)

    datt[...] = nt(dmid[...], fproj[...]).astype(BF16)
    scale_out = 1.0 / math.sqrt(73728)

    @pl.loop(0, 4)
    def _(pair):
        cols = pair_slice(0, pair)
        for index, (e_off, rows, q_off, q_rows, kind) in enumerate(WINDOWS):
            d_query, d_keys, d_vals = attend_back(
                qry[pl.ds(q_off, q_rows), cols],
                kv[pl.ds(e_off, rows), cols],
                kv[pl.ds(e_off, rows), pair_slice(512, pair)],
                raised_at(index, pair)[...],
                inverse[pair, pl.ds(2 * q_off, 2 * q_rows), :],
                att[pl.ds(q_off, q_rows), cols],
                datt[pl.ds(q_off, q_rows), cols],
            )
            dq[pl.ds(q_off, q_rows), cols] = d_query.astype(BF16)
            dkv[pl.ds(e_off, rows), cols] = d_keys.astype(BF16)
            dkv[pl.ds(e_off, rows), pair_slice(512, pair)] = d_vals.astype(BF16)

    @pl.loop(0, 2)
    def _(step):
        cols = pl.ds(pl.multiple_of(step * 256, 256), 256)
        left = cells(lambda off: normed[pl.ds(off, 48), :])
        value = (tn(left, dq[:, cols]) * scale_out).astype(BF16)
        grads[2 * step] = value[:, 0:128]
        grads[2 * step + 1] = value[:, 128:256]
        value = (tn(att[...], dmid[:, cols]) * scale_out).astype(BF16)
        grads[12 + 2 * step] = value[:, 0:128]
        grads[12 + 2 * step + 1] = value[:, 128:256]

    @pl.loop(0, 4)
    def _(step):
        cols = pl.ds(pl.multiple_of(step * 256, 256), 256)
        value = (tn(normed[...], dkv[:, cols]) * scale_out).astype(BF16)
        grads[4 + 2 * step] = value[:, 0:128]
        grads[4 + 2 * step + 1] = value[:, 128:256]

    @pl.loop(0, 8)
    def _(step):
        even = grads[2 * step]
        odd = grads[2 * step + 1]
        first = core == 0
        keep_ref[step] = jnp.where(first, even, odd)
        send_ref[step] = jnp.where(first, odd, even)

    @pl.loop(0, 2)
    def _(step):
        rows = pl.ds(pl.multiple_of(step * 256, 256), 256)
        base = nt(dkv[...], fqkv[rows, 512:1536])
        more = nt(dq[...], fqkv[rows, 0:512])
        dn_cols = pl.ds(pl.multiple_of(step * 256, 256), 256)
        dnorm[:, dn_cols] = base
        for quad in range(4):
            for e_off, q_off in zip(E_OFF[quad], Q_OFF[quad]):
                spot = (pl.ds(e_off, 48), dn_cols)
                dnorm[spot] = dnorm[spot] + more[q_off : q_off + 48]

    for quad in range(4):
        for (start, rows), e_off, q_off in zip(PIECES, E_OFF[quad], Q_OFF[quad]):
            spot = pl.ds(e_off, rows)
            d_norm = norm_back(
                x[spot, :], fgain, stat[0, spot, 0:1], stat[1, spot, 0:1], dnorm[spot, :]
            )
            head = d_norm[0:48] + dmid[pl.ds(q_off, 48), :].astype(F32)
            out_ref[quad, start : start + 48, :] = head.astype(BF16)
            if rows > 48:
                out_ref[quad, start + 48 : start + rows, :] = d_norm[48:].astype(BF16)


def work(place, quads, fgain, mgain, cgain, fqkv, fproj, mrg, mrg_t, mw, cqkv, cproj):
    anywhere = pl.BlockSpec(memory_space=pl.ANY)
    vmem = pl.BlockSpec(memory_space=pltpu.VMEM)
    scratch = [
        ((EXT, 512), BF16),
        ((2, CRS, 512), BF16),
        ((512, 1536), BF16),
        ((512, 512), BF16),
        ((4, CRS, QRY), BF16),
        ((4, QRY, CRS), BF16),
        ((2048, 1024), BF16),
        ((1024, 3072), BF16),
        ((1024, 1024), BF16),
        None,
        ((2, EXT, 128), F32),
        ((EXT, 512), BF16),
        ((EXT, 1024), BF16),
        ((QRY, 512), BF16),
        ((QRY, 512), BF16),
        ((4, 4, 96, 144), BF16),
        ((4, 4, 192, 160), BF16),
        ((4, 384, 192), BF16),
        ((4, 2 * QRY, 128), F32),
        ((2, 192, 160), F32),
        ((384, 192), F32),
        ((QRY, 512), BF16),
        ((CRS, 2048), BF16),
        ((2, CRS, 128), F32),
        ((CRS, 2048), BF16),
        ((CRS, 1024), BF16),
        ((2, CRS, 128), F32),
        ((CRS, 1024), BF16),
        ((CRS, 3072), BF16),
        ((CRS, 1024), BF16),
        ((8, 384, 192), BF16),
        ((8, 384, 128), F32),
        ((QRY, 512), BF16),
        ((QRY, 512), BF16),
        ((QRY, 512), BF16),
        ((EXT, 1024), BF16),
        ((EXT, 512), F32),
        ((CRS, 2048), F32),
        ((16, 512, 128), BF16),
    ]
    scratch = [
        pltpu.SemaphoreType.DMA((31,)) if item is None else pltpu.VMEM(*item) for item in scratch
    ]
    return pl.pallas_call(
        main_kernel,
        out_shape=(
            jax.ShapeDtypeStruct((4, SROWS, 512), BF16),
            jax.ShapeDtypeStruct((8, 512, 128), BF16),
            jax.ShapeDtypeStruct((8, 512, 128), BF16),
        ),
        in_specs=[pl.BlockSpec(memory_space=pltpu.SMEM)]
        + [anywhere] * 4
        + [vmem] * 3
        + [anywhere] * 7,
        out_specs=(vmem, vmem, vmem),
        scratch_shapes=scratch,
        compiler_params=pltpu.CompilerParams(vmem_limit_bytes=60 * 2**20),
    )(place, *quads, fgain, mgain, cgain, fqkv, fproj, mrg, mrg_t, mw, cqkv, cproj)


def shift(value, d_lat, d_lon):
    lats, lons = lax.axis_size("lat"), lax.axis_size("lon")
    pairs = []
    for a in range(lats):
        for b in range(lons):
            source = ((a + d_lat) % lats) * lons + (b + d_lon) % lons
            pairs.append((source, a * lons + b))
    return lax.ppermute(value, ("lat", "lon"), pairs)


def exchange(value, moves):
    lats, lons = lax.axis_size("lat"), lax.axis_size("lon")
    pairs = []
    for a in range(lats):
        for b in range(lons):
            to_a, to_b = moves(a, b)
            pairs.append((a * lons + b, to_a * lons + to_b))
    return lax.ppermute(value, ("lat", "lon"), pairs)


def reduce_terms(keep, send):
    lat, lon = lax.axis_index("lat"), lax.axis_index("lon")
    z, x = lon // 4, lat // 2
    got = exchange(send, lambda a, b: (a, b ^ 1))
    terms = (keep.astype(F32) + got.astype(F32)).astype(BF16)
    terms = terms.reshape(4, 2, 4, 2, 64, 128)

    def step_z(value, axis):
        total = lax.dynamic_index_in_dim(value, z, axis, keepdims=False).astype(F32)
        for d in (1, 2, 3):
            part = lax.dynamic_index_in_dim(value, z ^ d, axis, keepdims=False)
            total = total + exchange(part, lambda a, b: (a, b ^ (4 * d))).astype(F32)
        return total.astype(BF16)

    def step_x(value, axis):
        total = lax.dynamic_index_in_dim(value, x, axis, keepdims=False).astype(F32)
        for d in (1, 2, 3):
            part = lax.dynamic_index_in_dim(value, x ^ d, axis, keepdims=False)
            total = total + exchange(part, lambda a, b: (a ^ (2 * d), b)).astype(F32)
        return total.astype(BF16)

    low = step_z(terms[:, :, :, :, :32], 0)
    high = step_x(terms[:, :, :, :, 32:], 2)
    low = step_x(low, 1)
    high = step_z(high, 0)
    both = jnp.concatenate([low, high], axis=2).reshape(4, 64, 128)
    me = (lon // 2 % 2) * 2 + lat % 2
    total = lax.dynamic_index_in_dim(both, me, 0, keepdims=False).astype(F32)
    for d in (1, 2, 3):
        part = lax.dynamic_index_in_dim(both, me ^ d, 0, keepdims=False)
        moved = exchange(part, lambda a, b: (a ^ (d & 1), b ^ (d & 2)))
        total = total + moved.astype(F32)
    return total


def local(
    tokens,
    land_sea,
    land_vec,
    fine_gain,
    fine_qkv,
    fine_proj,
    merge_gain,
    merge_weight,
    coarse_gain,
    coarse_qkv,
    coarse_proj,
    cotangent,
):
    land = jnp.tile(land_sea.astype(F32).reshape(-1, 1), (2, 1))
    pick = jnp.asarray(PICK, BF16)
    cpick = jnp.asarray(CPICK, BF16)
    sends = prep(
        tokens.reshape(576, 512), land, land_vec.reshape(1, 512), cotangent, pick, cpick
    )
    quads = (sends[0], shift(sends[1], 1, 0), shift(sends[2], 0, 1), shift(sends[3], 1, 1))
    lat, lon = lax.axis_index("lat"), lax.axis_index("lon")
    place = jnp.stack([(lat == lax.axis_size("lat") - 1).astype(jnp.int32), lon % 2])
    back, keep, send = work(
        place,
        quads,
        fine_gain.reshape(1, -1),
        merge_gain.reshape(1, -1),
        coarse_gain.reshape(1, -1),
        fine_qkv,
        fine_proj,
        jnp.asarray(MERGE, BF16),
        jnp.asarray(MERGE.transpose(0, 2, 1), BF16),
        merge_weight,
        coarse_qkv,
        coarse_proj,
    )
    fine_grads = reduce_terms(keep, send)
    grad, coarse = finish(
        back[0],
        shift(back[1], -1, 0),
        shift(back[2], 0, -1),
        shift(back[3], -1, -1),
        jnp.asarray(PICK.transpose(0, 2, 1), BF16),
        jnp.asarray(CPICK.transpose(0, 2, 1), BF16),
    )
    return (coarse, grad.reshape(tokens.shape), fine_grads)


def solution(mesh):
    grid = P(None, "lat", "lon", None)
    placed = (grid, P("lat", "lon")) + (P(),) * 9 + (grid,)
    return jax.shard_map(
        local,
        mesh=mesh,
        in_specs=placed,
        out_specs=(grid, grid, P("lat", "lon")),
        check_vma=False,
    )
```

```python
import math

import jax
import jax.numpy as jnp
import numpy as np
from jax import lax
from jax.experimental import pallas as pl
from jax.experimental.pallas import tpu as pltpu
from jax.sharding import PartitionSpec as P

F32 = jnp.float32
BF16 = jnp.bfloat16
EPSILON = 1e-05
NEG = -1e30

QUADS = ((0, 0), (1, 0), (0, 1), (1, 1))
QROWS = 352
SROWS = QROWS + 96
PIECES = ((0, 144), (144, 80), (224, 80), (304, 48))
EXT = 1408
QRY = 768
CRS = 192

E_OFF = {
    0: (0, 576, 896, 1216),
    1: (144, 736, 976, 1312),
    2: (288, 656, 1056, 1264),
    3: (432, 816, 1136, 1360),
}
Q_OFF = {
    0: (0, 192, 384, 576),
    1: (48, 288, 432, 672),
    2: (96, 240, 480, 624),
    3: (144, 336, 528, 720),
}
CORDER = (0, 2, 1, 3)
C_OFF = {quad: 48 * place for place, quad in enumerate(CORDER)}

WINDOWS = (
    (0, 144, 0, 48, 0),
    (144, 144, 48, 48, 0),
    (288, 144, 96, 48, 0),
    (432, 144, 144, 48, 0),
    (576, 160, 192, 96, 1),
    (736, 160, 288, 96, 1),
    (896, 160, 384, 96, 2),
    (1056, 160, 480, 96, 2),
    (1216, 192, 576, 192, 3),
)


def piece_cells(quad):
    qr, qc = QUADS[quad]
    near_r, far_r, mid_r = ((1, 0, 2), (4, 5, 3))[qr]
    near_c, far_c, mid_c = ((1, 0, 2), (4, 5, 3))[qc]
    return (
        ((near_r, near_c), (near_r, far_c), (far_r, near_c), (far_r, far_c)),
        ((near_r, mid_c), (far_r, mid_c)),
        ((mid_r, near_c), (mid_r, far_c)),
        ((mid_r, mid_c),),
    )


def build_tables():
    pick = np.full((8, 384), -1, np.int32)
    cell_query = {}
    for quad in range(4):
        qr, qc = QUADS[quad]
        for (start, _), cells, q_off in zip(PIECES, piece_cells(quad), Q_OFF[quad]):
            cell_query[cells[0]] = q_off
            for number, (cr, cc) in enumerate(cells):
                for lev in range(2):
                    for i in range(3):
                        for j in range(6):
                            row = 3 * cr + i + 3 - 12 * qr
                            col = 6 * cc + j + 6 - 24 * qc
                            place = start + 36 * number + lev * 18 + i * 6 + j
                            pick[quad, place] = lev * 288 + row * 24 + col
    cpick = np.full((8, 128), -1, np.int32)
    merge = np.zeros((4, CRS, QRY), np.float32)
    for quad in range(4):
        qr, qc = QUADS[quad]
        for lev in range(2):
            for i in range(3):
                for j in range(6):
                    place = lev * 18 + i * 6 + j
                    row = i + 3 * (1 - qr)
                    col = j + 6 * (1 - qc)
                    cpick[quad, place] = (row * 12 + col) * 2 + lev
                    for k, (di, dj) in enumerate(((0, 0), (1, 0), (0, 1), (1, 1))):
                        er = 3 + 2 * (3 * qr + i) + di
                        ec = 6 + 2 * (6 * qc + j) + dj
                        spot = cell_query[(er // 3, ec // 6)] + lev * 18 + (er % 3) * 6 + ec % 6
                        merge[k, C_OFF[quad] + place, spot] = 1
    return pick, cpick, merge


PICK, CPICK, MERGE = build_tables()


def nn(left, right):
    return jnp.dot(left, right, preferred_element_type=F32)


def nt(left, right):
    return lax.dot_general(left, right, (((1,), (1,)), ((), ())), preferred_element_type=F32)


def tn(left, right):
    return lax.dot_general(left, right, (((0,), (0,)), ((), ())), preferred_element_type=F32)


def column(row):
    return jnp.broadcast_to(row, (128, 128)).T


def one_hot(row, count):
    blocks = []
    col = column(row)
    lane = lax.broadcasted_iota(jnp.int32, (128, 128), 1)
    for start in range(0, count, 128):
        hit = col == lane + start
        blocks.append(jnp.where(hit, 1.0, 0.0).astype(BF16))
    return jnp.concatenate(blocks, axis=1)[:, :count]


def one_hot_back(row, count):
    spot = lax.broadcasted_iota(jnp.int32, (count, row.shape[1]), 0)
    return jnp.where(spot == row, 1.0, 0.0).astype(BF16)


def pull(sources, targets, sems):
    copies = []
    for number, (source, target) in enumerate(zip(sources, targets)):
        copies.append(pltpu.make_async_copy(source, target, sems.at[number]))
        copies[-1].start()
    return copies


def prep_kernel(*refs):
    sources, outs, targets = refs[:6], refs[6:10], refs[10:16]
    tok, land_in, vec_in, cot_in, pick, cpick = targets
    slab, square, stream, built, sems, out_sems = refs[16:]
    copies = pull(sources, targets, sems)
    square[...] = jnp.zeros_like(square)
    slab[...] = jnp.zeros_like(slab)
    for number in (1, 2, 4, 0):
        copies[number].wait()
    square[0:12, 0:24] = land_in[...].astype(F32)
    flags = square[...].T
    vec = vec_in[...].astype(F32).reshape(1, 512)
    for step in range(12):
        row = 2 * step % 12
        land = jnp.concatenate([flags[0:24, row : row + 1], flags[0:24, row + 1 : row + 2]], axis=0)
        spot = slice(48 * step, 48 * step + 48)
        stream[spot, :] = (tok[spot, :].astype(F32) + land * vec).astype(BF16)
    copies[3].wait()
    copies[5].wait()
    slab[0:144, :] = cot_in[...].reshape(144, 1024)
    cot = slab[...]
    leaving = []
    for quad in (1, 2, 3, 0):
        out = built.at[quad]
        for start in (0, 128, 256):
            rows = min(128, QROWS - start)
            choice = one_hot(pick[quad : quad + 1, start : start + 128], 576)[:rows]
            out[start : start + rows, :] = nn(choice, stream[...]).astype(BF16)
        choice = one_hot(cpick[quad : quad + 1, :], CRS)[:48]
        picked = nn(choice, cot).astype(BF16)
        out[QROWS : QROWS + 48, :] = picked[:, 0:512]
        out[QROWS + 48 : SROWS, :] = picked[:, 512:1024]
        leaving.append(pltpu.make_async_copy(out, outs[quad], out_sems.at[quad]))
        leaving[-1].start()
    for copy in leaving:
        copy.wait()


HBM = pl.BlockSpec(memory_space=pltpu.HBM)
VMEM = pl.BlockSpec(memory_space=pltpu.VMEM)


def prep(tokens, land, vec, cot, pick, cpick):
    operands = (tokens, land, vec, cot, pick, cpick)
    return pl.pallas_call(
        prep_kernel,
        out_shape=(jax.ShapeDtypeStruct((SROWS, 512), BF16),) * 4,
        in_specs=[HBM] * 6,
        out_specs=(HBM,) * 4,
        scratch_shapes=[pltpu.VMEM(value.shape, value.dtype) for value in operands]
        + [
            pltpu.VMEM((CRS, 1024), BF16),
            pltpu.VMEM((128, 128), F32),
            pltpu.VMEM((576, 512), BF16),
            pltpu.VMEM((4, SROWS, 512), BF16),
            pltpu.SemaphoreType.DMA((6,)),
            pltpu.SemaphoreType.DMA((4,)),
        ],
        compiler_params=pltpu.CompilerParams(vmem_limit_bytes=60 * 2**20),
    )(*operands)


def finish_kernel(*refs):
    sources, grad_ref, coarse_ref, targets, sems = refs[:6], refs[6], refs[7], refs[8:14], refs[14]
    pick, cpick = targets[:2]
    copies = pull(sources, targets, sems)
    copies[0].wait()
    copies[1].wait()
    total = None
    crs = None
    for quad, ref in enumerate(targets[2:]):
        choice = one_hot_back(pick[quad : quad + 1, :], 576)
        small = one_hot_back(cpick[quad : quad + 1, :], CRS)[:, :48]
        copies[2 + quad].wait()
        term = nn(choice, ref[0:384, :])
        total = term if total is None else total + term
        wide = jnp.concatenate([ref[QROWS : QROWS + 48, :], ref[QROWS + 48 : SROWS, :]], axis=1)
        cterm = nn(small, wide)
        crs = cterm if crs is None else crs + cterm
    grad_ref[...] = total.astype(BF16)
    coarse_ref[...] = crs[0:144].astype(BF16).reshape(72, 2, 1024)


def finish(*operands):
    return pl.pallas_call(
        finish_kernel,
        out_shape=(
            jax.ShapeDtypeStruct((576, 512), BF16),
            jax.ShapeDtypeStruct((72, 2, 1024), BF16),
        ),
        in_specs=[HBM] * 6,
        scratch_shapes=[pltpu.VMEM(value.shape, value.dtype) for value in operands]
        + [pltpu.SemaphoreType.DMA((6,))],
        compiler_params=pltpu.CompilerParams(vmem_limit_bytes=60 * 2**20),
    )(*operands)


def norm_rows(values, gain):
    wide = values.astype(F32)
    centre = jnp.mean(wide, axis=-1, keepdims=True)
    moved = wide - centre
    scale = lax.rsqrt(jnp.mean(moved * moved, axis=-1, keepdims=True) + EPSILON)
    return (moved * scale * gain).astype(BF16), centre, scale


def norm_back(values, gain, centre, scale, d_normed):
    hat = (values.astype(F32) - centre) * scale
    weighted = d_normed * gain
    first = jnp.mean(weighted, axis=-1, keepdims=True)
    second = jnp.mean(weighted * hat, axis=-1, keepdims=True)
    return scale * (weighted - first - hat * second)


def norm_back_fresh(values, gain, d_normed):
    wide = values.astype(F32)
    moved = wide - jnp.mean(wide, axis=-1, keepdims=True)
    scale = lax.rsqrt(jnp.mean(moved * moved, axis=-1, keepdims=True) + EPSILON)
    hat = moved * scale
    weighted = d_normed * gain
    first = jnp.mean(weighted, axis=-1, keepdims=True)
    second = jnp.mean(weighted * hat, axis=-1, keepdims=True)
    return scale * (weighted - first - hat * second)


def lane_masks(rows):
    lane = lax.broadcasted_iota(jnp.int32, (rows, 128), 1)
    return lane < 64


def stacked(values):
    low = lane_masks(values.shape[0])
    zero = jnp.zeros_like(values)
    return jnp.concatenate([jnp.where(low, values, zero), jnp.where(low, zero, values)], axis=0)


def unstacked(values):
    half = values.shape[0] // 2
    return jnp.where(lane_masks(half), values[:half], values[half:])


def attend_all(queries, keys, vals, biases):
    scores = [nt(stacked(query), key) for query, key in zip(queries, keys)]
    scores = [s if bias is None else s + bias for s, bias in zip(scores, biases)]
    tops = [jnp.max(s, axis=-1, keepdims=True) for s in scores]
    raised = [jnp.exp(s - top).astype(BF16) for s, top in zip(scores, tops)]
    wide = [nn(r, jnp.concatenate([v, jnp.ones_like(v)], axis=1)) for r, v in zip(raised, vals)]
    inverse = [1.0 / w[:, 128:] for w in wide]
    mixed = [unstacked(w[:, :128] * i).astype(BF16) for w, i in zip(wide, inverse)]
    return raised, inverse, mixed


def back_all(queries, keys, vals, raised, inverse, mixed, d_mixed):
    d_scaled = [stacked(d).astype(F32) * i for d, i in zip(d_mixed, inverse)]
    twice = [jnp.concatenate([m, m], axis=0).astype(F32) for m in mixed]
    delta = [jnp.sum(d * t, axis=-1, keepdims=True) for d, t in zip(d_scaled, twice)]
    d_short = [d.astype(BF16) for d in d_scaled]
    d_probs = [nt(d, v) for d, v in zip(d_short, vals)]
    d_vals = [tn(r, d).astype(BF16) for r, d in zip(raised, d_short)]
    d_scores = [(r.astype(F32) * (p - t)).astype(BF16) for r, p, t in zip(raised, d_probs, delta)]
    d_query = [(unstacked(nn(d, k)) * 0.125).astype(BF16) for d, k in zip(d_scores, keys)]
    d_keys = [tn(d, stacked(q)).astype(BF16) for d, q in zip(d_scores, queries)]
    return d_query, d_keys, d_vals


def pair_slice(start, pair):
    return pl.ds(pl.multiple_of(start + pair * 128, 128), 128)


def main_kernel(
    q0_ref,
    q1_ref,
    q2_ref,
    q3_ref,
    fgain_ref,
    mgain_ref,
    cgain_ref,
    fqkv_hbm,
    fproj_hbm,
    merge_hbm,
    merge_t_hbm,
    mw_hbm,
    cqkv_hbm,
    cproj_hbm,
    keep_hbm,
    send_hbm,
    dqkv_hbm,
    dmid_hbm,
    cback_hbm,
    x,
    cot,
    fqkv,
    fproj,
    mrg,
    mrg_t,
    mw,
    cqkv,
    cproj,
    sems,
    normed,
    normed_t,
    kv,
    qry,
    att,
    att_t,
    raised_a,
    raised_b,
    raised_c,
    inverse,
    bias_b,
    bias_c,
    mid,
    merged,
    mstat,
    mnormed,
    c_in,
    cstat,
    cnormed,
    cq,
    catt,
    craised,
    cinverse,
    dmid,
    datt,
    dqkv,
    cdnorm,
    cback,
    keep,
    send,
    out_sems,
):
    last = jnp.where(lax.axis_index("lat") == lax.axis_size("lat") - 1, 1, 0)
    core = lax.axis_index("lon") % 2
    leaving = []

    def leave(src, dst):
        copy = pltpu.make_async_copy(src, dst, out_sems.at[len(leaving)])
        copy.start()
        leaving.append(copy)

    weights = (
        (fqkv_hbm, fqkv),
        (fproj_hbm, fproj),
        (merge_hbm, mrg),
        (mw_hbm, mw),
        (cqkv_hbm, cqkv),
        (cproj_hbm, cproj),
        (merge_t_hbm, mrg_t),
    )
    loads = [pltpu.make_async_copy(src, dst, sems.at[n]) for n, (src, dst) in enumerate(weights)]
    pulls = []
    cpulls = []
    number = len(loads)
    for quad, ref in enumerate((q0_ref, q1_ref, q2_ref, q3_ref)):
        for (start, rows), off in zip(PIECES, E_OFF[quad]):
            pulls.append(
                pltpu.make_async_copy(
                    ref.at[pl.ds(start, rows)], x.at[pl.ds(off, rows)], sems.at[number]
                )
            )
            number += 1
        for half in range(2):
            cpulls.append(
                pltpu.make_async_copy(
                    ref.at[pl.ds(QROWS + 48 * half, 48)],
                    cot.at[half, pl.ds(C_OFF[quad], 48)],
                    sems.at[number],
                )
            )
            number += 1
    for copy in pulls:
        copy.start()
    for copy in loads:
        copy.start()
    for copy in cpulls:
        copy.start()

    def bias_of(shape, q_rows, piece, valid, q_half, k_half, split):
        q_at = lax.broadcasted_iota(jnp.int32, shape, 0) % q_rows
        k_at = lax.broadcasted_iota(jnp.int32, shape, 1)
        bad = (k_at % piece) >= valid
        if split:
            other = (q_at >= q_half) != (k_at >= k_half)
            bad = jnp.logical_or(bad, jnp.logical_and(other, last == 1))
        return jnp.where(bad, NEG, 0.0)

    bias_b[0] = bias_of((192, 160), 96, 80, 72, 48, 80, False)
    bias_b[1] = bias_of((192, 160), 96, 80, 72, 48, 80, True)
    bias_c[...] = bias_of((384, 192), 192, 48, 36, 96, 96, True)

    for copy in pulls:
        copy.wait()
    fgain = fgain_ref[...].astype(F32)

    @pl.loop(0, 11)
    def _(step):
        rows = pl.ds(pl.multiple_of(step * 128, 128), 128)
        result, _, _ = norm_rows(x[rows, :], fgain)
        normed[rows, :] = result
        normed_t[:, rows] = result.T

    def cells(read):
        parts = []
        for q_start in range(0, QRY, 48):
            for quad in range(4):
                for e_off, q_off in zip(E_OFF[quad], Q_OFF[quad]):
                    if q_off == q_start:
                        parts.append(read(e_off))
        return jnp.concatenate(parts, axis=0)

    loads[0].wait()

    @pl.loop(0, 4)
    def _(step):
        kv[:, pl.ds(pl.multiple_of(step * 256, 256), 256)] = nn(
            normed[...], fqkv[:, pl.ds(pl.multiple_of(512 + step * 256, 256), 256)]
        ).astype(BF16)

    @pl.loop(0, 2)
    def _(step):
        cols = pl.ds(pl.multiple_of(step * 256, 256), 256)
        left = cells(lambda off: normed[pl.ds(off, 48), :])
        qry[:, cols] = (nn(left, fqkv[:, cols]).astype(BF16) * 0.125).astype(BF16)

    def raised_at(index, pair):
        kind = WINDOWS[index][4]
        if kind == 0:
            return raised_a.at[pair, index]
        if kind == 3:
            return raised_c.at[pair]
        return raised_b.at[pair, index - 4]

    def bias_at(kind):
        if kind == 0:
            return None
        return bias_c[...] if kind == 3 else bias_b[kind - 1]

    def queries_of(ref, pair):
        return [ref[pl.ds(q_off, q_rows), pair_slice(0, pair)] for _, _, q_off, q_rows, _ in WINDOWS]

    def keys_of(start, pair):
        return [kv[pl.ds(e_off, rows), pair_slice(start, pair)] for e_off, rows, _, _, _ in WINDOWS]

    @pl.loop(0, 4)
    def _(pair):
        raised, inv, mixed = attend_all(
            queries_of(qry, pair),
            keys_of(0, pair),
            keys_of(512, pair),
            [bias_at(window[4]) for window in WINDOWS],
        )
        for index, (_, _, q_off, q_rows, _) in enumerate(WINDOWS):
            raised_at(index, pair)[...] = raised[index]
            inverse[pair, pl.ds(2 * q_off, 2 * q_rows), :] = inv[index]
            att[pl.ds(q_off, q_rows), pair_slice(0, pair)] = mixed[index]

    loads[1].wait()

    @pl.loop(0, 2)
    def _(step):
        cols = pl.ds(pl.multiple_of(step * 256, 256), 256)
        left = cells(lambda off: x[pl.ds(off, 48), cols])
        mid[:, cols] = (left.astype(F32) + nn(att[...], fproj[:, cols])).astype(BF16)

    loads[2].wait()
    for k in range(4):
        merged[:, 512 * k : 512 * k + 512] = nn(mrg[k], mid[...]).astype(BF16)
    mgain = mgain_ref[...].astype(F32)
    result, centre, scale = norm_rows(merged[...], mgain)
    mnormed[...] = result
    mstat[0] = jnp.broadcast_to(centre, (CRS, 128))
    mstat[1] = jnp.broadcast_to(scale, (CRS, 128))
    loads[3].wait()

    @pl.loop(0, 4)
    def _(step):
        cols = pl.ds(pl.multiple_of(step * 256, 256), 256)
        c_in[:, cols] = nn(mnormed[...], mw[:, cols]).astype(BF16)

    cgain = cgain_ref[...].astype(F32)
    result, centre, scale = norm_rows(c_in[...], cgain)
    cnormed[...] = result
    cstat[0] = jnp.broadcast_to(centre, (CRS, 128))
    cstat[1] = jnp.broadcast_to(scale, (CRS, 128))
    loads[4].wait()

    @pl.loop(0, 6)
    def _(step):
        cols = pl.ds(pl.multiple_of(step * 512, 512), 512)
        value = nn(cnormed[...], cqkv[:, cols]).astype(BF16)
        cq[:, cols] = jnp.where(step < 2, value * 0.125, value).astype(BF16)

    def coarse_of(ref, start, group):
        return [ref[:, pair_slice(start, 4 * group + n)] for n in range(4)]

    @pl.loop(0, 2)
    def _(group):
        raised, inv, mixed = attend_all(
            coarse_of(cq, 0, group),
            coarse_of(cq, 1024, group),
            coarse_of(cq, 2048, group),
            [bias_c[...]] * 4,
        )
        for n in range(4):
            craised[4 * group + n] = raised[n]
            cinverse[4 * group + n] = inv[n]
            catt[:, pair_slice(0, 4 * group + n)] = mixed[n]

    loads[5].wait()
    for half in range(2):
        cols = slice(512 * half, 512 * half + 512)
        c_mid = (c_in[:, cols].astype(F32) + nn(catt[...], cproj[:, cols])).astype(BF16)
        for quad in range(4):
            off = C_OFF[quad]
            cback[quad, 48 * half : 48 * half + 48, :] = c_mid[off : off + 48]

    leave(cback, cback_hbm)

    for copy in cpulls:
        copy.wait()
    dcot = jnp.concatenate([cot[0], cot[1]], axis=1)
    dcatt = nt(dcot, cproj[...]).astype(BF16)
    mnormed[:, 0:1024] = dcatt
    dcq = cq

    @pl.loop(0, 2)
    def _(group):
        d_query, d_keys, d_vals = back_all(
            coarse_of(cq, 0, group),
            coarse_of(cq, 1024, group),
            coarse_of(cq, 2048, group),
            [craised[4 * group + n] for n in range(4)],
            [cinverse[4 * group + n] for n in range(4)],
            coarse_of(catt, 0, group),
            coarse_of(mnormed, 0, group),
        )
        for n in range(4):
            dcq[:, pair_slice(0, 4 * group + n)] = d_query[n]
            dcq[:, pair_slice(1024, 4 * group + n)] = d_keys[n]
            dcq[:, pair_slice(2048, 4 * group + n)] = d_vals[n]

    @pl.loop(0, 4)
    def _(step):
        rows = pl.ds(pl.multiple_of(step * 256, 256), 256)
        cdnorm[:, rows] = nt(dcq[...], cqkv[rows, :])

    d_norm = norm_back(
        c_in[...], cgain, cstat[0][:, 0:1], cstat[1][:, 0:1], cdnorm[:, 0:1024].astype(BF16).astype(F32)
    )
    d_c = (dcot.astype(F32) + d_norm.astype(BF16).astype(F32)).astype(BF16)
    cnormed[...] = d_c

    @pl.loop(0, 4)
    def _(step):
        rows = pl.ds(pl.multiple_of(step * 512, 512), 512)
        cdnorm[:, rows] = nt(cnormed[...], mw[rows, :])

    d_merged = norm_back(
        merged[...], mgain, mstat[0][:, 0:1], mstat[1][:, 0:1], cdnorm[...].astype(BF16).astype(F32)
    ).astype(BF16)
    merged[...] = d_merged
    loads[6].wait()
    total = nn(mrg_t[0], merged[:, 0:512])
    for k in range(1, 4):
        total = total + nn(mrg_t[k], merged[:, 512 * k : 512 * k + 512])
    dmid[...] = total.astype(BF16)

    leave(dmid, dmid_hbm)
    datt[...] = nt(dmid[...], fproj[...]).astype(BF16)
    att_t[...] = att[...].T
    scale_out = 1.0 / math.sqrt(73728)

    for quad in range(4):
        for (_, rows), e_off in zip(PIECES, E_OFF[quad]):
            if rows > 48:
                dqkv[pl.ds(e_off + 48, rows - 48), 0:512] = jnp.zeros((rows - 48, 512), BF16)

    def terms(step, value):
        value = (value * scale_out).astype(BF16)
        low, high = value[:, 0:128], value[:, 128:256]
        for part in range(4):
            rows = slice(128 * part, 128 * part + 128)
            keep[part, step] = jnp.where(core == 0, low[rows], high[rows])
            send[part, step] = jnp.where(core == 0, high[rows], low[rows])

    @pl.loop(0, 2)
    def _(step):
        cols = pl.ds(pl.multiple_of(step * 256, 256), 256)
        terms(6 + step, nn(att_t[...], dmid[:, cols]))

    @pl.loop(0, 4)
    def _(pair):
        d_query, d_keys, d_vals = back_all(
            queries_of(qry, pair),
            keys_of(0, pair),
            keys_of(512, pair),
            [raised_at(index, pair)[...] for index in range(9)],
            [inverse[pair, pl.ds(2 * w[2], 2 * w[3]), :] for w in WINDOWS],
            queries_of(att, pair),
            queries_of(datt, pair),
        )
        for index, (e_off, rows, q_off, q_rows, kind) in enumerate(WINDOWS):
            step = 48 if kind == 3 else 80
            for part in range(q_rows // 48):
                dqkv[pl.ds(e_off + step * part, 48), pair_slice(0, pair)] = d_query[index][
                    48 * part : 48 * part + 48
                ]
            dqkv[pl.ds(e_off, rows), pair_slice(512, pair)] = d_keys[index]
            dqkv[pl.ds(e_off, rows), pair_slice(1024, pair)] = d_vals[index]

    leave(dqkv, dqkv_hbm)

    @pl.loop(0, 6)
    def _(step):
        cols = pl.ds(pl.multiple_of(step * 256, 256), 256)
        terms(step, nn(normed_t[...], dqkv[:, cols]))

    leave(keep, keep_hbm)
    leave(send, send_hbm)
    for copy in leaving:
        copy.wait()


def tokens_kernel(*refs):
    sources, outs, targets = refs[:9], refs[9:13], refs[13:22]
    built, dnorm, sems, row_sems, out_sems = refs[22:]
    gain_in, fqkv, dqkv, dmid, cback = targets[:5]
    quads = targets[5:]
    copies = pull(sources[:2], targets[:2], sems)
    rows_in = []
    for part in range(4):
        rows = pl.ds(352 * part, 352)
        rows_in.append(
            pltpu.make_async_copy(sources[2].at[rows], dqkv.at[rows], row_sems.at[part])
        )
        rows_in[-1].start()
    for number in range(3, 9):
        copies.append(pltpu.make_async_copy(sources[number], targets[number], sems.at[number]))
        copies[-1].start()
    copies[0].wait()
    copies[1].wait()
    gain = gain_in[...].astype(F32).reshape(1, 512)
    for part in range(4):
        rows_in[part].wait()
        rows = pl.ds(352 * part, 352)
        dnorm[rows, :] = nt(dqkv[rows, :], fqkv[...])
    for copy in copies[2:]:
        copy.wait()
    leaving = []
    for quad in (1, 2, 3, 0):
        ref, out = quads[quad], built.at[quad]
        for (start, rows), e_off, q_off in zip(PIECES, E_OFF[quad], Q_OFF[quad]):
            d_norm = norm_back_fresh(ref[start : start + rows, :], gain, dnorm[pl.ds(e_off, rows), :])
            head = d_norm[0:48] + dmid[pl.ds(q_off, 48), :].astype(F32)
            out[start : start + 48, :] = head.astype(BF16)
            if rows > 48:
                out[start + 48 : start + rows, :] = d_norm[48:].astype(BF16)
        out[QROWS:SROWS, :] = cback[quad]
        leaving.append(pltpu.make_async_copy(out, outs[quad], out_sems.at[quad]))
        leaving[-1].start()
    for copy in leaving:
        copy.wait()


def token_grads(*operands):
    return pl.pallas_call(
        tokens_kernel,
        out_shape=(jax.ShapeDtypeStruct((SROWS, 512), BF16),) * 4,
        in_specs=[HBM] * 9,
        out_specs=(HBM,) * 4,
        scratch_shapes=[pltpu.VMEM(value.shape, value.dtype) for value in operands]
        + [
            pltpu.VMEM((4, SROWS, 512), BF16),
            pltpu.VMEM((EXT, 512), F32),
            pltpu.SemaphoreType.DMA((9,)),
            pltpu.SemaphoreType.DMA((4,)),
            pltpu.SemaphoreType.DMA((4,)),
        ],
        cost_estimate=pl.CostEstimate(
            flops=2 * EXT * 1536 * 512, bytes_accessed=24 * 2**20, transcendentals=0
        ),
        compiler_params=pltpu.CompilerParams(vmem_limit_bytes=60 * 2**20),
    )(*operands)


def work(quads, fgain, mgain, cgain, fqkv, fproj, mrg, mrg_t, mw, cqkv, cproj):
    scratch = [
        ((EXT, 512), BF16),
        ((2, CRS, 512), BF16),
        ((512, 1536), BF16),
        ((512, 512), BF16),
        ((4, CRS, QRY), BF16),
        ((4, QRY, CRS), BF16),
        ((2048, 1024), BF16),
        ((1024, 3072), BF16),
        ((1024, 1024), BF16),
        None,
        ((EXT, 512), BF16),
        ((512, EXT), BF16),
        ((EXT, 1024), BF16),
        ((QRY, 512), BF16),
        ((QRY, 512), BF16),
        ((512, QRY), BF16),
        ((4, 4, 96, 144), BF16),
        ((4, 4, 192, 160), BF16),
        ((4, 384, 192), BF16),
        ((4, 2 * QRY, 128), F32),
        ((2, 192, 160), F32),
        ((384, 192), F32),
        ((QRY, 512), BF16),
        ((CRS, 2048), BF16),
        ((2, CRS, 128), F32),
        ((CRS, 2048), BF16),
        ((CRS, 1024), BF16),
        ((2, CRS, 128), F32),
        ((CRS, 1024), BF16),
        ((CRS, 3072), BF16),
        ((CRS, 1024), BF16),
        ((8, 384, 192), BF16),
        ((8, 384, 128), F32),
        ((QRY, 512), BF16),
        ((QRY, 512), BF16),
        ((EXT, 1536), BF16),
        ((CRS, 2048), F32),
        ((4, 96, 512), BF16),
        ((4, 8, 128, 128), BF16),
        ((4, 8, 128, 128), BF16),
        None,
    ]
    scratch = [
        pltpu.SemaphoreType.DMA((31,)) if item is None else pltpu.VMEM(*item) for item in scratch
    ]
    return pl.pallas_call(
        main_kernel,
        out_shape=(
            jax.ShapeDtypeStruct((4, 8, 128, 128), BF16),
            jax.ShapeDtypeStruct((4, 8, 128, 128), BF16),
            jax.ShapeDtypeStruct((EXT, 1536), BF16),
            jax.ShapeDtypeStruct((QRY, 512), BF16),
            jax.ShapeDtypeStruct((4, 96, 512), BF16),
        ),
        in_specs=[HBM] * 4 + [VMEM] * 3 + [HBM] * 7,
        out_specs=(HBM,) * 5,
        scratch_shapes=scratch,
        compiler_params=pltpu.CompilerParams(vmem_limit_bytes=60 * 2**20),
    )(*quads, fgain, mgain, cgain, fqkv, fproj, mrg, mrg_t, mw, cqkv, cproj)


def shift(value, d_lat, d_lon):
    lats, lons = lax.axis_size("lat"), lax.axis_size("lon")
    pairs = []
    for a in range(lats):
        for b in range(lons):
            source = ((a + d_lat) % lats) * lons + (b + d_lon) % lons
            pairs.append((source, a * lons + b))
    return lax.ppermute(value, ("lat", "lon"), pairs)


def exchange(value, moves):
    lats, lons = lax.axis_size("lat"), lax.axis_size("lon")
    pairs = []
    for a in range(lats):
        for b in range(lons):
            to_a, to_b = moves(a, b)
            pairs.append((a * lons + b, to_a * lons + to_b))
    return lax.ppermute(value, ("lat", "lon"), pairs)


def spread(pieces, moves):
    total = pieces[0].astype(F32)
    for d in (1, 2, 3):
        total = total + exchange(pieces[d], lambda a, b: moves(a, b, d)).astype(F32)
    return total


def pieces_of(value, me):
    return [lax.dynamic_index_in_dim(value, me ^ d, 0, keepdims=False) for d in range(4)]


def local_grads(keep, send, lat):
    got = exchange(send, lambda a, b: (a, b ^ 1))
    pieces = []
    for mine, other in zip(pieces_of(keep, lat // 2), pieces_of(got, lat // 2)):
        pieces.append((mine.astype(F32) + other.astype(F32)).astype(BF16))
    return pieces


def local(
    tokens,
    land_sea,
    land_vec,
    fine_gain,
    fine_qkv,
    fine_proj,
    merge_gain,
    merge_weight,
    coarse_gain,
    coarse_qkv,
    coarse_proj,
    cotangent,
):
    pick, cpick = jnp.asarray(PICK), jnp.asarray(CPICK)
    cot = cotangent.transpose(1, 2, 0, 3).reshape(72, 2, 1024)
    sends = prep(tokens.reshape(576, 512), land_sea, land_vec, cot, pick, cpick)
    quads = (sends[0], shift(sends[1], 1, 0), shift(sends[2], 0, 1), shift(sends[3], 1, 1))
    keep, send, dqkv, dmid, cback = work(
        quads,
        fine_gain.reshape(1, -1),
        merge_gain.reshape(1, -1),
        coarse_gain.reshape(1, -1),
        fine_qkv,
        fine_proj,
        jnp.asarray(MERGE, BF16),
        jnp.asarray(MERGE.transpose(0, 2, 1), BF16),
        merge_weight,
        coarse_qkv,
        coarse_proj,
    )
    lat, lon = lax.axis_index("lat"), lax.axis_index("lon")
    pieces = local_grads(keep, send, lat)
    pieces, dqkv = lax.optimization_barrier((pieces, dqkv))
    back = token_grads(fine_gain, fine_qkv, dqkv, dmid, cback, *quads)
    terms = spread(pieces, lambda a, b, d: (a ^ (2 * d), b)).astype(BF16)
    terms, _ = lax.optimization_barrier((terms, back))
    moved = (shift(back[1], -1, 0), shift(back[2], 0, -1), shift(back[3], -1, -1))
    terms = pieces_of(terms.reshape(4, 2, 128, 128), lon // 4)
    terms = spread(terms, lambda a, b, d: (a, b ^ (4 * d))).astype(BF16)
    terms, moved = lax.optimization_barrier((terms, moved))
    terms = pieces_of(terms.reshape(4, 64, 128), (lon // 2 % 2) * 2 + lat % 2)
    fine_grads = spread(terms, lambda a, b, d: (a ^ (d & 1), b ^ (d & 2)))
    grad, coarse = finish(pick, cpick, back[0], *moved)
    coarse = coarse.reshape(6, 12, 2, 1024).transpose(2, 0, 1, 3)
    return (coarse, grad.reshape(tokens.shape), fine_grads)


def solution(mesh):
    grid = P(None, "lat", "lon", None)
    placed = (grid, P("lat", "lon")) + (P(),) * 9 + (grid,)
    return jax.shard_map(
        local,
        mesh=mesh,
        in_specs=placed,
        out_specs=(grid, grid, P("lat", "lon")),
        check_vma=False,
    )
```

```python
import math

import jax
import jax.numpy as jnp
import numpy as np
from jax import lax
from jax.experimental import pallas as pl
from jax.experimental.pallas import tpu as pltpu
from jax.sharding import PartitionSpec as P

F32 = jnp.float32
BF16 = jnp.bfloat16
EPSILON = 1e-05
NEG = -1e30

QUADS = ((0, 0), (1, 0), (0, 1), (1, 1))
SROWS = 400
TAIL = 144
PIECES = ((0, 144), (144, 80), (224, 80), (304, 48))
EXT = 1408
QRY = 768
CRS = 192

E_OFF = {
    0: (0, 576, 896, 1216),
    1: (144, 736, 976, 1312),
    2: (288, 656, 1056, 1264),
    3: (432, 816, 1136, 1360),
}
Q_OFF = {
    0: (0, 192, 384, 576),
    1: (48, 288, 432, 672),
    2: (96, 240, 480, 624),
    3: (144, 336, 528, 720),
}
CORDER = (0, 2, 1, 3)
C_OFF = {quad: 48 * place for place, quad in enumerate(CORDER)}

WINDOWS = (
    (0, 144, 0, 48, 0),
    (144, 144, 48, 48, 0),
    (288, 144, 96, 48, 0),
    (432, 144, 144, 48, 0),
    (576, 160, 192, 96, 1),
    (736, 160, 288, 96, 1),
    (896, 160, 384, 96, 2),
    (1056, 160, 480, 96, 2),
    (1216, 192, 576, 192, 3),
)


def piece_cells(quad):
    qr, qc = QUADS[quad]
    near_r, far_r, mid_r = ((1, 0, 2), (4, 5, 3))[qr]
    near_c, far_c, mid_c = ((1, 0, 2), (4, 5, 3))[qc]
    return (
        ((near_r, near_c), (near_r, far_c), (far_r, near_c), (far_r, far_c)),
        ((near_r, mid_c), (far_r, mid_c)),
        ((mid_r, near_c), (mid_r, far_c)),
        ((mid_r, mid_c),),
    )


def build_tables():
    pick = np.full((8, 384), -1, np.int32)
    cell_query = {}
    for quad in range(4):
        qr, qc = QUADS[quad]
        place = 0
        for cells, q_off in zip(piece_cells(quad), Q_OFF[quad]):
            cell_query[cells[0]] = q_off
            for cr, cc in cells:
                for lev in range(2):
                    for i in range(3):
                        for j in range(6):
                            row = 3 * cr + i + 3 - 12 * qr
                            col = 6 * cc + j + 6 - 24 * qc
                            pick[quad, place] = lev * 288 + row * 24 + col
                            place += 1
    expand = np.full((8, 384), -1, np.int32)
    for start, first, rows in ((0, 0, 72), (80, 72, 72), (160, 144, 36), (208, 184, 36), (256, 220, 36)):
        expand[0, start : start + rows] = first + np.arange(rows)
    cpick = np.full((16, 128), -1, np.int32)
    merge = np.zeros((4, CRS, QRY), np.float32)
    for quad in range(4):
        qr, qc = QUADS[quad]
        for lev in range(2):
            for i in range(3):
                for j in range(6):
                    place = lev * 18 + i * 6 + j
                    row = i + 3 * (1 - qr)
                    col = j + 6 * (1 - qc)
                    spot = (row * 12 + col) * 2 + lev
                    cpick[quad, 72 + place] = spot
                    if place < 20:
                        cpick[4 + quad, 108 + place] = spot
                    else:
                        cpick[8 + quad, place - 20] = spot
                    for k, (di, dj) in enumerate(((0, 0), (1, 0), (0, 1), (1, 1))):
                        er = 3 + 2 * (3 * qr + i) + di
                        ec = 6 + 2 * (6 * qc + j) + dj
                        spot = cell_query[(er // 3, ec // 6)] + lev * 18 + (er % 3) * 6 + ec % 6
                        merge[k, C_OFF[quad] + place, spot] = 1
    return pick, cpick, expand, merge


PICK, CPICK, EXPAND, MERGE = build_tables()


def nn(left, right):
    return jnp.dot(left, right, preferred_element_type=F32)


def nt(left, right):
    return lax.dot_general(left, right, (((1,), (1,)), ((), ())), preferred_element_type=F32)


def tn(left, right):
    return lax.dot_general(left, right, (((0,), (0,)), ((), ())), preferred_element_type=F32)


def column(row):
    return jnp.broadcast_to(row, (128, 128)).T


def one_hot(row, count):
    blocks = []
    col = column(row)
    lane = lax.broadcasted_iota(jnp.int32, (128, 128), 1)
    for start in range(0, count, 128):
        hit = col == lane + start
        blocks.append(jnp.where(hit, 1.0, 0.0).astype(BF16))
    return jnp.concatenate(blocks, axis=1)[:, :count]


def one_hot_back(row, count):
    spot = lax.broadcasted_iota(jnp.int32, (count, row.shape[1]), 0)
    return jnp.where(spot == row, 1.0, 0.0).astype(BF16)


def pull(sources, targets, sems):
    copies = []
    for number, (source, target) in enumerate(zip(sources, targets)):
        copies.append(pltpu.make_async_copy(source, target, sems.at[number]))
        copies[-1].start()
    return copies


def prep_kernel(*refs):
    sources, outs, targets = refs[:6], refs[6:10], refs[10:16]
    tok, land_in, vec_in, cot_in, pick, cpick = targets
    square, stream, built, sems, out_sems = refs[16:]
    copies = pull(sources, targets, sems)
    square[...] = jnp.zeros_like(square)
    for number in (1, 2, 4, 0):
        copies[number].wait()
    square[0:12, 0:24] = land_in[...].astype(F32)
    flags = square[...].T
    vec = vec_in[...].astype(F32).reshape(1, 512)
    for step in range(12):
        row = 2 * step % 12
        land = jnp.concatenate([flags[0:24, row : row + 1], flags[0:24, row + 1 : row + 2]], axis=0)
        spot = slice(48 * step, 48 * step + 48)
        stream[spot, :] = (tok[spot, :].astype(F32) + land * vec).astype(BF16)
    copies[3].wait()
    copies[5].wait()
    cot = cot_in[...].reshape(144, 1024)
    leaving = []
    for quad in (1, 2, 3, 0):
        out = built.at[quad]
        for start in (0, 128, 256):
            choice = one_hot(pick[quad : quad + 1, start : start + 128], 576)
            value = nn(choice, stream[...])
            if start == 256:
                first = one_hot(cpick[quad : quad + 1, :], 144)
                second = one_hot(cpick[4 + quad : 5 + quad, :], 144)
                value = value + nn(first, cot[:, 0:512]) + nn(second, cot[:, 512:1024])
            out[start : start + 128, :] = value.astype(BF16)
        rest = one_hot(cpick[8 + quad : 9 + quad, :], 144)[:16]
        out[384:400, :] = nn(rest, cot[:, 512:1024]).astype(BF16)
        leaving.append(pltpu.make_async_copy(out, outs[quad], out_sems.at[quad]))
        leaving[-1].start()
    for copy in leaving:
        copy.wait()


HBM = pl.BlockSpec(memory_space=pltpu.HBM)
VMEM = pl.BlockSpec(memory_space=pltpu.VMEM)


def prep(tokens, land, vec, cot, pick, cpick):
    operands = (tokens, land, vec, cot, pick, cpick)
    return pl.pallas_call(
        prep_kernel,
        out_shape=(jax.ShapeDtypeStruct((SROWS, 512), BF16),) * 4,
        in_specs=[HBM] * 6,
        out_specs=(HBM,) * 4,
        scratch_shapes=[pltpu.VMEM(value.shape, value.dtype) for value in operands]
        + [
            pltpu.VMEM((128, 128), F32),
            pltpu.VMEM((576, 512), BF16),
            pltpu.VMEM((4, SROWS, 512), BF16),
            pltpu.SemaphoreType.DMA((6,)),
            pltpu.SemaphoreType.DMA((4,)),
        ],
        compiler_params=pltpu.CompilerParams(vmem_limit_bytes=60 * 2**20),
    )(*operands)


def finish_kernel(*refs):
    sources, grad_ref, coarse_ref, targets, sems = refs[:6], refs[6], refs[7], refs[8:14], refs[14]
    pick, cpick = targets[:2]
    copies = pull(sources, targets, sems)
    copies[0].wait()
    copies[1].wait()
    total = None
    crs = None
    for quad, ref in enumerate(targets[2:]):
        choice = one_hot_back(pick[quad : quad + 1, :], 576)
        first = one_hot_back(cpick[quad : quad + 1, :], 144)
        second = one_hot_back(cpick[4 + quad : 5 + quad, :], 144)
        rest = one_hot_back(cpick[8 + quad : 9 + quad, :], 144)[:, :16]
        copies[2 + quad].wait()
        term = nn(choice, ref[0:384, :])
        total = term if total is None else total + term
        left = nn(first, ref[256:384, :])
        right = nn(second, ref[256:384, :]) + nn(rest, ref[384:400, :])
        cterm = jnp.concatenate([left, right], axis=1)
        crs = cterm if crs is None else crs + cterm
    grad_ref[...] = total.astype(BF16)
    coarse_ref[...] = crs.astype(BF16).reshape(72, 2, 1024)


def finish(*operands):
    return pl.pallas_call(
        finish_kernel,
        out_shape=(
            jax.ShapeDtypeStruct((576, 512), BF16),
            jax.ShapeDtypeStruct((72, 2, 1024), BF16),
        ),
        in_specs=[HBM] * 6,
        scratch_shapes=[pltpu.VMEM(value.shape, value.dtype) for value in operands]
        + [pltpu.SemaphoreType.DMA((6,))],
        compiler_params=pltpu.CompilerParams(vmem_limit_bytes=60 * 2**20),
    )(*operands)


def norm_rows(values, gain):
    wide = values.astype(F32)
    centre = jnp.mean(wide, axis=-1, keepdims=True)
    moved = wide - centre
    scale = lax.rsqrt(jnp.mean(moved * moved, axis=-1, keepdims=True) + EPSILON)
    return (moved * scale * gain).astype(BF16), centre, scale


def norm_back(values, gain, centre, scale, d_normed):
    hat = (values.astype(F32) - centre) * scale
    weighted = d_normed * gain
    first = jnp.mean(weighted, axis=-1, keepdims=True)
    second = jnp.mean(weighted * hat, axis=-1, keepdims=True)
    return scale * (weighted - first - hat * second)


def norm_back_fresh(values, gain, d_normed):
    wide = values.astype(F32)
    moved = wide - jnp.mean(wide, axis=-1, keepdims=True)
    scale = lax.rsqrt(jnp.mean(moved * moved, axis=-1, keepdims=True) + EPSILON)
    hat = moved * scale
    weighted = d_normed * gain
    first = jnp.mean(weighted, axis=-1, keepdims=True)
    second = jnp.mean(weighted * hat, axis=-1, keepdims=True)
    return scale * (weighted - first - hat * second)


def lane_masks(rows):
    lane = lax.broadcasted_iota(jnp.int32, (rows, 128), 1)
    return lane < 64


def stacked(values):
    low = lane_masks(values.shape[0])
    zero = jnp.zeros_like(values)
    return jnp.concatenate([jnp.where(low, values, zero), jnp.where(low, zero, values)], axis=0)


def unstacked(values):
    half = values.shape[0] // 2
    return jnp.where(lane_masks(half), values[:half], values[half:])


def attend_all(queries, keys, vals, biases):
    scores = [nt(stacked(query), key) for query, key in zip(queries, keys)]
    scores = [s if bias is None else s + bias for s, bias in zip(scores, biases)]
    tops = [jnp.max(s, axis=-1, keepdims=True) for s in scores]
    raised = [jnp.exp(s - top).astype(BF16) for s, top in zip(scores, tops)]
    wide = [nn(r, jnp.concatenate([v, jnp.ones_like(v)], axis=1)) for r, v in zip(raised, vals)]
    inverse = [1.0 / w[:, 128:] for w in wide]
    mixed = [unstacked(w[:, :128] * i).astype(BF16) for w, i in zip(wide, inverse)]
    return raised, inverse, mixed


def back_all(queries, keys, vals, raised, inverse, mixed, d_mixed):
    d_scaled = [stacked(d).astype(F32) * i for d, i in zip(d_mixed, inverse)]
    twice = [jnp.concatenate([m, m], axis=0).astype(F32) for m in mixed]
    delta = [jnp.sum(d * t, axis=-1, keepdims=True) for d, t in zip(d_scaled, twice)]
    d_short = [d.astype(BF16) for d in d_scaled]
    d_probs = [nt(d, v) for d, v in zip(d_short, vals)]
    d_vals = [tn(r, d).astype(BF16) for r, d in zip(raised, d_short)]
    d_scores = [(r.astype(F32) * (p - t)).astype(BF16) for r, p, t in zip(raised, d_probs, delta)]
    d_query = [(unstacked(nn(d, k)) * 0.125).astype(BF16) for d, k in zip(d_scores, keys)]
    d_keys = [tn(d, stacked(q)).astype(BF16) for d, q in zip(d_scores, queries)]
    return d_query, d_keys, d_vals


def pair_slice(start, pair):
    return pl.ds(pl.multiple_of(start + pair * 128, 128), 128)


def main_kernel(
    q0_ref,
    q1_ref,
    q2_ref,
    q3_ref,
    fgain_ref,
    mgain_ref,
    cgain_ref,
    fqkv_hbm,
    fproj_hbm,
    merge_hbm,
    merge_t_hbm,
    mw_hbm,
    cqkv_hbm,
    cproj_hbm,
    expand_hbm,
    keep_hbm,
    send_hbm,
    dqkv_hbm,
    dmid_hbm,
    cback_hbm,
    x_hbm,
    tails,
    expand,
    x,
    cot,
    fqkv,
    fproj,
    mrg,
    mrg_t,
    mw,
    cqkv,
    cproj,
    sems,
    normed,
    normed_t,
    kv,
    qry,
    att,
    att_t,
    raised_a,
    raised_b,
    raised_c,
    inverse,
    bias_b,
    bias_c,
    mid,
    merged,
    mstat,
    mnormed,
    c_in,
    cstat,
    cnormed,
    cq,
    catt,
    craised,
    cinverse,
    dmid,
    datt,
    dqkv,
    cdnorm,
    cback,
    keep,
    send,
    out_sems,
):
    last = jnp.where(lax.axis_index("lat") == lax.axis_size("lat") - 1, 1, 0)
    core = lax.axis_index("lon") % 2
    leaving = []

    def leave(src, dst):
        copy = pltpu.make_async_copy(src, dst, out_sems.at[len(leaving)])
        copy.start()
        leaving.append(copy)

    weights = (
        (fqkv_hbm, fqkv),
        (fproj_hbm, fproj),
        (merge_hbm, mrg),
        (mw_hbm, mw),
        (cqkv_hbm, cqkv),
        (cproj_hbm, cproj),
        (merge_t_hbm, mrg_t),
    )
    loads = [pltpu.make_async_copy(src, dst, sems.at[n]) for n, (src, dst) in enumerate(weights)]
    pulls = []
    number = len(loads)
    for quad, ref in enumerate((q0_ref, q1_ref, q2_ref, q3_ref)):
        pulls.append(
            pltpu.make_async_copy(
                ref.at[pl.ds(0, TAIL)], x.at[pl.ds(E_OFF[quad][0], TAIL)], sems.at[number]
            )
        )
        pulls.append(
            pltpu.make_async_copy(
                ref.at[pl.ds(TAIL, SROWS - TAIL)], tails.at[quad], sems.at[number + 1]
            )
        )
        number += 2
    pulls.append(pltpu.make_async_copy(expand_hbm, expand, sems.at[number]))
    for copy in pulls:
        copy.start()
    for copy in loads:
        copy.start()

    def bias_of(shape, q_rows, piece, valid, q_half, k_half, split):
        q_at = lax.broadcasted_iota(jnp.int32, shape, 0) % q_rows
        k_at = lax.broadcasted_iota(jnp.int32, shape, 1)
        bad = (k_at % piece) >= valid
        if split:
            other = (q_at >= q_half) != (k_at >= k_half)
            bad = jnp.logical_or(bad, jnp.logical_and(other, last == 1))
        return jnp.where(bad, NEG, 0.0)

    bias_b[0] = bias_of((192, 160), 96, 80, 72, 48, 80, False)
    bias_b[1] = bias_of((192, 160), 96, 80, 72, 48, 80, True)
    bias_c[...] = bias_of((384, 192), 192, 48, 36, 96, 96, True)

    spread_out = []
    for copy in pulls:
        copy.wait()
    for start in (0, 128, 256):
        spread_out.append(one_hot(expand[0:1, start : start + 128], 256))
    spread_out = jnp.concatenate(spread_out, axis=0)[:304]
    for quad in range(4):
        value = nn(spread_out, tails[quad]).astype(BF16)
        for (start, rows), off in list(zip(PIECES, E_OFF[quad]))[1:]:
            x[pl.ds(off, rows), :] = value[start - TAIL : start - TAIL + rows]
        for half in range(2):
            cot[half, pl.ds(C_OFF[quad], 48), :] = value[208 + 48 * half : 256 + 48 * half]
    leave(x, x_hbm)
    fgain = fgain_ref[...].astype(F32)

    @pl.loop(0, 11)
    def _(step):
        rows = pl.ds(pl.multiple_of(step * 128, 128), 128)
        result, _, _ = norm_rows(x[rows, :], fgain)
        normed[rows, :] = result
        normed_t[:, rows] = result.T

    def cells(read):
        parts = []
        for q_start in range(0, QRY, 48):
            for quad in range(4):
                for e_off, q_off in zip(E_OFF[quad], Q_OFF[quad]):
                    if q_off == q_start:
                        parts.append(read(e_off))
        return jnp.concatenate(parts, axis=0)

    loads[0].wait()

    @pl.loop(0, 4)
    def _(step):
        kv[:, pl.ds(pl.multiple_of(step * 256, 256), 256)] = nn(
            normed[...], fqkv[:, pl.ds(pl.multiple_of(512 + step * 256, 256), 256)]
        ).astype(BF16)

    @pl.loop(0, 2)
    def _(step):
        cols = pl.ds(pl.multiple_of(step * 256, 256), 256)
        left = cells(lambda off: normed[pl.ds(off, 48), :])
        qry[:, cols] = (nn(left, fqkv[:, cols]).astype(BF16) * 0.125).astype(BF16)

    def raised_at(index, pair):
        kind = WINDOWS[index][4]
        if kind == 0:
            return raised_a.at[pair, index]
        if kind == 3:
            return raised_c.at[pair]
        return raised_b.at[pair, index - 4]

    def bias_at(kind):
        if kind == 0:
            return None
        return bias_c[...] if kind == 3 else bias_b[kind - 1]

    def queries_of(ref, pair):
        return [ref[pl.ds(q_off, q_rows), pair_slice(0, pair)] for _, _, q_off, q_rows, _ in WINDOWS]

    def keys_of(start, pair):
        return [kv[pl.ds(e_off, rows), pair_slice(start, pair)] for e_off, rows, _, _, _ in WINDOWS]

    @pl.loop(0, 4)
    def _(pair):
        raised, inv, mixed = attend_all(
            queries_of(qry, pair),
            keys_of(0, pair),
            keys_of(512, pair),
            [bias_at(window[4]) for window in WINDOWS],
        )
        for index, (_, _, q_off, q_rows, _) in enumerate(WINDOWS):
            raised_at(index, pair)[...] = raised[index]
            inverse[pair, pl.ds(2 * q_off, 2 * q_rows), :] = inv[index]
            att[pl.ds(q_off, q_rows), pair_slice(0, pair)] = mixed[index]

    loads[1].wait()

    @pl.loop(0, 2)
    def _(step):
        cols = pl.ds(pl.multiple_of(step * 256, 256), 256)
        left = cells(lambda off: x[pl.ds(off, 48), cols])
        mid[:, cols] = (left.astype(F32) + nn(att[...], fproj[:, cols])).astype(BF16)

    loads[2].wait()
    for k in range(4):
        merged[:, 512 * k : 512 * k + 512] = nn(mrg[k], mid[...]).astype(BF16)
    mgain = mgain_ref[...].astype(F32)
    result, centre, scale = norm_rows(merged[...], mgain)
    mnormed[...] = result
    mstat[0] = jnp.broadcast_to(centre, (CRS, 128))
    mstat[1] = jnp.broadcast_to(scale, (CRS, 128))
    loads[3].wait()

    @pl.loop(0, 4)
    def _(step):
        cols = pl.ds(pl.multiple_of(step * 256, 256), 256)
        c_in[:, cols] = nn(mnormed[...], mw[:, cols]).astype(BF16)

    cgain = cgain_ref[...].astype(F32)
    result, centre, scale = norm_rows(c_in[...], cgain)
    cnormed[...] = result
    cstat[0] = jnp.broadcast_to(centre, (CRS, 128))
    cstat[1] = jnp.broadcast_to(scale, (CRS, 128))
    loads[4].wait()

    @pl.loop(0, 6)
    def _(step):
        cols = pl.ds(pl.multiple_of(step * 512, 512), 512)
        value = nn(cnormed[...], cqkv[:, cols]).astype(BF16)
        cq[:, cols] = jnp.where(step < 2, value * 0.125, value).astype(BF16)

    def coarse_of(ref, start, group):
        return [ref[:, pair_slice(start, 4 * group + n)] for n in range(4)]

    @pl.loop(0, 2)
    def _(group):
        raised, inv, mixed = attend_all(
            coarse_of(cq, 0, group),
            coarse_of(cq, 1024, group),
            coarse_of(cq, 2048, group),
            [bias_c[...]] * 4,
        )
        for n in range(4):
            craised[4 * group + n] = raised[n]
            cinverse[4 * group + n] = inv[n]
            catt[:, pair_slice(0, 4 * group + n)] = mixed[n]

    loads[5].wait()
    for half in range(2):
        cols = slice(512 * half, 512 * half + 512)
        c_mid = (c_in[:, cols].astype(F32) + nn(catt[...], cproj[:, cols])).astype(BF16)
        for quad in range(4):
            off = C_OFF[quad]
            cback[quad, 48 * half : 48 * half + 48, :] = c_mid[off : off + 48]

    leave(cback, cback_hbm)

    dcot = jnp.concatenate([cot[0], cot[1]], axis=1)
    dcatt = nt(dcot, cproj[...]).astype(BF16)
    mnormed[:, 0:1024] = dcatt
    dcq = cq

    @pl.loop(0, 2)
    def _(group):
        d_query, d_keys, d_vals = back_all(
            coarse_of(cq, 0, group),
            coarse_of(cq, 1024, group),
            coarse_of(cq, 2048, group),
            [craised[4 * group + n] for n in range(4)],
            [cinverse[4 * group + n] for n in range(4)],
            coarse_of(catt, 0, group),
            coarse_of(mnormed, 0, group),
        )
        for n in range(4):
            dcq[:, pair_slice(0, 4 * group + n)] = d_query[n]
            dcq[:, pair_slice(1024, 4 * group + n)] = d_keys[n]
            dcq[:, pair_slice(2048, 4 * group + n)] = d_vals[n]

    @pl.loop(0, 4)
    def _(step):
        rows = pl.ds(pl.multiple_of(step * 256, 256), 256)
        cdnorm[:, rows] = nt(dcq[...], cqkv[rows, :])

    d_norm = norm_back(
        c_in[...], cgain, cstat[0][:, 0:1], cstat[1][:, 0:1], cdnorm[:, 0:1024].astype(BF16).astype(F32)
    )
    d_c = (dcot.astype(F32) + d_norm.astype(BF16).astype(F32)).astype(BF16)
    cnormed[...] = d_c

    @pl.loop(0, 4)
    def _(step):
        rows = pl.ds(pl.multiple_of(step * 512, 512), 512)
        cdnorm[:, rows] = nt(cnormed[...], mw[rows, :])

    d_merged = norm_back(
        merged[...], mgain, mstat[0][:, 0:1], mstat[1][:, 0:1], cdnorm[...].astype(BF16).astype(F32)
    ).astype(BF16)
    merged[...] = d_merged
    loads[6].wait()
    total = nn(mrg_t[0], merged[:, 0:512])
    for k in range(1, 4):
        total = total + nn(mrg_t[k], merged[:, 512 * k : 512 * k + 512])
    dmid[...] = total.astype(BF16)

    leave(dmid, dmid_hbm)
    datt[...] = nt(dmid[...], fproj[...]).astype(BF16)
    att_t[...] = att[...].T
    scale_out = 1.0 / math.sqrt(73728)

    for quad in range(4):
        for (_, rows), e_off in zip(PIECES, E_OFF[quad]):
            if rows > 48:
                dqkv[pl.ds(e_off + 48, rows - 48), 0:512] = jnp.zeros((rows - 48, 512), BF16)

    def terms(step, value):
        value = (value * scale_out).astype(BF16)
        low, high = value[:, 0:128], value[:, 128:256]
        for part in range(4):
            rows = slice(128 * part, 128 * part + 128)
            keep[part, step] = jnp.where(core == 0, low[rows], high[rows])
            send[part, step] = jnp.where(core == 0, high[rows], low[rows])

    @pl.loop(0, 2)
    def _(step):
        cols = pl.ds(pl.multiple_of(step * 256, 256), 256)
        terms(6 + step, nn(att_t[...], dmid[:, cols]))

    @pl.loop(0, 4)
    def _(pair):
        d_query, d_keys, d_vals = back_all(
            queries_of(qry, pair),
            keys_of(0, pair),
            keys_of(512, pair),
            [raised_at(index, pair)[...] for index in range(9)],
            [inverse[pair, pl.ds(2 * w[2], 2 * w[3]), :] for w in WINDOWS],
            queries_of(att, pair),
            queries_of(datt, pair),
        )
        for index, (e_off, rows, q_off, q_rows, kind) in enumerate(WINDOWS):
            step = 48 if kind == 3 else 80
            for part in range(q_rows // 48):
                dqkv[pl.ds(e_off + step * part, 48), pair_slice(0, pair)] = d_query[index][
                    48 * part : 48 * part + 48
                ]
            dqkv[pl.ds(e_off, rows), pair_slice(512, pair)] = d_keys[index]
            dqkv[pl.ds(e_off, rows), pair_slice(1024, pair)] = d_vals[index]

    leave(dqkv, dqkv_hbm)

    @pl.loop(0, 6)
    def _(step):
        cols = pl.ds(pl.multiple_of(step * 256, 256), 256)
        terms(step, nn(normed_t[...], dqkv[:, cols]))

    leave(keep, keep_hbm)
    leave(send, send_hbm)
    for copy in leaving:
        copy.wait()


def tokens_kernel(*refs):
    sources, outs, targets = refs[:7], refs[7:11], refs[11:18]
    built, padded, dnorm, sems, row_sems, out_sems = refs[18:]
    gain_in, fqkv, dqkv, dmid, cback, x, expand = targets
    copies = pull(sources[:2], targets[:2], sems)
    rows_in = []
    for part in range(4):
        rows = pl.ds(352 * part, 352)
        rows_in.append(
            pltpu.make_async_copy(sources[2].at[rows], dqkv.at[rows], row_sems.at[part])
        )
        rows_in[-1].start()
    for number in range(3, 7):
        copies.append(pltpu.make_async_copy(sources[number], targets[number], sems.at[number]))
        copies[-1].start()
    copies[0].wait()
    copies[1].wait()
    gain = gain_in[...].astype(F32).reshape(1, 512)
    for part in range(4):
        rows_in[part].wait()
        rows = pl.ds(352 * part, 352)
        dnorm[rows, :] = nt(dqkv[rows, :], fqkv[...])
    for copy in copies[2:]:
        copy.wait()
    pack = one_hot_back(expand[0:1, :], SROWS - TAIL)[:, :304]
    leaving = []
    for quad in (1, 2, 3, 0):
        out = built.at[quad]
        for (start, rows), e_off, q_off in zip(PIECES, E_OFF[quad], Q_OFF[quad]):
            spot = pl.ds(e_off, rows)
            d_norm = norm_back_fresh(x[spot, :], gain, dnorm[spot, :])
            head = d_norm[0:48] + dmid[pl.ds(q_off, 48), :].astype(F32)
            whole = jnp.concatenate([head, d_norm[48:]], axis=0) if rows > 48 else head
            if start == 0:
                out[0:TAIL, :] = whole.astype(BF16)
            else:
                padded[quad, start - TAIL : start - TAIL + rows, :] = whole.astype(BF16)
        padded[quad, 208:304, :] = cback[quad]
        out[TAIL:SROWS, :] = nn(pack, padded[quad]).astype(BF16)
        leaving.append(pltpu.make_async_copy(out, outs[quad], out_sems.at[quad]))
        leaving[-1].start()
    for copy in leaving:
        copy.wait()


def token_grads(*operands):
    return pl.pallas_call(
        tokens_kernel,
        out_shape=(jax.ShapeDtypeStruct((SROWS, 512), BF16),) * 4,
        in_specs=[HBM] * 7,
        out_specs=(HBM,) * 4,
        scratch_shapes=[pltpu.VMEM(value.shape, value.dtype) for value in operands]
        + [
            pltpu.VMEM((4, SROWS, 512), BF16),
            pltpu.VMEM((4, 304, 512), BF16),
            pltpu.VMEM((EXT, 512), F32),
            pltpu.SemaphoreType.DMA((7,)),
            pltpu.SemaphoreType.DMA((4,)),
            pltpu.SemaphoreType.DMA((4,)),
        ],
        cost_estimate=pl.CostEstimate(
            flops=2 * EXT * 1536 * 512, bytes_accessed=24 * 2**20, transcendentals=0
        ),
        compiler_params=pltpu.CompilerParams(vmem_limit_bytes=60 * 2**20),
    )(*operands)


def work(quads, fgain, mgain, cgain, fqkv, fproj, mrg, mrg_t, mw, cqkv, cproj, expand):
    scratch = [
        ((4, SROWS - TAIL, 512), BF16),
        ((8, 384), jnp.int32),
        ((EXT, 512), BF16),
        ((2, CRS, 512), BF16),
        ((512, 1536), BF16),
        ((512, 512), BF16),
        ((4, CRS, QRY), BF16),
        ((4, QRY, CRS), BF16),
        ((2048, 1024), BF16),
        ((1024, 3072), BF16),
        ((1024, 1024), BF16),
        None,
        ((EXT, 512), BF16),
        ((512, EXT), BF16),
        ((EXT, 1024), BF16),
        ((QRY, 512), BF16),
        ((QRY, 512), BF16),
        ((512, QRY), BF16),
        ((4, 4, 96, 144), BF16),
        ((4, 4, 192, 160), BF16),
        ((4, 384, 192), BF16),
        ((4, 2 * QRY, 128), F32),
        ((2, 192, 160), F32),
        ((384, 192), F32),
        ((QRY, 512), BF16),
        ((CRS, 2048), BF16),
        ((2, CRS, 128), F32),
        ((CRS, 2048), BF16),
        ((CRS, 1024), BF16),
        ((2, CRS, 128), F32),
        ((CRS, 1024), BF16),
        ((CRS, 3072), BF16),
        ((CRS, 1024), BF16),
        ((8, 384, 192), BF16),
        ((8, 384, 128), F32),
        ((QRY, 512), BF16),
        ((QRY, 512), BF16),
        ((EXT, 1536), BF16),
        ((CRS, 2048), F32),
        ((4, 96, 512), BF16),
        ((4, 8, 128, 128), BF16),
        ((4, 8, 128, 128), BF16),
        None,
    ]
    scratch = [
        pltpu.SemaphoreType.DMA((31,)) if item is None else pltpu.VMEM(*item) for item in scratch
    ]
    return pl.pallas_call(
        main_kernel,
        out_shape=(
            jax.ShapeDtypeStruct((4, 8, 128, 128), BF16),
            jax.ShapeDtypeStruct((4, 8, 128, 128), BF16),
            jax.ShapeDtypeStruct((EXT, 1536), BF16),
            jax.ShapeDtypeStruct((QRY, 512), BF16),
            jax.ShapeDtypeStruct((4, 96, 512), BF16),
            jax.ShapeDtypeStruct((EXT, 512), BF16),
        ),
        in_specs=[HBM] * 4 + [VMEM] * 3 + [HBM] * 8,
        out_specs=(HBM,) * 6,
        scratch_shapes=scratch,
        compiler_params=pltpu.CompilerParams(vmem_limit_bytes=60 * 2**20),
    )(*quads, fgain, mgain, cgain, fqkv, fproj, mrg, mrg_t, mw, cqkv, cproj, expand)


def shift(value, d_lat, d_lon):
    lats, lons = lax.axis_size("lat"), lax.axis_size("lon")
    pairs = []
    for a in range(lats):
        for b in range(lons):
            source = ((a + d_lat) % lats) * lons + (b + d_lon) % lons
            pairs.append((source, a * lons + b))
    return lax.ppermute(value, ("lat", "lon"), pairs)


def exchange(value, moves):
    lats, lons = lax.axis_size("lat"), lax.axis_size("lon")
    pairs = []
    for a in range(lats):
        for b in range(lons):
            to_a, to_b = moves(a, b)
            pairs.append((a * lons + b, to_a * lons + to_b))
    return lax.ppermute(value, ("lat", "lon"), pairs)


def spread(pieces, moves):
    total = pieces[0].astype(F32)
    for d in (1, 2, 3):
        total = total + exchange(pieces[d], lambda a, b: moves(a, b, d)).astype(F32)
    return total


def pieces_of(value, me):
    return [lax.dynamic_index_in_dim(value, me ^ d, 0, keepdims=False) for d in range(4)]


def local_grads(keep, send, lat):
    got = exchange(send, lambda a, b: (a, b ^ 1))
    pieces = []
    for mine, other in zip(pieces_of(keep, lat // 2), pieces_of(got, lat // 2)):
        pieces.append((mine.astype(F32) + other.astype(F32)).astype(BF16))
    return pieces


def local(
    tokens,
    land_sea,
    land_vec,
    fine_gain,
    fine_qkv,
    fine_proj,
    merge_gain,
    merge_weight,
    coarse_gain,
    coarse_qkv,
    coarse_proj,
    cotangent,
):
    pick, cpick, expand = jnp.asarray(PICK), jnp.asarray(CPICK), jnp.asarray(EXPAND)
    cot = cotangent.transpose(1, 2, 0, 3).reshape(72, 2, 1024)
    sends = prep(tokens.reshape(576, 512), land_sea, land_vec, cot, pick, cpick)
    quads = (sends[0], shift(sends[1], 1, 0), shift(sends[2], 0, 1), shift(sends[3], 1, 1))
    keep, send, dqkv, dmid, cback, x = work(
        quads,
        fine_gain.reshape(1, -1),
        merge_gain.reshape(1, -1),
        coarse_gain.reshape(1, -1),
        fine_qkv,
        fine_proj,
        jnp.asarray(MERGE, BF16),
        jnp.asarray(MERGE.transpose(0, 2, 1), BF16),
        merge_weight,
        coarse_qkv,
        coarse_proj,
        expand,
    )
    lat, lon = lax.axis_index("lat"), lax.axis_index("lon")
    pieces = local_grads(keep, send, lat)
    pieces, dqkv = lax.optimization_barrier((pieces, dqkv))
    back = token_grads(fine_gain, fine_qkv, dqkv, dmid, cback, x, expand)
    terms = spread(pieces, lambda a, b, d: (a ^ (2 * d), b)).astype(BF16)
    terms, _ = lax.optimization_barrier((terms, back))
    moved = (shift(back[1], -1, 0), shift(back[2], 0, -1), shift(back[3], -1, -1))
    terms = pieces_of(terms.reshape(4, 2, 128, 128), lon // 4)
    terms = spread(terms, lambda a, b, d: (a, b ^ (4 * d))).astype(BF16)
    terms, moved = lax.optimization_barrier((terms, moved))
    terms = pieces_of(terms.reshape(4, 64, 128), (lon // 2 % 2) * 2 + lat % 2)
    fine_grads = spread(terms, lambda a, b, d: (a ^ (d & 1), b ^ (d & 2)))
    grad, coarse = finish(pick, cpick, back[0], *moved)
    coarse = coarse.reshape(6, 12, 2, 1024).transpose(2, 0, 1, 3)
    return (coarse, grad.reshape(tokens.shape), fine_grads)


def solution(mesh):
    grid = P(None, "lat", "lon", None)
    placed = (grid, P("lat", "lon")) + (P(),) * 9 + (grid,)
    return jax.shard_map(
        local,
        mesh=mesh,
        in_specs=placed,
        out_specs=(grid, grid, P("lat", "lon")),
        check_vma=False,
    )
```

```python
import math

import jax
import jax.numpy as jnp
import numpy as np
from jax import lax
from jax.experimental import pallas as pl
from jax.experimental.pallas import tpu as pltpu
from jax.sharding import PartitionSpec as P

F32 = jnp.float32
BF16 = jnp.bfloat16
EPSILON = 1e-05
NEG = -1e30

QUADS = ((0, 0), (1, 0), (0, 1), (1, 1))
SROWS = 400
TAIL = 144
PIECES = ((0, 144), (144, 80), (224, 80), (304, 48))
EXT = 1408
QRY = 768
CRS = 192

E_OFF = {
    0: (0, 576, 896, 1216),
    1: (144, 736, 976, 1312),
    2: (288, 656, 1056, 1264),
    3: (432, 816, 1136, 1360),
}
Q_OFF = {
    0: (0, 192, 384, 576),
    1: (48, 288, 432, 672),
    2: (96, 240, 480, 624),
    3: (144, 336, 528, 720),
}
CORDER = (0, 2, 1, 3)
C_OFF = {quad: 48 * place for place, quad in enumerate(CORDER)}

WINDOWS = (
    (0, 144, 0, 48, 0),
    (144, 144, 48, 48, 0),
    (288, 144, 96, 48, 0),
    (432, 144, 144, 48, 0),
    (576, 160, 192, 96, 1),
    (736, 160, 288, 96, 1),
    (896, 160, 384, 96, 2),
    (1056, 160, 480, 96, 2),
    (1216, 192, 576, 192, 3),
)


def piece_cells(quad):
    qr, qc = QUADS[quad]
    near_r, far_r, mid_r = ((1, 0, 2), (4, 5, 3))[qr]
    near_c, far_c, mid_c = ((1, 0, 2), (4, 5, 3))[qc]
    return (
        ((near_r, near_c), (near_r, far_c), (far_r, near_c), (far_r, far_c)),
        ((near_r, mid_c), (far_r, mid_c)),
        ((mid_r, near_c), (mid_r, far_c)),
        ((mid_r, mid_c),),
    )


def build_tables():
    pick = np.full((8, 384), -1, np.int32)
    cell_query = {}
    for quad in range(4):
        qr, qc = QUADS[quad]
        place = 0
        for cells, q_off in zip(piece_cells(quad), Q_OFF[quad]):
            cell_query[cells[0]] = q_off
            for cr, cc in cells:
                for lev in range(2):
                    for i in range(3):
                        for j in range(6):
                            row = 3 * cr + i + 3 - 12 * qr
                            col = 6 * cc + j + 6 - 24 * qc
                            pick[quad, place] = lev * 288 + row * 24 + col
                            place += 1
    expand = np.full((8, 384), -1, np.int32)
    for start, first, rows in ((0, 0, 72), (80, 72, 72), (160, 144, 36), (208, 184, 36), (256, 220, 36)):
        expand[0, start : start + rows] = first + np.arange(rows)
    cpick = np.full((16, 128), -1, np.int32)
    merge = np.zeros((4, CRS, QRY), np.float32)
    for quad in range(4):
        qr, qc = QUADS[quad]
        for lev in range(2):
            for i in range(3):
                for j in range(6):
                    place = lev * 18 + i * 6 + j
                    row = i + 3 * (1 - qr)
                    col = j + 6 * (1 - qc)
                    spot = (row * 12 + col) * 2 + lev
                    cpick[quad, 72 + place] = spot
                    if place < 20:
                        cpick[4 + quad, 108 + place] = spot
                    else:
                        cpick[8 + quad, place - 20] = spot
                    for k, (di, dj) in enumerate(((0, 0), (1, 0), (0, 1), (1, 1))):
                        er = 3 + 2 * (3 * qr + i) + di
                        ec = 6 + 2 * (6 * qc + j) + dj
                        spot = cell_query[(er // 3, ec // 6)] + lev * 18 + (er % 3) * 6 + ec % 6
                        merge[k, C_OFF[quad] + place, spot] = 1
    return pick, cpick, expand, merge


PICK, CPICK, EXPAND, MERGE = build_tables()


def nn(left, right):
    return jnp.dot(left, right, preferred_element_type=F32)


def nt(left, right):
    return lax.dot_general(left, right, (((1,), (1,)), ((), ())), preferred_element_type=F32)


def tn(left, right):
    return lax.dot_general(left, right, (((0,), (0,)), ((), ())), preferred_element_type=F32)


def column(row):
    return jnp.broadcast_to(row, (128, 128)).T


def one_hot(row, count):
    blocks = []
    col = column(row)
    lane = lax.broadcasted_iota(jnp.int32, (128, 128), 1)
    for start in range(0, count, 128):
        hit = col == lane + start
        blocks.append(jnp.where(hit, 1.0, 0.0).astype(BF16))
    return jnp.concatenate(blocks, axis=1)[:, :count]


def one_hot_back(row, count):
    spot = lax.broadcasted_iota(jnp.int32, (count, row.shape[1]), 0)
    return jnp.where(spot == row, 1.0, 0.0).astype(BF16)


def pull(sources, targets, sems):
    copies = []
    for number, (source, target) in enumerate(zip(sources, targets)):
        copies.append(pltpu.make_async_copy(source, target, sems.at[number]))
        copies[-1].start()
    return copies


def prep_kernel(*refs):
    sources, outs, targets = refs[:6], refs[6:10], refs[10:16]
    tok, land_in, vec_in, cot_in, pick, cpick = targets
    square, stream, built, sems, out_sems = refs[16:]
    copies = pull(sources, targets, sems)
    square[...] = jnp.zeros_like(square)
    for number in (1, 2, 4, 0):
        copies[number].wait()
    square[0:12, 0:24] = land_in[...].astype(F32)
    flags = square[...].T
    vec = vec_in[...].astype(F32).reshape(1, 512)
    for step in range(12):
        row = 2 * step % 12
        land = jnp.concatenate([flags[0:24, row : row + 1], flags[0:24, row + 1 : row + 2]], axis=0)
        spot = slice(48 * step, 48 * step + 48)
        stream[spot, :] = (tok[spot, :].astype(F32) + land * vec).astype(BF16)
    copies[3].wait()
    copies[5].wait()
    cot = cot_in[...].reshape(144, 1024)
    leaving = []
    for quad in (1, 2, 3, 0):
        out = built.at[quad]
        choice = jnp.concatenate(
            [one_hot(pick[quad : quad + 1, n : n + 128], 576) for n in (0, 128, 256)], axis=0
        )
        value = nn(choice, stream[...])
        out[0:256, :] = value[0:256].astype(BF16)
        first = one_hot(cpick[quad : quad + 1, :], 144)
        second = one_hot(cpick[4 + quad : 5 + quad, :], 144)
        value = value[256:384] + nn(first, cot[:, 0:512]) + nn(second, cot[:, 512:1024])
        out[256:384, :] = value.astype(BF16)
        rest = one_hot(cpick[8 + quad : 9 + quad, :], 144)[:16]
        out[384:400, :] = nn(rest, cot[:, 512:1024]).astype(BF16)
        leaving.append(pltpu.make_async_copy(out, outs[quad], out_sems.at[quad]))
        leaving[-1].start()
    for copy in leaving:
        copy.wait()


HBM = pl.BlockSpec(memory_space=pltpu.HBM)
VMEM = pl.BlockSpec(memory_space=pltpu.VMEM)


def prep(tokens, land, vec, cot, pick, cpick):
    operands = (tokens, land, vec, cot, pick, cpick)
    return pl.pallas_call(
        prep_kernel,
        out_shape=(jax.ShapeDtypeStruct((SROWS, 512), BF16),) * 4,
        in_specs=[HBM] * 6,
        out_specs=(HBM,) * 4,
        scratch_shapes=[pltpu.VMEM(value.shape, value.dtype) for value in operands]
        + [
            pltpu.VMEM((128, 128), F32),
            pltpu.VMEM((576, 512), BF16),
            pltpu.VMEM((4, SROWS, 512), BF16),
            pltpu.SemaphoreType.DMA((6,)),
            pltpu.SemaphoreType.DMA((4,)),
        ],
        compiler_params=pltpu.CompilerParams(vmem_limit_bytes=60 * 2**20),
    )(*operands)


def finish_kernel(*refs):
    sources, grad_ref, coarse_ref, targets, sems = refs[:6], refs[6], refs[7], refs[8:14], refs[14]
    pick, cpick = targets[:2]
    copies = pull(sources, targets, sems)
    copies[0].wait()
    copies[1].wait()
    choices, firsts, seconds, rests = [], [], [], []
    for quad in range(4):
        choices.append(one_hot_back(pick[quad : quad + 1, :], 576))
        firsts.append(one_hot_back(cpick[quad : quad + 1, :], 144))
        seconds.append(one_hot_back(cpick[4 + quad : 5 + quad, :], 144))
        rests.append(one_hot_back(cpick[8 + quad : 9 + quad, :], 144)[:, :16])
    for copy in copies[2:]:
        copy.wait()

    def joined(low, high):
        return jnp.concatenate([ref[low:high, :] for ref in targets[2:]], axis=0)

    total = nn(jnp.concatenate(choices, axis=1), joined(0, 384))
    middle = joined(256, 384)
    left = nn(jnp.concatenate(firsts, axis=1), middle)
    right = nn(jnp.concatenate(seconds, axis=1), middle)
    for quad, ref in enumerate(targets[2:]):
        right = right + nn(rests[quad], ref[384:400, :])
    crs = jnp.concatenate([left, right], axis=1)
    grad_ref[...] = total.astype(BF16)
    coarse_ref[...] = crs.astype(BF16).reshape(72, 2, 1024)


def finish(*operands):
    return pl.pallas_call(
        finish_kernel,
        out_shape=(
            jax.ShapeDtypeStruct((576, 512), BF16),
            jax.ShapeDtypeStruct((72, 2, 1024), BF16),
        ),
        in_specs=[HBM] * 6,
        scratch_shapes=[pltpu.VMEM(value.shape, value.dtype) for value in operands]
        + [pltpu.SemaphoreType.DMA((6,))],
        compiler_params=pltpu.CompilerParams(vmem_limit_bytes=60 * 2**20),
    )(*operands)


def norm_rows(values, gain):
    wide = values.astype(F32)
    centre = jnp.mean(wide, axis=-1, keepdims=True)
    moved = wide - centre
    scale = lax.rsqrt(jnp.mean(moved * moved, axis=-1, keepdims=True) + EPSILON)
    return (moved * scale * gain).astype(BF16), centre, scale


def norm_back(values, gain, centre, scale, d_normed):
    hat = (values.astype(F32) - centre) * scale
    weighted = d_normed * gain
    first = jnp.mean(weighted, axis=-1, keepdims=True)
    second = jnp.mean(weighted * hat, axis=-1, keepdims=True)
    return scale * (weighted - first - hat * second)


def norm_back_fresh(values, gain, d_normed):
    wide = values.astype(F32)
    moved = wide - jnp.mean(wide, axis=-1, keepdims=True)
    scale = lax.rsqrt(jnp.mean(moved * moved, axis=-1, keepdims=True) + EPSILON)
    hat = moved * scale
    weighted = d_normed * gain
    first = jnp.mean(weighted, axis=-1, keepdims=True)
    second = jnp.mean(weighted * hat, axis=-1, keepdims=True)
    return scale * (weighted - first - hat * second)


def lane_masks(rows):
    lane = lax.broadcasted_iota(jnp.int32, (rows, 128), 1)
    return lane < 64


def stacked(values):
    low = lane_masks(values.shape[0])
    zero = jnp.zeros_like(values)
    return jnp.concatenate([jnp.where(low, values, zero), jnp.where(low, zero, values)], axis=0)


def unstacked(values):
    half = values.shape[0] // 2
    return jnp.where(lane_masks(half), values[:half], values[half:])


def attend_all(queries, keys, vals, biases):
    scores = [nt(stacked(query), key) for query, key in zip(queries, keys)]
    scores = [s if bias is None else s + bias for s, bias in zip(scores, biases)]
    tops = [jnp.max(s, axis=-1, keepdims=True) for s in scores]
    raised = [jnp.exp(s - top).astype(BF16) for s, top in zip(scores, tops)]
    wide = [nn(r, jnp.concatenate([v, jnp.ones_like(v)], axis=1)) for r, v in zip(raised, vals)]
    inverse = [1.0 / w[:, 128:] for w in wide]
    mixed = [unstacked(w[:, :128] * i).astype(BF16) for w, i in zip(wide, inverse)]
    return raised, inverse, mixed


def back_all(queries, keys, vals, raised, inverse, mixed, d_mixed):
    d_scaled = [stacked(d).astype(F32) * i for d, i in zip(d_mixed, inverse)]
    twice = [jnp.concatenate([m, m], axis=0).astype(F32) for m in mixed]
    delta = [jnp.sum(d * t, axis=-1, keepdims=True) for d, t in zip(d_scaled, twice)]
    d_short = [d.astype(BF16) for d in d_scaled]
    d_probs = [nt(d, v) for d, v in zip(d_short, vals)]
    d_vals = [tn(r, d).astype(BF16) for r, d in zip(raised, d_short)]
    d_scores = [(r.astype(F32) * (p - t)).astype(BF16) for r, p, t in zip(raised, d_probs, delta)]
    d_query = [(unstacked(nn(d, k)) * 0.125).astype(BF16) for d, k in zip(d_scores, keys)]
    d_keys = [tn(d, stacked(q)).astype(BF16) for d, q in zip(d_scores, queries)]
    return d_query, d_keys, d_vals


def pair_slice(start, pair):
    return pl.ds(pl.multiple_of(start + pair * 128, 128), 128)


def main_kernel(
    q0_ref,
    q1_ref,
    q2_ref,
    q3_ref,
    fgain_ref,
    mgain_ref,
    cgain_ref,
    fqkv_hbm,
    fproj_hbm,
    merge_hbm,
    merge_t_hbm,
    mw_hbm,
    cqkv_hbm,
    cproj_hbm,
    expand_hbm,
    keep_hbm,
    send_hbm,
    dqkv_hbm,
    dmid_hbm,
    cback_hbm,
    x_hbm,
    tails,
    expand,
    x,
    cot,
    fqkv,
    fproj,
    mrg,
    mrg_t,
    mw,
    cqkv,
    cproj,
    sems,
    normed,
    normed_t,
    kv,
    qry,
    att,
    att_t,
    raised_a,
    raised_b,
    raised_c,
    inverse,
    bias_b,
    bias_c,
    mid,
    merged,
    mstat,
    mnormed,
    c_in,
    cstat,
    cnormed,
    cq,
    catt,
    craised,
    cinverse,
    dmid,
    datt,
    dqkv,
    cdnorm,
    cback,
    keep,
    send,
    out_sems,
):
    last = jnp.where(lax.axis_index("lat") == lax.axis_size("lat") - 1, 1, 0)
    core = lax.axis_index("lon") % 2
    leaving = []

    def leave(src, dst):
        copy = pltpu.make_async_copy(src, dst, out_sems.at[len(leaving)])
        copy.start()
        leaving.append(copy)

    weights = (
        (fqkv_hbm, fqkv),
        (fproj_hbm, fproj),
        (merge_hbm, mrg),
        (mw_hbm, mw),
        (cqkv_hbm, cqkv),
        (cproj_hbm, cproj),
        (merge_t_hbm, mrg_t),
    )
    loads = [pltpu.make_async_copy(src, dst, sems.at[n]) for n, (src, dst) in enumerate(weights)]
    pulls = []
    number = len(loads)
    for quad, ref in enumerate((q0_ref, q1_ref, q2_ref, q3_ref)):
        pulls.append(
            pltpu.make_async_copy(
                ref.at[pl.ds(0, TAIL)], x.at[pl.ds(E_OFF[quad][0], TAIL)], sems.at[number]
            )
        )
        pulls.append(
            pltpu.make_async_copy(
                ref.at[pl.ds(TAIL, SROWS - TAIL)], tails.at[quad], sems.at[number + 1]
            )
        )
        number += 2
    pulls.append(pltpu.make_async_copy(expand_hbm, expand, sems.at[number]))
    for copy in pulls:
        copy.start()
    for copy in loads:
        copy.start()

    def bias_of(shape, q_rows, piece, valid, q_half, k_half, split):
        q_at = lax.broadcasted_iota(jnp.int32, shape, 0) % q_rows
        k_at = lax.broadcasted_iota(jnp.int32, shape, 1)
        bad = (k_at % piece) >= valid
        if split:
            other = (q_at >= q_half) != (k_at >= k_half)
            bad = jnp.logical_or(bad, jnp.logical_and(other, last == 1))
        return jnp.where(bad, NEG, 0.0)

    bias_b[0] = bias_of((192, 160), 96, 80, 72, 48, 80, False)
    bias_b[1] = bias_of((192, 160), 96, 80, 72, 48, 80, True)
    bias_c[...] = bias_of((384, 192), 192, 48, 36, 96, 96, True)

    spread_out = []
    for copy in pulls:
        copy.wait()
    for start in (0, 128, 256):
        spread_out.append(one_hot(expand[0:1, start : start + 128], 256))
    spread_out = jnp.concatenate(spread_out, axis=0)[:304]
    for quad in range(4):
        value = nn(spread_out, tails[quad]).astype(BF16)
        for (start, rows), off in list(zip(PIECES, E_OFF[quad]))[1:]:
            x[pl.ds(off, rows), :] = value[start - TAIL : start - TAIL + rows]
        for half in range(2):
            cot[half, pl.ds(C_OFF[quad], 48), :] = value[208 + 48 * half : 256 + 48 * half]
    leave(x, x_hbm)
    fgain = fgain_ref[...].astype(F32)

    @pl.loop(0, 11)
    def _(step):
        rows = pl.ds(pl.multiple_of(step * 128, 128), 128)
        result, _, _ = norm_rows(x[rows, :], fgain)
        normed[rows, :] = result
        normed_t[:, rows] = result.T

    def cells(read):
        parts = []
        for q_start in range(0, QRY, 48):
            for quad in range(4):
                for e_off, q_off in zip(E_OFF[quad], Q_OFF[quad]):
                    if q_off == q_start:
                        parts.append(read(e_off))
        return jnp.concatenate(parts, axis=0)

    loads[0].wait()

    for step in range(4):
        kv[:, pl.ds(step * 256, 256)] = nn(
            normed[...], fqkv[:, pl.ds(512 + step * 256, 256)]
        ).astype(BF16)

    @pl.loop(0, 2)
    def _(step):
        cols = pl.ds(pl.multiple_of(step * 256, 256), 256)
        left = cells(lambda off: normed[pl.ds(off, 48), :])
        qry[:, cols] = (nn(left, fqkv[:, cols]).astype(BF16) * 0.125).astype(BF16)

    def raised_at(index, pair):
        kind = WINDOWS[index][4]
        if kind == 0:
            return raised_a.at[pair, index]
        if kind == 3:
            return raised_c.at[pair]
        return raised_b.at[pair, index - 4]

    def bias_at(kind):
        if kind == 0:
            return None
        return bias_c[...] if kind == 3 else bias_b[kind - 1]

    def queries_of(ref, pair):
        return [ref[pl.ds(q_off, q_rows), pair_slice(0, pair)] for _, _, q_off, q_rows, _ in WINDOWS]

    def keys_of(start, pair):
        return [kv[pl.ds(e_off, rows), pair_slice(start, pair)] for e_off, rows, _, _, _ in WINDOWS]

    @pl.loop(0, 4)
    def _(pair):
        raised, inv, mixed = attend_all(
            queries_of(qry, pair),
            keys_of(0, pair),
            keys_of(512, pair),
            [bias_at(window[4]) for window in WINDOWS],
        )
        for index, (_, _, q_off, q_rows, _) in enumerate(WINDOWS):
            raised_at(index, pair)[...] = raised[index]
            inverse[pair, pl.ds(2 * q_off, 2 * q_rows), :] = inv[index]
            att[pl.ds(q_off, q_rows), pair_slice(0, pair)] = mixed[index]

    loads[1].wait()

    @pl.loop(0, 2)
    def _(step):
        cols = pl.ds(pl.multiple_of(step * 256, 256), 256)
        left = cells(lambda off: x[pl.ds(off, 48), cols])
        mid[:, cols] = (left.astype(F32) + nn(att[...], fproj[:, cols])).astype(BF16)

    loads[2].wait()
    for k in range(4):
        merged[:, 512 * k : 512 * k + 512] = nn(mrg[k], mid[...]).astype(BF16)
    mgain = mgain_ref[...].astype(F32)
    result, centre, scale = norm_rows(merged[...], mgain)
    mnormed[...] = result
    mstat[0] = jnp.broadcast_to(centre, (CRS, 128))
    mstat[1] = jnp.broadcast_to(scale, (CRS, 128))
    loads[3].wait()

    for step in range(4):
        cols = pl.ds(step * 256, 256)
        c_in[:, cols] = nn(mnormed[...], mw[:, cols]).astype(BF16)

    cgain = cgain_ref[...].astype(F32)
    result, centre, scale = norm_rows(c_in[...], cgain)
    cnormed[...] = result
    cstat[0] = jnp.broadcast_to(centre, (CRS, 128))
    cstat[1] = jnp.broadcast_to(scale, (CRS, 128))
    loads[4].wait()

    for step in range(6):
        cols = pl.ds(step * 512, 512)
        value = nn(cnormed[...], cqkv[:, cols]).astype(BF16)
        cq[:, cols] = (value * 0.125).astype(BF16) if step < 2 else value

    def coarse_of(ref, start, group):
        return [ref[:, pair_slice(start, 4 * group + n)] for n in range(4)]

    @pl.loop(0, 2)
    def _(group):
        raised, inv, mixed = attend_all(
            coarse_of(cq, 0, group),
            coarse_of(cq, 1024, group),
            coarse_of(cq, 2048, group),
            [bias_c[...]] * 4,
        )
        for n in range(4):
            craised[4 * group + n] = raised[n]
            cinverse[4 * group + n] = inv[n]
            catt[:, pair_slice(0, 4 * group + n)] = mixed[n]

    loads[5].wait()
    for half in range(2):
        cols = slice(512 * half, 512 * half + 512)
        c_mid = (c_in[:, cols].astype(F32) + nn(catt[...], cproj[:, cols])).astype(BF16)
        for quad in range(4):
            off = C_OFF[quad]
            cback[quad, 48 * half : 48 * half + 48, :] = c_mid[off : off + 48]

    leave(cback, cback_hbm)

    dcot = jnp.concatenate([cot[0], cot[1]], axis=1)
    dcatt = nt(dcot, cproj[...]).astype(BF16)
    mnormed[:, 0:1024] = dcatt
    dcq = cq

    @pl.loop(0, 2)
    def _(group):
        d_query, d_keys, d_vals = back_all(
            coarse_of(cq, 0, group),
            coarse_of(cq, 1024, group),
            coarse_of(cq, 2048, group),
            [craised[4 * group + n] for n in range(4)],
            [cinverse[4 * group + n] for n in range(4)],
            coarse_of(catt, 0, group),
            coarse_of(mnormed, 0, group),
        )
        for n in range(4):
            dcq[:, pair_slice(0, 4 * group + n)] = d_query[n]
            dcq[:, pair_slice(1024, 4 * group + n)] = d_keys[n]
            dcq[:, pair_slice(2048, 4 * group + n)] = d_vals[n]

    for step in range(4):
        rows = pl.ds(step * 256, 256)
        cdnorm[:, rows] = nt(dcq[...], cqkv[rows, :])

    d_norm = norm_back(
        c_in[...], cgain, cstat[0][:, 0:1], cstat[1][:, 0:1], cdnorm[:, 0:1024].astype(BF16).astype(F32)
    )
    d_c = (dcot.astype(F32) + d_norm.astype(BF16).astype(F32)).astype(BF16)
    cnormed[...] = d_c

    for step in range(4):
        rows = pl.ds(step * 512, 512)
        cdnorm[:, rows] = nt(cnormed[...], mw[rows, :])

    d_merged = norm_back(
        merged[...], mgain, mstat[0][:, 0:1], mstat[1][:, 0:1], cdnorm[...].astype(BF16).astype(F32)
    ).astype(BF16)
    merged[...] = d_merged
    loads[6].wait()
    total = nn(mrg_t[0], merged[:, 0:512])
    for k in range(1, 4):
        total = total + nn(mrg_t[k], merged[:, 512 * k : 512 * k + 512])
    dmid[...] = total.astype(BF16)

    leave(dmid, dmid_hbm)
    datt[...] = nt(dmid[...], fproj[...]).astype(BF16)
    att_t[...] = att[...].T
    scale_out = 1.0 / math.sqrt(73728)

    for quad in range(4):
        for (_, rows), e_off in zip(PIECES, E_OFF[quad]):
            if rows > 48:
                dqkv[pl.ds(e_off + 48, rows - 48), 0:512] = jnp.zeros((rows - 48, 512), BF16)

    def terms(step, value):
        value = (value * scale_out).astype(BF16)
        low, high = value[:, 0:128], value[:, 128:256]
        for part in range(4):
            rows = slice(128 * part, 128 * part + 128)
            keep[part, step] = jnp.where(core == 0, low[rows], high[rows])
            send[part, step] = jnp.where(core == 0, high[rows], low[rows])

    @pl.loop(0, 2)
    def _(step):
        cols = pl.ds(pl.multiple_of(step * 256, 256), 256)
        terms(6 + step, nn(att_t[...], dmid[:, cols]))

    @pl.loop(0, 4)
    def _(pair):
        d_query, d_keys, d_vals = back_all(
            queries_of(qry, pair),
            keys_of(0, pair),
            keys_of(512, pair),
            [raised_at(index, pair)[...] for index in range(9)],
            [inverse[pair, pl.ds(2 * w[2], 2 * w[3]), :] for w in WINDOWS],
            queries_of(att, pair),
            queries_of(datt, pair),
        )
        for index, (e_off, rows, q_off, q_rows, kind) in enumerate(WINDOWS):
            step = 48 if kind == 3 else 80
            for part in range(q_rows // 48):
                dqkv[pl.ds(e_off + step * part, 48), pair_slice(0, pair)] = d_query[index][
                    48 * part : 48 * part + 48
                ]
            dqkv[pl.ds(e_off, rows), pair_slice(512, pair)] = d_keys[index]
            dqkv[pl.ds(e_off, rows), pair_slice(1024, pair)] = d_vals[index]

    leave(dqkv, dqkv_hbm)

    @pl.loop(0, 6)
    def _(step):
        cols = pl.ds(pl.multiple_of(step * 256, 256), 256)
        terms(step, nn(normed_t[...], dqkv[:, cols]))

    leave(keep, keep_hbm)
    leave(send, send_hbm)
    for copy in leaving:
        copy.wait()


def tokens_kernel(*refs):
    sources, outs, targets = refs[:7], refs[7:11], refs[11:18]
    built, padded, dnorm, sems, row_sems, out_sems = refs[18:]
    gain_in, fqkv, dqkv, dmid, cback, x, expand = targets
    copies = pull(sources[:2], targets[:2], sems)
    rows_in = []
    for part in range(4):
        rows = pl.ds(352 * part, 352)
        rows_in.append(
            pltpu.make_async_copy(sources[2].at[rows], dqkv.at[rows], row_sems.at[part])
        )
        rows_in[-1].start()
    for number in range(3, 7):
        copies.append(pltpu.make_async_copy(sources[number], targets[number], sems.at[number]))
        copies[-1].start()
    copies[0].wait()
    copies[1].wait()
    gain = gain_in[...].astype(F32).reshape(1, 512)
    for part in range(4):
        rows_in[part].wait()
        rows = pl.ds(352 * part, 352)
        dnorm[rows, :] = nt(dqkv[rows, :], fqkv[...])
    for copy in copies[2:]:
        copy.wait()
    pack = one_hot_back(expand[0:1, :], SROWS - TAIL)[:, :304]
    leaving = []
    for quad in (1, 2, 3, 0):
        out = built.at[quad]
        for (start, rows), e_off, q_off in zip(PIECES, E_OFF[quad], Q_OFF[quad]):
            spot = pl.ds(e_off, rows)
            d_norm = norm_back_fresh(x[spot, :], gain, dnorm[spot, :])
            head = d_norm[0:48] + dmid[pl.ds(q_off, 48), :].astype(F32)
            whole = jnp.concatenate([head, d_norm[48:]], axis=0) if rows > 48 else head
            if start == 0:
                out[0:TAIL, :] = whole.astype(BF16)
            else:
                padded[quad, start - TAIL : start - TAIL + rows, :] = whole.astype(BF16)
        padded[quad, 208:304, :] = cback[quad]
        out[TAIL:SROWS, :] = nn(pack, padded[quad]).astype(BF16)
        leaving.append(pltpu.make_async_copy(out, outs[quad], out_sems.at[quad]))
        leaving[-1].start()
    for copy in leaving:
        copy.wait()


def token_grads(*operands):
    return pl.pallas_call(
        tokens_kernel,
        out_shape=(jax.ShapeDtypeStruct((SROWS, 512), BF16),) * 4,
        in_specs=[HBM] * 7,
        out_specs=(HBM,) * 4,
        scratch_shapes=[pltpu.VMEM(value.shape, value.dtype) for value in operands]
        + [
            pltpu.VMEM((4, SROWS, 512), BF16),
            pltpu.VMEM((4, 304, 512), BF16),
            pltpu.VMEM((EXT, 512), F32),
            pltpu.SemaphoreType.DMA((7,)),
            pltpu.SemaphoreType.DMA((4,)),
            pltpu.SemaphoreType.DMA((4,)),
        ],
        cost_estimate=pl.CostEstimate(
            flops=2 * EXT * 1536 * 512, bytes_accessed=24 * 2**20, transcendentals=0
        ),
        compiler_params=pltpu.CompilerParams(vmem_limit_bytes=60 * 2**20),
    )(*operands)


def work(quads, fgain, mgain, cgain, fqkv, fproj, mrg, mrg_t, mw, cqkv, cproj, expand):
    scratch = [
        ((4, SROWS - TAIL, 512), BF16),
        ((8, 384), jnp.int32),
        ((EXT, 512), BF16),
        ((2, CRS, 512), BF16),
        ((512, 1536), BF16),
        ((512, 512), BF16),
        ((4, CRS, QRY), BF16),
        ((4, QRY, CRS), BF16),
        ((2048, 1024), BF16),
        ((1024, 3072), BF16),
        ((1024, 1024), BF16),
        None,
        ((EXT, 512), BF16),
        ((512, EXT), BF16),
        ((EXT, 1024), BF16),
        ((QRY, 512), BF16),
        ((QRY, 512), BF16),
        ((512, QRY), BF16),
        ((4, 4, 96, 144), BF16),
        ((4, 4, 192, 160), BF16),
        ((4, 384, 192), BF16),
        ((4, 2 * QRY, 128), F32),
        ((2, 192, 160), F32),
        ((384, 192), F32),
        ((QRY, 512), BF16),
        ((CRS, 2048), BF16),
        ((2, CRS, 128), F32),
        ((CRS, 2048), BF16),
        ((CRS, 1024), BF16),
        ((2, CRS, 128), F32),
        ((CRS, 1024), BF16),
        ((CRS, 3072), BF16),
        ((CRS, 1024), BF16),
        ((8, 384, 192), BF16),
        ((8, 384, 128), F32),
        ((QRY, 512), BF16),
        ((QRY, 512), BF16),
        ((EXT, 1536), BF16),
        ((CRS, 2048), F32),
        ((4, 96, 512), BF16),
        ((4, 8, 128, 128), BF16),
        ((4, 8, 128, 128), BF16),
        None,
    ]
    scratch = [
        pltpu.SemaphoreType.DMA((31,)) if item is None else pltpu.VMEM(*item) for item in scratch
    ]
    return pl.pallas_call(
        main_kernel,
        out_shape=(
            jax.ShapeDtypeStruct((4, 8, 128, 128), BF16),
            jax.ShapeDtypeStruct((4, 8, 128, 128), BF16),
            jax.ShapeDtypeStruct((EXT, 1536), BF16),
            jax.ShapeDtypeStruct((QRY, 512), BF16),
            jax.ShapeDtypeStruct((4, 96, 512), BF16),
            jax.ShapeDtypeStruct((EXT, 512), BF16),
        ),
        in_specs=[HBM] * 4 + [VMEM] * 3 + [HBM] * 8,
        out_specs=(HBM,) * 6,
        scratch_shapes=scratch,
        compiler_params=pltpu.CompilerParams(vmem_limit_bytes=60 * 2**20),
    )(*quads, fgain, mgain, cgain, fqkv, fproj, mrg, mrg_t, mw, cqkv, cproj, expand)


def shift(value, d_lat, d_lon):
    lats, lons = lax.axis_size("lat"), lax.axis_size("lon")
    pairs = []
    for a in range(lats):
        for b in range(lons):
            source = ((a + d_lat) % lats) * lons + (b + d_lon) % lons
            pairs.append((source, a * lons + b))
    return lax.ppermute(value, ("lat", "lon"), pairs)


def exchange(value, moves):
    lats, lons = lax.axis_size("lat"), lax.axis_size("lon")
    pairs = []
    for a in range(lats):
        for b in range(lons):
            to_a, to_b = moves(a, b)
            pairs.append((a * lons + b, to_a * lons + to_b))
    return lax.ppermute(value, ("lat", "lon"), pairs)


def spread(pieces, moves):
    total = pieces[0].astype(F32)
    for d in (1, 2, 3):
        total = total + exchange(pieces[d], lambda a, b: moves(a, b, d)).astype(F32)
    return total


def pieces_of(value, me):
    return [lax.dynamic_index_in_dim(value, me ^ d, 0, keepdims=False) for d in range(4)]


def local_grads(keep, send, lat):
    got = exchange(send, lambda a, b: (a, b ^ 1))
    pieces = []
    for mine, other in zip(pieces_of(keep, lat // 2), pieces_of(got, lat // 2)):
        pieces.append((mine.astype(F32) + other.astype(F32)).astype(BF16))
    return pieces


def local(
    tokens,
    land_sea,
    land_vec,
    fine_gain,
    fine_qkv,
    fine_proj,
    merge_gain,
    merge_weight,
    coarse_gain,
    coarse_qkv,
    coarse_proj,
    cotangent,
):
    pick, cpick, expand = jnp.asarray(PICK), jnp.asarray(CPICK), jnp.asarray(EXPAND)
    cot = cotangent.transpose(1, 2, 0, 3).reshape(72, 2, 1024)
    sends = prep(tokens.reshape(576, 512), land_sea, land_vec, cot, pick, cpick)
    quads = (sends[0], shift(sends[1], 1, 0), shift(sends[2], 0, 1), shift(sends[3], 1, 1))
    keep, send, dqkv, dmid, cback, x = work(
        quads,
        fine_gain.reshape(1, -1),
        merge_gain.reshape(1, -1),
        coarse_gain.reshape(1, -1),
        fine_qkv,
        fine_proj,
        jnp.asarray(MERGE, BF16),
        jnp.asarray(MERGE.transpose(0, 2, 1), BF16),
        merge_weight,
        coarse_qkv,
        coarse_proj,
        expand,
    )
    lat, lon = lax.axis_index("lat"), lax.axis_index("lon")
    pieces = local_grads(keep, send, lat)
    pieces, dqkv = lax.optimization_barrier((pieces, dqkv))
    back = token_grads(fine_gain, fine_qkv, dqkv, dmid, cback, x, expand)
    terms = spread(pieces, lambda a, b, d: (a ^ (2 * d), b)).astype(BF16)
    terms, _ = lax.optimization_barrier((terms, back))
    moved = (shift(back[1], -1, 0), shift(back[2], 0, -1), shift(back[3], -1, -1))
    terms = pieces_of(terms.reshape(4, 2, 128, 128), lon // 4)
    terms = spread(terms, lambda a, b, d: (a, b ^ (4 * d))).astype(BF16)
    terms, moved = lax.optimization_barrier((terms, moved))
    terms = pieces_of(terms.reshape(4, 64, 128), (lon // 2 % 2) * 2 + lat % 2)
    fine_grads = spread(terms, lambda a, b, d: (a ^ (d & 1), b ^ (d & 2)))
    grad, coarse = finish(pick, cpick, back[0], *moved)
    coarse = coarse.reshape(6, 12, 2, 1024).transpose(2, 0, 1, 3)
    return (coarse, grad.reshape(tokens.shape), fine_grads)


def solution(mesh):
    grid = P(None, "lat", "lon", None)
    placed = (grid, P("lat", "lon")) + (P(),) * 9 + (grid,)
    return jax.shard_map(
        local,
        mesh=mesh,
        in_specs=placed,
        out_specs=(grid, grid, P("lat", "lon")),
        check_vma=False,
    )
```

```python
import math

import jax
import jax.numpy as jnp
import numpy as np
from jax import lax
from jax.experimental import pallas as pl
from jax.experimental.pallas import tpu as pltpu
from jax.sharding import PartitionSpec as P

F32 = jnp.float32
BF16 = jnp.bfloat16
EPSILON = 1e-05
NEG = -1e30

QUADS = ((0, 0), (1, 0), (0, 1), (1, 1))
SROWS = 400
TAIL = 144
PIECES = ((0, 144), (144, 80), (224, 80), (304, 48))
EXT = 1408
QRY = 768
CRS = 192

E_OFF = {
    0: (0, 576, 896, 1216),
    1: (144, 736, 976, 1312),
    2: (288, 656, 1056, 1264),
    3: (432, 816, 1136, 1360),
}
Q_OFF = {
    0: (0, 192, 384, 576),
    1: (48, 288, 432, 672),
    2: (96, 240, 480, 624),
    3: (144, 336, 528, 720),
}
CORDER = (0, 2, 1, 3)
C_OFF = {quad: 48 * place for place, quad in enumerate(CORDER)}

WINDOWS = (
    (0, 144, 0, 48, 0),
    (144, 144, 48, 48, 0),
    (288, 144, 96, 48, 0),
    (432, 144, 144, 48, 0),
    (576, 160, 192, 96, 1),
    (736, 160, 288, 96, 1),
    (896, 160, 384, 96, 2),
    (1056, 160, 480, 96, 2),
    (1216, 192, 576, 192, 3),
)


def piece_cells(quad):
    qr, qc = QUADS[quad]
    near_r, far_r, mid_r = ((1, 0, 2), (4, 5, 3))[qr]
    near_c, far_c, mid_c = ((1, 0, 2), (4, 5, 3))[qc]
    return (
        ((near_r, near_c), (near_r, far_c), (far_r, near_c), (far_r, far_c)),
        ((near_r, mid_c), (far_r, mid_c)),
        ((mid_r, near_c), (mid_r, far_c)),
        ((mid_r, mid_c),),
    )


def build_tables():
    pick = np.full((8, 384), -1, np.int32)
    cell_query = {}
    for quad in range(4):
        qr, qc = QUADS[quad]
        place = 0
        for cells, q_off in zip(piece_cells(quad), Q_OFF[quad]):
            cell_query[cells[0]] = q_off
            for cr, cc in cells:
                for lev in range(2):
                    for i in range(3):
                        for j in range(6):
                            row = 3 * cr + i + 3 - 12 * qr
                            col = 6 * cc + j + 6 - 24 * qc
                            pick[quad, place] = lev * 288 + row * 24 + col
                            place += 1
    expand = np.full((8, 384), -1, np.int32)
    for start, first, rows in ((0, 0, 72), (80, 72, 72), (160, 144, 36), (208, 184, 36), (256, 220, 36)):
        expand[0, start : start + rows] = first + np.arange(rows)
    cpick = np.full((16, 128), -1, np.int32)
    merge = np.zeros((4, CRS, QRY), np.float32)
    for quad in range(4):
        qr, qc = QUADS[quad]
        for lev in range(2):
            for i in range(3):
                for j in range(6):
                    place = lev * 18 + i * 6 + j
                    row = i + 3 * (1 - qr)
                    col = j + 6 * (1 - qc)
                    spot = (row * 12 + col) * 2 + lev
                    cpick[quad, 72 + place] = spot
                    if place < 20:
                        cpick[4 + quad, 108 + place] = spot
                    else:
                        cpick[8 + quad, place - 20] = spot
                    for k, (di, dj) in enumerate(((0, 0), (1, 0), (0, 1), (1, 1))):
                        er = 3 + 2 * (3 * qr + i) + di
                        ec = 6 + 2 * (6 * qc + j) + dj
                        spot = cell_query[(er // 3, ec // 6)] + lev * 18 + (er % 3) * 6 + ec % 6
                        merge[k, C_OFF[quad] + place, spot] = 1
    return pick, cpick, expand, merge


PICK, CPICK, EXPAND, MERGE = build_tables()


def nn(left, right):
    return jnp.dot(left, right, preferred_element_type=F32)


def nt(left, right):
    return lax.dot_general(left, right, (((1,), (1,)), ((), ())), preferred_element_type=F32)


def tn(left, right):
    return lax.dot_general(left, right, (((0,), (0,)), ((), ())), preferred_element_type=F32)


def column(row):
    return jnp.broadcast_to(row, (128, 128)).T


def one_hot(row, count):
    blocks = []
    col = column(row)
    lane = lax.broadcasted_iota(jnp.int32, (128, 128), 1)
    for start in range(0, count, 128):
        hit = col == lane + start
        blocks.append(jnp.where(hit, 1.0, 0.0).astype(BF16))
    return jnp.concatenate(blocks, axis=1)[:, :count]


def one_hot_back(row, count):
    spot = lax.broadcasted_iota(jnp.int32, (count, row.shape[1]), 0)
    return jnp.where(spot == row, 1.0, 0.0).astype(BF16)


def pull(sources, targets, sems):
    copies = []
    for number, (source, target) in enumerate(zip(sources, targets)):
        copies.append(pltpu.make_async_copy(source, target, sems.at[number]))
        copies[-1].start()
    return copies


def prep_kernel(*refs):
    sources, outs, targets = refs[:6], refs[6:10], refs[10:16]
    tok, land_in, vec_in, cot_in, pick, cpick = targets
    square, stream, built, sems, out_sems = refs[16:]
    copies = pull(sources, targets, sems)
    square[...] = jnp.zeros_like(square)
    for number in (1, 2, 4, 0):
        copies[number].wait()
    square[0:12, 0:24] = land_in[...].astype(F32)
    flags = square[...].T
    vec = vec_in[...].astype(F32).reshape(1, 512)
    for step in range(12):
        row = 2 * step % 12
        land = jnp.concatenate([flags[0:24, row : row + 1], flags[0:24, row + 1 : row + 2]], axis=0)
        spot = slice(48 * step, 48 * step + 48)
        stream[spot, :] = (tok[spot, :].astype(F32) + land * vec).astype(BF16)
    copies[3].wait()
    copies[5].wait()
    cot = cot_in[...].reshape(144, 1024)
    leaving = []
    for quad in (1, 2, 3, 0):
        out = built.at[quad]
        choice = jnp.concatenate(
            [one_hot(pick[quad : quad + 1, n : n + 128], 576) for n in (0, 128, 256)], axis=0
        )
        value = nn(choice, stream[...])
        out[0:256, :] = value[0:256].astype(BF16)
        first = one_hot(cpick[quad : quad + 1, :], 144)
        second = one_hot(cpick[4 + quad : 5 + quad, :], 144)
        value = value[256:384] + nn(first, cot[:, 0:512]) + nn(second, cot[:, 512:1024])
        out[256:384, :] = value.astype(BF16)
        rest = one_hot(cpick[8 + quad : 9 + quad, :], 144)[:16]
        out[384:400, :] = nn(rest, cot[:, 512:1024]).astype(BF16)
        leaving.append(pltpu.make_async_copy(out, outs[quad], out_sems.at[quad]))
        leaving[-1].start()
    for copy in leaving:
        copy.wait()


HBM = pl.BlockSpec(memory_space=pltpu.HBM)
VMEM = pl.BlockSpec(memory_space=pltpu.VMEM)


def prep(tokens, land, vec, cot, pick, cpick):
    operands = (tokens, land, vec, cot, pick, cpick)
    return pl.pallas_call(
        prep_kernel,
        out_shape=(jax.ShapeDtypeStruct((SROWS, 512), BF16),) * 4,
        in_specs=[HBM] * 6,
        out_specs=(HBM,) * 4,
        scratch_shapes=[pltpu.VMEM(value.shape, value.dtype) for value in operands]
        + [
            pltpu.VMEM((128, 128), F32),
            pltpu.VMEM((576, 512), BF16),
            pltpu.VMEM((4, SROWS, 512), BF16),
            pltpu.SemaphoreType.DMA((6,)),
            pltpu.SemaphoreType.DMA((4,)),
        ],
        compiler_params=pltpu.CompilerParams(vmem_limit_bytes=60 * 2**20),
    )(*operands)


def finish_kernel(*refs):
    sources, grad_ref, coarse_ref, targets, sems = refs[:6], refs[6], refs[7], refs[8:14], refs[14]
    pick, cpick = targets[:2]
    copies = pull(sources, targets, sems)
    copies[0].wait()
    copies[1].wait()
    choices, firsts, seconds, rests = [], [], [], []
    for quad in range(4):
        choices.append(one_hot_back(pick[quad : quad + 1, :], 576))
        firsts.append(one_hot_back(cpick[quad : quad + 1, :], 144))
        seconds.append(one_hot_back(cpick[4 + quad : 5 + quad, :], 144))
        rests.append(one_hot_back(cpick[8 + quad : 9 + quad, :], 144)[:, :16])
    for copy in copies[2:]:
        copy.wait()

    def joined(low, high):
        return jnp.concatenate([ref[low:high, :] for ref in targets[2:]], axis=0)

    total = nn(jnp.concatenate(choices, axis=1), joined(0, 384))
    middle = joined(256, 384)
    left = nn(jnp.concatenate(firsts, axis=1), middle)
    right = nn(jnp.concatenate(seconds, axis=1), middle)
    for quad, ref in enumerate(targets[2:]):
        right = right + nn(rests[quad], ref[384:400, :])
    crs = jnp.concatenate([left, right], axis=1)
    grad_ref[...] = total.astype(BF16)
    coarse_ref[...] = crs.astype(BF16).reshape(72, 2, 1024)


def finish(*operands):
    return pl.pallas_call(
        finish_kernel,
        out_shape=(
            jax.ShapeDtypeStruct((576, 512), BF16),
            jax.ShapeDtypeStruct((72, 2, 1024), BF16),
        ),
        in_specs=[HBM] * 6,
        scratch_shapes=[pltpu.VMEM(value.shape, value.dtype) for value in operands]
        + [pltpu.SemaphoreType.DMA((6,))],
        compiler_params=pltpu.CompilerParams(vmem_limit_bytes=60 * 2**20),
    )(*operands)


def norm_rows(values, gain):
    wide = values.astype(F32)
    centre = jnp.mean(wide, axis=-1, keepdims=True)
    moved = wide - centre
    scale = lax.rsqrt(jnp.mean(moved * moved, axis=-1, keepdims=True) + EPSILON)
    return (moved * scale * gain).astype(BF16), centre, scale


def norm_back(values, gain, centre, scale, d_normed):
    hat = (values.astype(F32) - centre) * scale
    weighted = d_normed * gain
    first = jnp.mean(weighted, axis=-1, keepdims=True)
    second = jnp.mean(weighted * hat, axis=-1, keepdims=True)
    return scale * (weighted - first - hat * second)


def norm_back_fresh(values, gain, d_normed):
    wide = values.astype(F32)
    moved = wide - jnp.mean(wide, axis=-1, keepdims=True)
    scale = lax.rsqrt(jnp.mean(moved * moved, axis=-1, keepdims=True) + EPSILON)
    hat = moved * scale
    weighted = d_normed * gain
    first = jnp.mean(weighted, axis=-1, keepdims=True)
    second = jnp.mean(weighted * hat, axis=-1, keepdims=True)
    return scale * (weighted - first - hat * second)


def lane_masks(rows):
    lane = lax.broadcasted_iota(jnp.int32, (rows, 128), 1)
    return lane < 64


def stacked(values):
    low = lane_masks(values.shape[0])
    zero = jnp.zeros_like(values)
    return jnp.concatenate([jnp.where(low, values, zero), jnp.where(low, zero, values)], axis=0)


def unstacked(values):
    half = values.shape[0] // 2
    return jnp.where(lane_masks(half), values[:half], values[half:])


def attend_all(queries, keys, vals, biases):
    scores = [nt(stacked(query), key) for query, key in zip(queries, keys)]
    scores = [s if bias is None else s + bias for s, bias in zip(scores, biases)]
    tops = [jnp.max(s, axis=-1, keepdims=True) for s in scores]
    raised = [jnp.exp(s - top).astype(BF16) for s, top in zip(scores, tops)]
    wide = [nn(r, jnp.concatenate([v, jnp.ones_like(v)], axis=1)) for r, v in zip(raised, vals)]
    inverse = [1.0 / w[:, 128:] for w in wide]
    mixed = [unstacked(w[:, :128] * i).astype(BF16) for w, i in zip(wide, inverse)]
    return raised, inverse, mixed


def back_all(queries, keys, vals, raised, inverse, mixed, d_mixed):
    d_scaled = [stacked(d).astype(F32) * i for d, i in zip(d_mixed, inverse)]
    twice = [jnp.concatenate([m, m], axis=0).astype(F32) for m in mixed]
    delta = [jnp.sum(d * t, axis=-1, keepdims=True) for d, t in zip(d_scaled, twice)]
    d_short = [d.astype(BF16) for d in d_scaled]
    d_probs = [nt(d, v) for d, v in zip(d_short, vals)]
    d_vals = [tn(r, d).astype(BF16) for r, d in zip(raised, d_short)]
    d_scores = [(r.astype(F32) * (p - t)).astype(BF16) for r, p, t in zip(raised, d_probs, delta)]
    d_query = [(unstacked(nn(d, k)) * 0.125).astype(BF16) for d, k in zip(d_scores, keys)]
    d_keys = [tn(d, stacked(q)).astype(BF16) for d, q in zip(d_scores, queries)]
    return d_query, d_keys, d_vals


def pair_slice(start, pair):
    return pl.ds(pl.multiple_of(start + pair * 128, 128), 128)


def main_kernel(
    q0_ref,
    q1_ref,
    q2_ref,
    q3_ref,
    fgain_ref,
    mgain_ref,
    cgain_ref,
    fqkv_hbm,
    fproj_hbm,
    merge_hbm,
    merge_t_hbm,
    mw_hbm,
    cqkv_hbm,
    cproj_hbm,
    expand_hbm,
    keep_hbm,
    send_hbm,
    dqkv_hbm,
    dmid_hbm,
    cback_hbm,
    x_hbm,
    tails,
    expand,
    x,
    cot,
    fqkv,
    fproj,
    mrg,
    mrg_t,
    mw,
    cqkv,
    cproj,
    sems,
    normed,
    normed_t,
    kv,
    qry,
    att,
    att_t,
    raised_a,
    raised_b,
    raised_c,
    inverse,
    bias_b,
    bias_c,
    mid,
    merged,
    mstat,
    mnormed,
    c_in,
    cstat,
    cnormed,
    cq,
    catt,
    craised,
    cinverse,
    dmid,
    datt,
    dqkv,
    cdnorm,
    cback,
    keep,
    send,
    out_sems,
):
    last = jnp.where(lax.axis_index("lat") == lax.axis_size("lat") - 1, 1, 0)
    core = lax.axis_index("lon") % 2
    leaving = []

    def leave(src, dst):
        copy = pltpu.make_async_copy(src, dst, out_sems.at[len(leaving)])
        copy.start()
        leaving.append(copy)

    weights = (
        (fqkv_hbm, fqkv),
        (fproj_hbm, fproj),
        (merge_hbm, mrg),
        (mw_hbm, mw),
        (cqkv_hbm, cqkv),
        (cproj_hbm, cproj),
        (merge_t_hbm, mrg_t),
    )
    loads = [pltpu.make_async_copy(src, dst, sems.at[n]) for n, (src, dst) in enumerate(weights)]
    pulls = []
    number = len(loads)
    for quad, ref in enumerate((q0_ref, q1_ref, q2_ref, q3_ref)):
        pulls.append(
            pltpu.make_async_copy(
                ref.at[pl.ds(0, TAIL)], x.at[pl.ds(E_OFF[quad][0], TAIL)], sems.at[number]
            )
        )
        pulls.append(
            pltpu.make_async_copy(
                ref.at[pl.ds(TAIL, SROWS - TAIL)], tails.at[quad], sems.at[number + 1]
            )
        )
        number += 2
    pulls.append(pltpu.make_async_copy(expand_hbm, expand, sems.at[number]))
    for copy in pulls:
        copy.start()
    for copy in loads:
        copy.start()

    def bias_of(shape, q_rows, piece, valid, q_half, k_half, split):
        q_at = lax.broadcasted_iota(jnp.int32, shape, 0) % q_rows
        k_at = lax.broadcasted_iota(jnp.int32, shape, 1)
        bad = (k_at % piece) >= valid
        if split:
            other = (q_at >= q_half) != (k_at >= k_half)
            bad = jnp.logical_or(bad, jnp.logical_and(other, last == 1))
        return jnp.where(bad, NEG, 0.0)

    bias_b[0] = bias_of((192, 160), 96, 80, 72, 48, 80, False)
    bias_b[1] = bias_of((192, 160), 96, 80, 72, 48, 80, True)
    bias_c[...] = bias_of((384, 192), 192, 48, 36, 96, 96, True)

    spread_out = []
    for copy in pulls:
        copy.wait()
    for start in (0, 128, 256):
        spread_out.append(one_hot(expand[0:1, start : start + 128], 256))
    spread_out = jnp.concatenate(spread_out, axis=0)[:304]
    for quad in range(4):
        value = nn(spread_out, tails[quad]).astype(BF16)
        for (start, rows), off in list(zip(PIECES, E_OFF[quad]))[1:]:
            x[pl.ds(off, rows), :] = value[start - TAIL : start - TAIL + rows]
        for half in range(2):
            cot[half, pl.ds(C_OFF[quad], 48), :] = value[208 + 48 * half : 256 + 48 * half]
    leave(x, x_hbm)
    fgain = fgain_ref[...].astype(F32)

    for step in range(11):
        rows = pl.ds(step * 128, 128)
        result, _, _ = norm_rows(x[rows, :], fgain)
        normed[rows, :] = result
        normed_t[:, rows] = result.T

    def cells(read):
        parts = []
        for q_start in range(0, QRY, 48):
            for quad in range(4):
                for e_off, q_off in zip(E_OFF[quad], Q_OFF[quad]):
                    if q_off == q_start:
                        parts.append(read(e_off))
        return jnp.concatenate(parts, axis=0)

    loads[0].wait()

    for step in range(4):
        kv[:, pl.ds(step * 256, 256)] = nn(
            normed[...], fqkv[:, pl.ds(512 + step * 256, 256)]
        ).astype(BF16)

    @pl.loop(0, 2)
    def _(step):
        cols = pl.ds(pl.multiple_of(step * 256, 256), 256)
        left = cells(lambda off: normed[pl.ds(off, 48), :])
        qry[:, cols] = (nn(left, fqkv[:, cols]).astype(BF16) * 0.125).astype(BF16)

    def raised_at(index, pair):
        kind = WINDOWS[index][4]
        if kind == 0:
            return raised_a.at[pair, index]
        if kind == 3:
            return raised_c.at[pair]
        return raised_b.at[pair, index - 4]

    def bias_at(kind):
        if kind == 0:
            return None
        return bias_c[...] if kind == 3 else bias_b[kind - 1]

    def queries_of(ref, pair):
        return [ref[pl.ds(q_off, q_rows), pair_slice(0, pair)] for _, _, q_off, q_rows, _ in WINDOWS]

    def keys_of(start, pair):
        return [kv[pl.ds(e_off, rows), pair_slice(start, pair)] for e_off, rows, _, _, _ in WINDOWS]

    @pl.loop(0, 4)
    def _(pair):
        raised, inv, mixed = attend_all(
            queries_of(qry, pair),
            keys_of(0, pair),
            keys_of(512, pair),
            [bias_at(window[4]) for window in WINDOWS],
        )
        for index, (_, _, q_off, q_rows, _) in enumerate(WINDOWS):
            raised_at(index, pair)[...] = raised[index]
            inverse[pair, pl.ds(2 * q_off, 2 * q_rows), :] = inv[index]
            att[pl.ds(q_off, q_rows), pair_slice(0, pair)] = mixed[index]

    loads[1].wait()

    @pl.loop(0, 2)
    def _(step):
        cols = pl.ds(pl.multiple_of(step * 256, 256), 256)
        left = cells(lambda off: x[pl.ds(off, 48), cols])
        mid[:, cols] = (left.astype(F32) + nn(att[...], fproj[:, cols])).astype(BF16)

    loads[2].wait()
    for k in range(4):
        merged[:, 512 * k : 512 * k + 512] = nn(mrg[k], mid[...]).astype(BF16)
    mgain = mgain_ref[...].astype(F32)
    result, centre, scale = norm_rows(merged[...], mgain)
    mnormed[...] = result
    mstat[0] = jnp.broadcast_to(centre, (CRS, 128))
    mstat[1] = jnp.broadcast_to(scale, (CRS, 128))
    loads[3].wait()

    for step in range(4):
        cols = pl.ds(step * 256, 256)
        c_in[:, cols] = nn(mnormed[...], mw[:, cols]).astype(BF16)

    cgain = cgain_ref[...].astype(F32)
    result, centre, scale = norm_rows(c_in[...], cgain)
    cnormed[...] = result
    cstat[0] = jnp.broadcast_to(centre, (CRS, 128))
    cstat[1] = jnp.broadcast_to(scale, (CRS, 128))
    loads[4].wait()

    for step in range(6):
        cols = pl.ds(step * 512, 512)
        value = nn(cnormed[...], cqkv[:, cols]).astype(BF16)
        cq[:, cols] = (value * 0.125).astype(BF16) if step < 2 else value

    def coarse_of(ref, start, group):
        return [ref[:, pair_slice(start, 4 * group + n)] for n in range(4)]

    @pl.loop(0, 2)
    def _(group):
        raised, inv, mixed = attend_all(
            coarse_of(cq, 0, group),
            coarse_of(cq, 1024, group),
            coarse_of(cq, 2048, group),
            [bias_c[...]] * 4,
        )
        for n in range(4):
            craised[4 * group + n] = raised[n]
            cinverse[4 * group + n] = inv[n]
            catt[:, pair_slice(0, 4 * group + n)] = mixed[n]

    loads[5].wait()
    for half in range(2):
        cols = slice(512 * half, 512 * half + 512)
        c_mid = (c_in[:, cols].astype(F32) + nn(catt[...], cproj[:, cols])).astype(BF16)
        for quad in range(4):
            off = C_OFF[quad]
            cback[quad, 48 * half : 48 * half + 48, :] = c_mid[off : off + 48]

    leave(cback, cback_hbm)

    dcot = jnp.concatenate([cot[0], cot[1]], axis=1)
    dcatt = nt(dcot, cproj[...]).astype(BF16)
    mnormed[:, 0:1024] = dcatt
    dcq = cq

    @pl.loop(0, 2)
    def _(group):
        d_query, d_keys, d_vals = back_all(
            coarse_of(cq, 0, group),
            coarse_of(cq, 1024, group),
            coarse_of(cq, 2048, group),
            [craised[4 * group + n] for n in range(4)],
            [cinverse[4 * group + n] for n in range(4)],
            coarse_of(catt, 0, group),
            coarse_of(mnormed, 0, group),
        )
        for n in range(4):
            dcq[:, pair_slice(0, 4 * group + n)] = d_query[n]
            dcq[:, pair_slice(1024, 4 * group + n)] = d_keys[n]
            dcq[:, pair_slice(2048, 4 * group + n)] = d_vals[n]

    for step in range(4):
        rows = pl.ds(step * 256, 256)
        cdnorm[:, rows] = nt(dcq[...], cqkv[rows, :])

    d_norm = norm_back(
        c_in[...], cgain, cstat[0][:, 0:1], cstat[1][:, 0:1], cdnorm[:, 0:1024].astype(BF16).astype(F32)
    )
    d_c = (dcot.astype(F32) + d_norm.astype(BF16).astype(F32)).astype(BF16)
    cnormed[...] = d_c

    for step in range(4):
        rows = pl.ds(step * 512, 512)
        cdnorm[:, rows] = nt(cnormed[...], mw[rows, :])

    d_merged = norm_back(
        merged[...], mgain, mstat[0][:, 0:1], mstat[1][:, 0:1], cdnorm[...].astype(BF16).astype(F32)
    ).astype(BF16)
    merged[...] = d_merged
    loads[6].wait()
    total = nn(mrg_t[0], merged[:, 0:512])
    for k in range(1, 4):
        total = total + nn(mrg_t[k], merged[:, 512 * k : 512 * k + 512])
    dmid[...] = total.astype(BF16)

    leave(dmid, dmid_hbm)
    datt[...] = nt(dmid[...], fproj[...]).astype(BF16)
    att_t[...] = att[...].T
    scale_out = 1.0 / math.sqrt(73728)

    for quad in range(4):
        for (_, rows), e_off in zip(PIECES, E_OFF[quad]):
            if rows > 48:
                dqkv[pl.ds(e_off + 48, rows - 48), 0:512] = jnp.zeros((rows - 48, 512), BF16)

    def terms(step, value):
        value = (value * scale_out).astype(BF16)
        low, high = value[:, 0:128], value[:, 128:256]
        for part in range(4):
            rows = slice(128 * part, 128 * part + 128)
            keep[part, step] = jnp.where(core == 0, low[rows], high[rows])
            send[part, step] = jnp.where(core == 0, high[rows], low[rows])

    for step in range(2):
        cols = pl.ds(step * 256, 256)
        terms(6 + step, nn(att_t[...], dmid[:, cols]))

    @pl.loop(0, 4)
    def _(pair):
        d_query, d_keys, d_vals = back_all(
            queries_of(qry, pair),
            keys_of(0, pair),
            keys_of(512, pair),
            [raised_at(index, pair)[...] for index in range(9)],
            [inverse[pair, pl.ds(2 * w[2], 2 * w[3]), :] for w in WINDOWS],
            queries_of(att, pair),
            queries_of(datt, pair),
        )
        for index, (e_off, rows, q_off, q_rows, kind) in enumerate(WINDOWS):
            step = 48 if kind == 3 else 80
            for part in range(q_rows // 48):
                dqkv[pl.ds(e_off + step * part, 48), pair_slice(0, pair)] = d_query[index][
                    48 * part : 48 * part + 48
                ]
            dqkv[pl.ds(e_off, rows), pair_slice(512, pair)] = d_keys[index]
            dqkv[pl.ds(e_off, rows), pair_slice(1024, pair)] = d_vals[index]

    leave(dqkv, dqkv_hbm)

    for step in range(6):
        cols = pl.ds(step * 256, 256)
        terms(step, nn(normed_t[...], dqkv[:, cols]))

    leave(keep, keep_hbm)
    leave(send, send_hbm)
    for copy in leaving:
        copy.wait()


def tokens_kernel(*refs):
    sources, outs, targets = refs[:7], refs[7:11], refs[11:18]
    built, padded, dnorm, sems, row_sems, out_sems = refs[18:]
    gain_in, fqkv, dqkv, dmid, cback, x, expand = targets
    copies = pull(sources[:2], targets[:2], sems)
    rows_in = []
    for part in range(4):
        rows = pl.ds(352 * part, 352)
        rows_in.append(
            pltpu.make_async_copy(sources[2].at[rows], dqkv.at[rows], row_sems.at[part])
        )
        rows_in[-1].start()
    for number in range(3, 7):
        copies.append(pltpu.make_async_copy(sources[number], targets[number], sems.at[number]))
        copies[-1].start()
    copies[0].wait()
    copies[1].wait()
    gain = gain_in[...].astype(F32).reshape(1, 512)
    for part in range(4):
        rows_in[part].wait()
        rows = pl.ds(352 * part, 352)
        dnorm[rows, :] = nt(dqkv[rows, :], fqkv[...])
    for copy in copies[2:]:
        copy.wait()
    pack = one_hot_back(expand[0:1, :], SROWS - TAIL)[:, :304]
    leaving = []
    for quad in (1, 2, 3, 0):
        out = built.at[quad]
        for (start, rows), e_off, q_off in zip(PIECES, E_OFF[quad], Q_OFF[quad]):
            spot = pl.ds(e_off, rows)
            d_norm = norm_back_fresh(x[spot, :], gain, dnorm[spot, :])
            head = d_norm[0:48] + dmid[pl.ds(q_off, 48), :].astype(F32)
            whole = jnp.concatenate([head, d_norm[48:]], axis=0) if rows > 48 else head
            if start == 0:
                out[0:TAIL, :] = whole.astype(BF16)
            else:
                padded[quad, start - TAIL : start - TAIL + rows, :] = whole.astype(BF16)
        padded[quad, 208:304, :] = cback[quad]
        out[TAIL:SROWS, :] = nn(pack, padded[quad]).astype(BF16)
        leaving.append(pltpu.make_async_copy(out, outs[quad], out_sems.at[quad]))
        leaving[-1].start()
    for copy in leaving:
        copy.wait()


def token_grads(*operands):
    return pl.pallas_call(
        tokens_kernel,
        out_shape=(jax.ShapeDtypeStruct((SROWS, 512), BF16),) * 4,
        in_specs=[HBM] * 7,
        out_specs=(HBM,) * 4,
        scratch_shapes=[pltpu.VMEM(value.shape, value.dtype) for value in operands]
        + [
            pltpu.VMEM((4, SROWS, 512), BF16),
            pltpu.VMEM((4, 304, 512), BF16),
            pltpu.VMEM((EXT, 512), F32),
            pltpu.SemaphoreType.DMA((7,)),
            pltpu.SemaphoreType.DMA((4,)),
            pltpu.SemaphoreType.DMA((4,)),
        ],
        cost_estimate=pl.CostEstimate(
            flops=2 * EXT * 1536 * 512, bytes_accessed=24 * 2**20, transcendentals=0
        ),
        compiler_params=pltpu.CompilerParams(vmem_limit_bytes=60 * 2**20),
    )(*operands)


def work(quads, fgain, mgain, cgain, fqkv, fproj, mrg, mrg_t, mw, cqkv, cproj, expand):
    scratch = [
        ((4, SROWS - TAIL, 512), BF16),
        ((8, 384), jnp.int32),
        ((EXT, 512), BF16),
        ((2, CRS, 512), BF16),
        ((512, 1536), BF16),
        ((512, 512), BF16),
        ((4, CRS, QRY), BF16),
        ((4, QRY, CRS), BF16),
        ((2048, 1024), BF16),
        ((1024, 3072), BF16),
        ((1024, 1024), BF16),
        None,
        ((EXT, 512), BF16),
        ((512, EXT), BF16),
        ((EXT, 1024), BF16),
        ((QRY, 512), BF16),
        ((QRY, 512), BF16),
        ((512, QRY), BF16),
        ((4, 4, 96, 144), BF16),
        ((4, 4, 192, 160), BF16),
        ((4, 384, 192), BF16),
        ((4, 2 * QRY, 128), F32),
        ((2, 192, 160), F32),
        ((384, 192), F32),
        ((QRY, 512), BF16),
        ((CRS, 2048), BF16),
        ((2, CRS, 128), F32),
        ((CRS, 2048), BF16),
        ((CRS, 1024), BF16),
        ((2, CRS, 128), F32),
        ((CRS, 1024), BF16),
        ((CRS, 3072), BF16),
        ((CRS, 1024), BF16),
        ((8, 384, 192), BF16),
        ((8, 384, 128), F32),
        ((QRY, 512), BF16),
        ((QRY, 512), BF16),
        ((EXT, 1536), BF16),
        ((CRS, 2048), F32),
        ((4, 96, 512), BF16),
        ((4, 8, 128, 128), BF16),
        ((4, 8, 128, 128), BF16),
        None,
    ]
    scratch = [
        pltpu.SemaphoreType.DMA((31,)) if item is None else pltpu.VMEM(*item) for item in scratch
    ]
    return pl.pallas_call(
        main_kernel,
        out_shape=(
            jax.ShapeDtypeStruct((4, 8, 128, 128), BF16),
            jax.ShapeDtypeStruct((4, 8, 128, 128), BF16),
            jax.ShapeDtypeStruct((EXT, 1536), BF16),
            jax.ShapeDtypeStruct((QRY, 512), BF16),
            jax.ShapeDtypeStruct((4, 96, 512), BF16),
            jax.ShapeDtypeStruct((EXT, 512), BF16),
        ),
        in_specs=[HBM] * 4 + [VMEM] * 3 + [HBM] * 8,
        out_specs=(HBM,) * 6,
        scratch_shapes=scratch,
        compiler_params=pltpu.CompilerParams(vmem_limit_bytes=60 * 2**20),
    )(*quads, fgain, mgain, cgain, fqkv, fproj, mrg, mrg_t, mw, cqkv, cproj, expand)


def shift(value, d_lat, d_lon):
    lats, lons = lax.axis_size("lat"), lax.axis_size("lon")
    pairs = []
    for a in range(lats):
        for b in range(lons):
            source = ((a + d_lat) % lats) * lons + (b + d_lon) % lons
            pairs.append((source, a * lons + b))
    return lax.ppermute(value, ("lat", "lon"), pairs)


def exchange(value, moves):
    lats, lons = lax.axis_size("lat"), lax.axis_size("lon")
    pairs = []
    for a in range(lats):
        for b in range(lons):
            to_a, to_b = moves(a, b)
            pairs.append((a * lons + b, to_a * lons + to_b))
    return lax.ppermute(value, ("lat", "lon"), pairs)


def spread(pieces, moves):
    total = pieces[0].astype(F32)
    for d in (1, 2, 3):
        total = total + exchange(pieces[d], lambda a, b: moves(a, b, d)).astype(F32)
    return total


def pieces_of(value, me):
    return [lax.dynamic_index_in_dim(value, me ^ d, 0, keepdims=False) for d in range(4)]


def local_grads(keep, send, lat):
    got = exchange(send, lambda a, b: (a, b ^ 1))
    pieces = []
    for mine, other in zip(pieces_of(keep, lat // 2), pieces_of(got, lat // 2)):
        pieces.append((mine.astype(F32) + other.astype(F32)).astype(BF16))
    return pieces


def local(
    tokens,
    land_sea,
    land_vec,
    fine_gain,
    fine_qkv,
    fine_proj,
    merge_gain,
    merge_weight,
    coarse_gain,
    coarse_qkv,
    coarse_proj,
    cotangent,
):
    pick, cpick, expand = jnp.asarray(PICK), jnp.asarray(CPICK), jnp.asarray(EXPAND)
    cot = cotangent.transpose(1, 2, 0, 3).reshape(72, 2, 1024)
    sends = prep(tokens.reshape(576, 512), land_sea, land_vec, cot, pick, cpick)
    quads = (sends[0], shift(sends[1], 1, 0), shift(sends[2], 0, 1), shift(sends[3], 1, 1))
    keep, send, dqkv, dmid, cback, x = work(
        quads,
        fine_gain.reshape(1, -1),
        merge_gain.reshape(1, -1),
        coarse_gain.reshape(1, -1),
        fine_qkv,
        fine_proj,
        jnp.asarray(MERGE, BF16),
        jnp.asarray(MERGE.transpose(0, 2, 1), BF16),
        merge_weight,
        coarse_qkv,
        coarse_proj,
        expand,
    )
    lat, lon = lax.axis_index("lat"), lax.axis_index("lon")
    pieces = local_grads(keep, send, lat)
    pieces, dqkv = lax.optimization_barrier((pieces, dqkv))
    back = token_grads(fine_gain, fine_qkv, dqkv, dmid, cback, x, expand)
    terms = spread(pieces, lambda a, b, d: (a ^ (2 * d), b)).astype(BF16)
    terms, _ = lax.optimization_barrier((terms, back))
    moved = (shift(back[1], -1, 0), shift(back[2], 0, -1), shift(back[3], -1, -1))
    terms = pieces_of(terms.reshape(4, 2, 128, 128), lon // 4)
    terms = spread(terms, lambda a, b, d: (a, b ^ (4 * d))).astype(BF16)
    terms, moved = lax.optimization_barrier((terms, moved))
    terms = pieces_of(terms.reshape(4, 64, 128), (lon // 2 % 2) * 2 + lat % 2)
    fine_grads = spread(terms, lambda a, b, d: (a ^ (d & 1), b ^ (d & 2)))
    grad, coarse = finish(pick, cpick, back[0], *moved)
    coarse = coarse.reshape(6, 12, 2, 1024).transpose(2, 0, 1, 3)
    return (coarse, grad.reshape(tokens.shape), fine_grads)


def solution(mesh):
    grid = P(None, "lat", "lon", None)
    placed = (grid, P("lat", "lon")) + (P(),) * 9 + (grid,)
    return jax.shard_map(
        local,
        mesh=mesh,
        in_specs=placed,
        out_specs=(grid, grid, P("lat", "lon")),
        check_vma=False,
    )
```

```python
import math

import jax
import jax.numpy as jnp
import numpy as np
from jax import lax
from jax.experimental import pallas as pl
from jax.experimental.pallas import tpu as pltpu
from jax.sharding import PartitionSpec as P

F32 = jnp.float32
BF16 = jnp.bfloat16
EPSILON = 1e-05
NEG = -1e30

QUADS = ((0, 0), (1, 0), (0, 1), (1, 1))
SROWS = 400
TAIL = 144
PIECES = ((0, 144), (144, 80), (224, 80), (304, 48))
EXT = 1408
QRY = 768
CRS = 192

E_OFF = {
    0: (0, 576, 896, 1216),
    1: (144, 736, 976, 1312),
    2: (288, 656, 1056, 1264),
    3: (432, 816, 1136, 1360),
}
Q_OFF = {
    0: (0, 192, 384, 576),
    1: (48, 288, 432, 672),
    2: (96, 240, 480, 624),
    3: (144, 336, 528, 720),
}
CORDER = (0, 2, 1, 3)
C_OFF = {quad: 48 * place for place, quad in enumerate(CORDER)}

WINDOWS = (
    (0, 144, 0, 48, 0),
    (144, 144, 48, 48, 0),
    (288, 144, 96, 48, 0),
    (432, 144, 144, 48, 0),
    (576, 160, 192, 96, 1),
    (736, 160, 288, 96, 1),
    (896, 160, 384, 96, 2),
    (1056, 160, 480, 96, 2),
    (1216, 192, 576, 192, 3),
)


def piece_cells(quad):
    qr, qc = QUADS[quad]
    near_r, far_r, mid_r = ((1, 0, 2), (4, 5, 3))[qr]
    near_c, far_c, mid_c = ((1, 0, 2), (4, 5, 3))[qc]
    return (
        ((near_r, near_c), (near_r, far_c), (far_r, near_c), (far_r, far_c)),
        ((near_r, mid_c), (far_r, mid_c)),
        ((mid_r, near_c), (mid_r, far_c)),
        ((mid_r, mid_c),),
    )


def build_tables():
    pick = np.full((8, 384), -1, np.int32)
    cell_query = {}
    for quad in range(4):
        qr, qc = QUADS[quad]
        place = 0
        for cells, q_off in zip(piece_cells(quad), Q_OFF[quad]):
            cell_query[cells[0]] = q_off
            for cr, cc in cells:
                for lev in range(2):
                    for i in range(3):
                        for j in range(6):
                            row = 3 * cr + i + 3 - 12 * qr
                            col = 6 * cc + j + 6 - 24 * qc
                            pick[quad, place] = lev * 288 + row * 24 + col
                            place += 1
    expand = np.full((8, 384), -1, np.int32)
    for start, first, rows in ((0, 0, 72), (80, 72, 72), (160, 144, 36), (208, 184, 36), (256, 220, 36)):
        expand[0, start : start + rows] = first + np.arange(rows)
    cpick = np.full((16, 128), -1, np.int32)
    merge = np.zeros((4, CRS, QRY), np.float32)
    for quad in range(4):
        qr, qc = QUADS[quad]
        for lev in range(2):
            for i in range(3):
                for j in range(6):
                    place = lev * 18 + i * 6 + j
                    row = i + 3 * (1 - qr)
                    col = j + 6 * (1 - qc)
                    spot = (row * 12 + col) * 2 + lev
                    cpick[quad, 72 + place] = spot
                    if place < 20:
                        cpick[4 + quad, 108 + place] = spot
                    else:
                        cpick[8 + quad, place - 20] = spot
                    for k, (di, dj) in enumerate(((0, 0), (1, 0), (0, 1), (1, 1))):
                        er = 3 + 2 * (3 * qr + i) + di
                        ec = 6 + 2 * (6 * qc + j) + dj
                        spot = cell_query[(er // 3, ec // 6)] + lev * 18 + (er % 3) * 6 + ec % 6
                        merge[k, C_OFF[quad] + place, spot] = 1
    return pick, cpick, expand, merge


PICK, CPICK, EXPAND, MERGE = build_tables()


def nn(left, right):
    return jnp.dot(left, right, preferred_element_type=F32)


def nt(left, right):
    return lax.dot_general(left, right, (((1,), (1,)), ((), ())), preferred_element_type=F32)


def tn(left, right):
    return lax.dot_general(left, right, (((0,), (0,)), ((), ())), preferred_element_type=F32)


def column(row):
    return jnp.broadcast_to(row, (128, 128)).T


def one_hot(row, count):
    blocks = []
    col = column(row)
    lane = lax.broadcasted_iota(jnp.int32, (128, 128), 1)
    for start in range(0, count, 128):
        hit = col == lane + start
        blocks.append(jnp.where(hit, 1.0, 0.0).astype(BF16))
    return jnp.concatenate(blocks, axis=1)[:, :count]


def one_hot_back(row, count):
    spot = lax.broadcasted_iota(jnp.int32, (count, row.shape[1]), 0)
    return jnp.where(spot == row, 1.0, 0.0).astype(BF16)


def pull(sources, targets, sems):
    copies = []
    for number, (source, target) in enumerate(zip(sources, targets)):
        copies.append(pltpu.make_async_copy(source, target, sems.at[number]))
        copies[-1].start()
    return copies


def prep_kernel(*refs):
    sources, outs, targets = refs[:6], refs[6:10], refs[10:16]
    tok, land_in, vec_in, cot_in, pick, cpick = targets
    square, stream, built, sems, out_sems = refs[16:]
    copies = pull(sources, targets, sems)
    square[...] = jnp.zeros_like(square)
    for number in (1, 2, 4, 0):
        copies[number].wait()
    square[0:12, 0:24] = land_in[...].astype(F32)
    flags = square[...].T
    vec = vec_in[...].astype(F32).reshape(1, 512)
    for step in range(12):
        row = 2 * step % 12
        land = jnp.concatenate([flags[0:24, row : row + 1], flags[0:24, row + 1 : row + 2]], axis=0)
        spot = slice(48 * step, 48 * step + 48)
        stream[spot, :] = (tok[spot, :].astype(F32) + land * vec).astype(BF16)
    copies[3].wait()
    copies[5].wait()
    cot = cot_in[...].reshape(144, 1024)
    leaving = []
    for quad in (1, 2, 3, 0):
        out = built.at[quad]
        choice = jnp.concatenate(
            [one_hot(pick[quad : quad + 1, n : n + 128], 576) for n in (0, 128, 256)], axis=0
        )
        value = nn(choice, stream[...])
        out[0:256, :] = value[0:256].astype(BF16)
        first = one_hot(cpick[quad : quad + 1, :], 144)
        second = one_hot(cpick[4 + quad : 5 + quad, :], 144)
        value = value[256:384] + nn(first, cot[:, 0:512]) + nn(second, cot[:, 512:1024])
        out[256:384, :] = value.astype(BF16)
        rest = one_hot(cpick[8 + quad : 9 + quad, :], 144)[:16]
        out[384:400, :] = nn(rest, cot[:, 512:1024]).astype(BF16)
        leaving.append(pltpu.make_async_copy(out, outs[quad], out_sems.at[quad]))
        leaving[-1].start()
    for copy in leaving:
        copy.wait()


HBM = pl.BlockSpec(memory_space=pltpu.HBM)
VMEM = pl.BlockSpec(memory_space=pltpu.VMEM)


def prep(tokens, land, vec, cot, pick, cpick):
    operands = (tokens, land, vec, cot, pick, cpick)
    return pl.pallas_call(
        prep_kernel,
        out_shape=(jax.ShapeDtypeStruct((SROWS, 512), BF16),) * 4,
        in_specs=[HBM] * 6,
        out_specs=(HBM,) * 4,
        scratch_shapes=[pltpu.VMEM(value.shape, value.dtype) for value in operands]
        + [
            pltpu.VMEM((128, 128), F32),
            pltpu.VMEM((576, 512), BF16),
            pltpu.VMEM((4, SROWS, 512), BF16),
            pltpu.SemaphoreType.DMA((6,)),
            pltpu.SemaphoreType.DMA((4,)),
        ],
        compiler_params=pltpu.CompilerParams(vmem_limit_bytes=60 * 2**20),
    )(*operands)


def finish_kernel(*refs):
    sources, grad_ref, coarse_ref, targets, sems = refs[:6], refs[6], refs[7], refs[8:14], refs[14]
    pick, cpick = targets[:2]
    copies = pull(sources, targets, sems)
    copies[0].wait()
    copies[1].wait()
    choices, firsts, seconds, rests = [], [], [], []
    for quad in range(4):
        choices.append(one_hot_back(pick[quad : quad + 1, :], 576))
        firsts.append(one_hot_back(cpick[quad : quad + 1, :], 144))
        seconds.append(one_hot_back(cpick[4 + quad : 5 + quad, :], 144))
        rests.append(one_hot_back(cpick[8 + quad : 9 + quad, :], 144)[:, :16])
    for copy in copies[2:]:
        copy.wait()

    def joined(low, high):
        return jnp.concatenate([ref[low:high, :] for ref in targets[2:]], axis=0)

    total = nn(jnp.concatenate(choices, axis=1), joined(0, 384))
    middle = joined(256, 384)
    left = nn(jnp.concatenate(firsts, axis=1), middle)
    right = nn(jnp.concatenate(seconds, axis=1), middle)
    for quad, ref in enumerate(targets[2:]):
        right = right + nn(rests[quad], ref[384:400, :])
    crs = jnp.concatenate([left, right], axis=1)
    grad_ref[...] = total.astype(BF16)
    coarse_ref[...] = crs.astype(BF16).reshape(72, 2, 1024)


def finish(*operands):
    return pl.pallas_call(
        finish_kernel,
        out_shape=(
            jax.ShapeDtypeStruct((576, 512), BF16),
            jax.ShapeDtypeStruct((72, 2, 1024), BF16),
        ),
        in_specs=[HBM] * 6,
        scratch_shapes=[pltpu.VMEM(value.shape, value.dtype) for value in operands]
        + [pltpu.SemaphoreType.DMA((6,))],
        compiler_params=pltpu.CompilerParams(vmem_limit_bytes=60 * 2**20),
    )(*operands)


def norm_rows(values, gain):
    wide = values.astype(F32)
    centre = jnp.mean(wide, axis=-1, keepdims=True)
    moved = wide - centre
    scale = lax.rsqrt(jnp.mean(moved * moved, axis=-1, keepdims=True) + EPSILON)
    return (moved * scale * gain).astype(BF16), centre, scale


def norm_back(values, gain, centre, scale, d_normed):
    hat = (values.astype(F32) - centre) * scale
    weighted = d_normed * gain
    first = jnp.mean(weighted, axis=-1, keepdims=True)
    second = jnp.mean(weighted * hat, axis=-1, keepdims=True)
    return scale * (weighted - first - hat * second)


def norm_back_fresh(values, gain, d_normed):
    wide = values.astype(F32)
    moved = wide - jnp.mean(wide, axis=-1, keepdims=True)
    scale = lax.rsqrt(jnp.mean(moved * moved, axis=-1, keepdims=True) + EPSILON)
    hat = moved * scale
    weighted = d_normed * gain
    first = jnp.mean(weighted, axis=-1, keepdims=True)
    second = jnp.mean(weighted * hat, axis=-1, keepdims=True)
    return scale * (weighted - first - hat * second)


def lane_masks(rows):
    lane = lax.broadcasted_iota(jnp.int32, (rows, 128), 1)
    return lane < 64


def stacked(values):
    low = lane_masks(values.shape[0])
    zero = jnp.zeros_like(values)
    return jnp.concatenate([jnp.where(low, values, zero), jnp.where(low, zero, values)], axis=0)


def unstacked(values):
    half = values.shape[0] // 2
    return jnp.where(lane_masks(half), values[:half], values[half:])


def attend_all(queries, keys, vals, biases):
    scores = [nt(stacked(query), key) for query, key in zip(queries, keys)]
    scores = [s if bias is None else s + bias for s, bias in zip(scores, biases)]
    tops = [jnp.max(s, axis=-1, keepdims=True) for s in scores]
    raised = [jnp.exp(s - top).astype(BF16) for s, top in zip(scores, tops)]
    wide = [nn(r, jnp.concatenate([v, jnp.ones_like(v)], axis=1)) for r, v in zip(raised, vals)]
    inverse = [1.0 / w[:, 128:] for w in wide]
    mixed = [unstacked(w[:, :128] * i).astype(BF16) for w, i in zip(wide, inverse)]
    return raised, inverse, mixed


def back_all(queries, keys, vals, raised, inverse, mixed, d_mixed):
    d_scaled = [stacked(d).astype(F32) * i for d, i in zip(d_mixed, inverse)]
    twice = [jnp.concatenate([m, m], axis=0).astype(F32) for m in mixed]
    delta = [jnp.sum(d * t, axis=-1, keepdims=True) for d, t in zip(d_scaled, twice)]
    d_short = [d.astype(BF16) for d in d_scaled]
    d_probs = [nt(d, v) for d, v in zip(d_short, vals)]
    d_vals = [tn(r, d).astype(BF16) for r, d in zip(raised, d_short)]
    d_scores = [(r.astype(F32) * (p - t)).astype(BF16) for r, p, t in zip(raised, d_probs, delta)]
    d_query = [(unstacked(nn(d, k)) * 0.125).astype(BF16) for d, k in zip(d_scores, keys)]
    d_keys = [tn(d, stacked(q)).astype(BF16) for d, q in zip(d_scores, queries)]
    return d_query, d_keys, d_vals


def pair_slice(start, pair):
    if isinstance(pair, int):
        return pl.ds(start + pair * 128, 128)
    return pl.ds(pl.multiple_of(start + pair * 128, 128), 128)


def main_kernel(
    q0_ref,
    q1_ref,
    q2_ref,
    q3_ref,
    fgain_ref,
    mgain_ref,
    cgain_ref,
    fqkv_hbm,
    fproj_hbm,
    merge_hbm,
    merge_t_hbm,
    mw_hbm,
    cqkv_hbm,
    cproj_hbm,
    expand_hbm,
    keep_hbm,
    send_hbm,
    dqkv_hbm,
    dmid_hbm,
    cback_hbm,
    x_hbm,
    tails,
    expand,
    x,
    cot,
    fqkv,
    fproj,
    mrg,
    mrg_t,
    mw,
    cqkv,
    cproj,
    sems,
    normed,
    normed_t,
    kv,
    qry,
    att,
    att_t,
    raised_a,
    raised_b,
    raised_c,
    inverse,
    bias_b,
    bias_c,
    mid,
    merged,
    mstat,
    mnormed,
    c_in,
    cstat,
    cnormed,
    cq,
    catt,
    craised,
    cinverse,
    dmid,
    datt,
    dqkv,
    cdnorm,
    cback,
    keep,
    send,
    out_sems,
):
    last = jnp.where(lax.axis_index("lat") == lax.axis_size("lat") - 1, 1, 0)
    core = lax.axis_index("lon") % 2
    leaving = []

    def leave(src, dst):
        copy = pltpu.make_async_copy(src, dst, out_sems.at[len(leaving)])
        copy.start()
        leaving.append(copy)

    weights = (
        (fqkv_hbm, fqkv),
        (fproj_hbm, fproj),
        (merge_hbm, mrg),
        (mw_hbm, mw),
        (cqkv_hbm, cqkv),
        (cproj_hbm, cproj),
        (merge_t_hbm, mrg_t),
    )
    loads = [pltpu.make_async_copy(src, dst, sems.at[n]) for n, (src, dst) in enumerate(weights)]
    pulls = []
    number = len(loads)
    for quad, ref in enumerate((q0_ref, q1_ref, q2_ref, q3_ref)):
        pulls.append(
            pltpu.make_async_copy(
                ref.at[pl.ds(0, TAIL)], x.at[pl.ds(E_OFF[quad][0], TAIL)], sems.at[number]
            )
        )
        pulls.append(
            pltpu.make_async_copy(
                ref.at[pl.ds(TAIL, SROWS - TAIL)], tails.at[quad], sems.at[number + 1]
            )
        )
        number += 2
    pulls.append(pltpu.make_async_copy(expand_hbm, expand, sems.at[number]))
    for copy in pulls:
        copy.start()
    for copy in loads:
        copy.start()

    def bias_of(shape, q_rows, piece, valid, q_half, k_half, split):
        q_at = lax.broadcasted_iota(jnp.int32, shape, 0) % q_rows
        k_at = lax.broadcasted_iota(jnp.int32, shape, 1)
        bad = (k_at % piece) >= valid
        if split:
            other = (q_at >= q_half) != (k_at >= k_half)
            bad = jnp.logical_or(bad, jnp.logical_and(other, last == 1))
        return jnp.where(bad, NEG, 0.0)

    bias_b[0] = bias_of((192, 160), 96, 80, 72, 48, 80, False)
    bias_b[1] = bias_of((192, 160), 96, 80, 72, 48, 80, True)
    bias_c[...] = bias_of((384, 192), 192, 48, 36, 96, 96, True)

    spread_out = []
    for copy in pulls:
        copy.wait()
    for start in (0, 128, 256):
        spread_out.append(one_hot(expand[0:1, start : start + 128], 256))
    spread_out = jnp.concatenate(spread_out, axis=0)[:304]
    for quad in range(4):
        value = nn(spread_out, tails[quad]).astype(BF16)
        for (start, rows), off in list(zip(PIECES, E_OFF[quad]))[1:]:
            x[pl.ds(off, rows), :] = value[start - TAIL : start - TAIL + rows]
        for half in range(2):
            cot[half, pl.ds(C_OFF[quad], 48), :] = value[208 + 48 * half : 256 + 48 * half]
    leave(x, x_hbm)
    fgain = fgain_ref[...].astype(F32)

    for step in range(11):
        rows = pl.ds(step * 128, 128)
        result, _, _ = norm_rows(x[rows, :], fgain)
        normed[rows, :] = result
        normed_t[:, rows] = result.T

    def cells(read):
        parts = []
        for q_start in range(0, QRY, 48):
            for quad in range(4):
                for e_off, q_off in zip(E_OFF[quad], Q_OFF[quad]):
                    if q_off == q_start:
                        parts.append(read(e_off))
        return jnp.concatenate(parts, axis=0)

    loads[0].wait()

    for step in range(4):
        kv[:, pl.ds(step * 256, 256)] = nn(
            normed[...], fqkv[:, pl.ds(512 + step * 256, 256)]
        ).astype(BF16)

    for step in range(2):
        cols = pl.ds(step * 256, 256)
        left = cells(lambda off: normed[pl.ds(off, 48), :])
        qry[:, cols] = (nn(left, fqkv[:, cols]).astype(BF16) * 0.125).astype(BF16)

    def raised_at(index, pair):
        kind = WINDOWS[index][4]
        if kind == 0:
            return raised_a.at[pair, index]
        if kind == 3:
            return raised_c.at[pair]
        return raised_b.at[pair, index - 4]

    def bias_at(kind):
        if kind == 0:
            return None
        return bias_c[...] if kind == 3 else bias_b[kind - 1]

    def queries_of(ref, pair):
        return [ref[pl.ds(q_off, q_rows), pair_slice(0, pair)] for _, _, q_off, q_rows, _ in WINDOWS]

    def keys_of(start, pair):
        return [kv[pl.ds(e_off, rows), pair_slice(start, pair)] for e_off, rows, _, _, _ in WINDOWS]

    @pl.loop(0, 4)
    def _(pair):
        raised, inv, mixed = attend_all(
            queries_of(qry, pair),
            keys_of(0, pair),
            keys_of(512, pair),
            [bias_at(window[4]) for window in WINDOWS],
        )
        for index, (_, _, q_off, q_rows, _) in enumerate(WINDOWS):
            raised_at(index, pair)[...] = raised[index]
            inverse[pair, pl.ds(2 * q_off, 2 * q_rows), :] = inv[index]
            att[pl.ds(q_off, q_rows), pair_slice(0, pair)] = mixed[index]

    loads[1].wait()

    for step in range(2):
        cols = pl.ds(step * 256, 256)
        left = cells(lambda off: x[pl.ds(off, 48), cols])
        mid[:, cols] = (left.astype(F32) + nn(att[...], fproj[:, cols])).astype(BF16)

    loads[2].wait()
    for k in range(4):
        merged[:, 512 * k : 512 * k + 512] = nn(mrg[k], mid[...]).astype(BF16)
    mgain = mgain_ref[...].astype(F32)
    result, centre, scale = norm_rows(merged[...], mgain)
    mnormed[...] = result
    mstat[0] = jnp.broadcast_to(centre, (CRS, 128))
    mstat[1] = jnp.broadcast_to(scale, (CRS, 128))
    loads[3].wait()

    for step in range(4):
        cols = pl.ds(step * 256, 256)
        c_in[:, cols] = nn(mnormed[...], mw[:, cols]).astype(BF16)

    cgain = cgain_ref[...].astype(F32)
    result, centre, scale = norm_rows(c_in[...], cgain)
    cnormed[...] = result
    cstat[0] = jnp.broadcast_to(centre, (CRS, 128))
    cstat[1] = jnp.broadcast_to(scale, (CRS, 128))
    loads[4].wait()

    for step in range(6):
        cols = pl.ds(step * 512, 512)
        value = nn(cnormed[...], cqkv[:, cols]).astype(BF16)
        cq[:, cols] = (value * 0.125).astype(BF16) if step < 2 else value

    def coarse_of(ref, start, group):
        return [ref[:, pair_slice(start, 4 * group + n)] for n in range(4)]

    for group in range(2):
        raised, inv, mixed = attend_all(
            coarse_of(cq, 0, group),
            coarse_of(cq, 1024, group),
            coarse_of(cq, 2048, group),
            [bias_c[...]] * 4,
        )
        for n in range(4):
            craised[4 * group + n] = raised[n]
            cinverse[4 * group + n] = inv[n]
            catt[:, pair_slice(0, 4 * group + n)] = mixed[n]

    loads[5].wait()
    for half in range(2):
        cols = slice(512 * half, 512 * half + 512)
        c_mid = (c_in[:, cols].astype(F32) + nn(catt[...], cproj[:, cols])).astype(BF16)
        for quad in range(4):
            off = C_OFF[quad]
            cback[quad, 48 * half : 48 * half + 48, :] = c_mid[off : off + 48]

    leave(cback, cback_hbm)

    dcot = jnp.concatenate([cot[0], cot[1]], axis=1)
    dcatt = nt(dcot, cproj[...]).astype(BF16)
    mnormed[:, 0:1024] = dcatt
    dcq = cq

    for group in range(2):
        d_query, d_keys, d_vals = back_all(
            coarse_of(cq, 0, group),
            coarse_of(cq, 1024, group),
            coarse_of(cq, 2048, group),
            [craised[4 * group + n] for n in range(4)],
            [cinverse[4 * group + n] for n in range(4)],
            coarse_of(catt, 0, group),
            coarse_of(mnormed, 0, group),
        )
        for n in range(4):
            dcq[:, pair_slice(0, 4 * group + n)] = d_query[n]
            dcq[:, pair_slice(1024, 4 * group + n)] = d_keys[n]
            dcq[:, pair_slice(2048, 4 * group + n)] = d_vals[n]

    for step in range(4):
        rows = pl.ds(step * 256, 256)
        cdnorm[:, rows] = nt(dcq[...], cqkv[rows, :])

    d_norm = norm_back(
        c_in[...], cgain, cstat[0][:, 0:1], cstat[1][:, 0:1], cdnorm[:, 0:1024].astype(BF16).astype(F32)
    )
    d_c = (dcot.astype(F32) + d_norm.astype(BF16).astype(F32)).astype(BF16)
    cnormed[...] = d_c

    for step in range(4):
        rows = pl.ds(step * 512, 512)
        cdnorm[:, rows] = nt(cnormed[...], mw[rows, :])

    d_merged = norm_back(
        merged[...], mgain, mstat[0][:, 0:1], mstat[1][:, 0:1], cdnorm[...].astype(BF16).astype(F32)
    ).astype(BF16)
    merged[...] = d_merged
    loads[6].wait()
    total = nn(mrg_t[0], merged[:, 0:512])
    for k in range(1, 4):
        total = total + nn(mrg_t[k], merged[:, 512 * k : 512 * k + 512])
    dmid[...] = total.astype(BF16)

    leave(dmid, dmid_hbm)
    datt[...] = nt(dmid[...], fproj[...]).astype(BF16)
    att_t[...] = att[...].T
    scale_out = 1.0 / math.sqrt(73728)

    for quad in range(4):
        for (_, rows), e_off in zip(PIECES, E_OFF[quad]):
            if rows > 48:
                dqkv[pl.ds(e_off + 48, rows - 48), 0:512] = jnp.zeros((rows - 48, 512), BF16)

    def terms(step, value):
        value = (value * scale_out).astype(BF16)
        low, high = value[:, 0:128], value[:, 128:256]
        for part in range(4):
            rows = slice(128 * part, 128 * part + 128)
            keep[part, step] = jnp.where(core == 0, low[rows], high[rows])
            send[part, step] = jnp.where(core == 0, high[rows], low[rows])

    for step in range(2):
        cols = pl.ds(step * 256, 256)
        terms(6 + step, nn(att_t[...], dmid[:, cols]))

    @pl.loop(0, 4)
    def _(pair):
        d_query, d_keys, d_vals = back_all(
            queries_of(qry, pair),
            keys_of(0, pair),
            keys_of(512, pair),
            [raised_at(index, pair)[...] for index in range(9)],
            [inverse[pair, pl.ds(2 * w[2], 2 * w[3]), :] for w in WINDOWS],
            queries_of(att, pair),
            queries_of(datt, pair),
        )
        for index, (e_off, rows, q_off, q_rows, kind) in enumerate(WINDOWS):
            step = 48 if kind == 3 else 80
            for part in range(q_rows // 48):
                dqkv[pl.ds(e_off + step * part, 48), pair_slice(0, pair)] = d_query[index][
                    48 * part : 48 * part + 48
                ]
            dqkv[pl.ds(e_off, rows), pair_slice(512, pair)] = d_keys[index]
            dqkv[pl.ds(e_off, rows), pair_slice(1024, pair)] = d_vals[index]

    leave(dqkv, dqkv_hbm)

    for step in range(6):
        cols = pl.ds(step * 256, 256)
        terms(step, nn(normed_t[...], dqkv[:, cols]))

    leave(keep, keep_hbm)
    leave(send, send_hbm)
    for copy in leaving:
        copy.wait()


def tokens_kernel(*refs):
    sources, outs, targets = refs[:7], refs[7:11], refs[11:18]
    built, padded, dnorm, sems, row_sems, out_sems = refs[18:]
    gain_in, fqkv, dqkv, dmid, cback, x, expand = targets
    copies = pull(sources[:2], targets[:2], sems)
    rows_in = []
    for part in range(4):
        rows = pl.ds(352 * part, 352)
        rows_in.append(
            pltpu.make_async_copy(sources[2].at[rows], dqkv.at[rows], row_sems.at[part])
        )
        rows_in[-1].start()
    for number in range(3, 7):
        copies.append(pltpu.make_async_copy(sources[number], targets[number], sems.at[number]))
        copies[-1].start()
    copies[0].wait()
    copies[1].wait()
    gain = gain_in[...].astype(F32).reshape(1, 512)
    for part in range(4):
        rows_in[part].wait()
        rows = pl.ds(352 * part, 352)
        dnorm[rows, :] = nt(dqkv[rows, :], fqkv[...])
    for copy in copies[2:]:
        copy.wait()
    pack = one_hot_back(expand[0:1, :], SROWS - TAIL)[:, :304]
    leaving = []
    for quad in (1, 2, 3, 0):
        out = built.at[quad]
        for (start, rows), e_off, q_off in zip(PIECES, E_OFF[quad], Q_OFF[quad]):
            spot = pl.ds(e_off, rows)
            d_norm = norm_back_fresh(x[spot, :], gain, dnorm[spot, :])
            head = d_norm[0:48] + dmid[pl.ds(q_off, 48), :].astype(F32)
            whole = jnp.concatenate([head, d_norm[48:]], axis=0) if rows > 48 else head
            if start == 0:
                out[0:TAIL, :] = whole.astype(BF16)
            else:
                padded[quad, start - TAIL : start - TAIL + rows, :] = whole.astype(BF16)
        padded[quad, 208:304, :] = cback[quad]
        out[TAIL:SROWS, :] = nn(pack, padded[quad]).astype(BF16)
        leaving.append(pltpu.make_async_copy(out, outs[quad], out_sems.at[quad]))
        leaving[-1].start()
    for copy in leaving:
        copy.wait()


def token_grads(*operands):
    return pl.pallas_call(
        tokens_kernel,
        out_shape=(jax.ShapeDtypeStruct((SROWS, 512), BF16),) * 4,
        in_specs=[HBM] * 7,
        out_specs=(HBM,) * 4,
        scratch_shapes=[pltpu.VMEM(value.shape, value.dtype) for value in operands]
        + [
            pltpu.VMEM((4, SROWS, 512), BF16),
            pltpu.VMEM((4, 304, 512), BF16),
            pltpu.VMEM((EXT, 512), F32),
            pltpu.SemaphoreType.DMA((7,)),
            pltpu.SemaphoreType.DMA((4,)),
            pltpu.SemaphoreType.DMA((4,)),
        ],
        cost_estimate=pl.CostEstimate(
            flops=2 * EXT * 1536 * 512, bytes_accessed=24 * 2**20, transcendentals=0
        ),
        compiler_params=pltpu.CompilerParams(vmem_limit_bytes=60 * 2**20),
    )(*operands)


def work(quads, fgain, mgain, cgain, fqkv, fproj, mrg, mrg_t, mw, cqkv, cproj, expand):
    scratch = [
        ((4, SROWS - TAIL, 512), BF16),
        ((8, 384), jnp.int32),
        ((EXT, 512), BF16),
        ((2, CRS, 512), BF16),
        ((512, 1536), BF16),
        ((512, 512), BF16),
        ((4, CRS, QRY), BF16),
        ((4, QRY, CRS), BF16),
        ((2048, 1024), BF16),
        ((1024, 3072), BF16),
        ((1024, 1024), BF16),
        None,
        ((EXT, 512), BF16),
        ((512, EXT), BF16),
        ((EXT, 1024), BF16),
        ((QRY, 512), BF16),
        ((QRY, 512), BF16),
        ((512, QRY), BF16),
        ((4, 4, 96, 144), BF16),
        ((4, 4, 192, 160), BF16),
        ((4, 384, 192), BF16),
        ((4, 2 * QRY, 128), F32),
        ((2, 192, 160), F32),
        ((384, 192), F32),
        ((QRY, 512), BF16),
        ((CRS, 2048), BF16),
        ((2, CRS, 128), F32),
        ((CRS, 2048), BF16),
        ((CRS, 1024), BF16),
        ((2, CRS, 128), F32),
        ((CRS, 1024), BF16),
        ((CRS, 3072), BF16),
        ((CRS, 1024), BF16),
        ((8, 384, 192), BF16),
        ((8, 384, 128), F32),
        ((QRY, 512), BF16),
        ((QRY, 512), BF16),
        ((EXT, 1536), BF16),
        ((CRS, 2048), F32),
        ((4, 96, 512), BF16),
        ((4, 8, 128, 128), BF16),
        ((4, 8, 128, 128), BF16),
        None,
    ]
    scratch = [
        pltpu.SemaphoreType.DMA((31,)) if item is None else pltpu.VMEM(*item) for item in scratch
    ]
    return pl.pallas_call(
        main_kernel,
        out_shape=(
            jax.ShapeDtypeStruct((4, 8, 128, 128), BF16),
            jax.ShapeDtypeStruct((4, 8, 128, 128), BF16),
            jax.ShapeDtypeStruct((EXT, 1536), BF16),
            jax.ShapeDtypeStruct((QRY, 512), BF16),
            jax.ShapeDtypeStruct((4, 96, 512), BF16),
            jax.ShapeDtypeStruct((EXT, 512), BF16),
        ),
        in_specs=[HBM] * 4 + [VMEM] * 3 + [HBM] * 8,
        out_specs=(HBM,) * 6,
        scratch_shapes=scratch,
        compiler_params=pltpu.CompilerParams(vmem_limit_bytes=60 * 2**20),
    )(*quads, fgain, mgain, cgain, fqkv, fproj, mrg, mrg_t, mw, cqkv, cproj, expand)


def shift(value, d_lat, d_lon):
    lats, lons = lax.axis_size("lat"), lax.axis_size("lon")
    pairs = []
    for a in range(lats):
        for b in range(lons):
            source = ((a + d_lat) % lats) * lons + (b + d_lon) % lons
            pairs.append((source, a * lons + b))
    return lax.ppermute(value, ("lat", "lon"), pairs)


def exchange(value, moves):
    lats, lons = lax.axis_size("lat"), lax.axis_size("lon")
    pairs = []
    for a in range(lats):
        for b in range(lons):
            to_a, to_b = moves(a, b)
            pairs.append((a * lons + b, to_a * lons + to_b))
    return lax.ppermute(value, ("lat", "lon"), pairs)


def spread(pieces, moves):
    total = pieces[0].astype(F32)
    for d in (1, 2, 3):
        total = total + exchange(pieces[d], lambda a, b: moves(a, b, d)).astype(F32)
    return total


def pieces_of(value, me):
    return [lax.dynamic_index_in_dim(value, me ^ d, 0, keepdims=False) for d in range(4)]


def local_grads(keep, send, lat):
    got = exchange(send, lambda a, b: (a, b ^ 1))
    pieces = []
    for mine, other in zip(pieces_of(keep, lat // 2), pieces_of(got, lat // 2)):
        pieces.append((mine.astype(F32) + other.astype(F32)).astype(BF16))
    return pieces


def local(
    tokens,
    land_sea,
    land_vec,
    fine_gain,
    fine_qkv,
    fine_proj,
    merge_gain,
    merge_weight,
    coarse_gain,
    coarse_qkv,
    coarse_proj,
    cotangent,
):
    pick, cpick, expand = jnp.asarray(PICK), jnp.asarray(CPICK), jnp.asarray(EXPAND)
    cot = cotangent.transpose(1, 2, 0, 3).reshape(72, 2, 1024)
    sends = prep(tokens.reshape(576, 512), land_sea, land_vec, cot, pick, cpick)
    quads = (sends[0], shift(sends[1], 1, 0), shift(sends[2], 0, 1), shift(sends[3], 1, 1))
    keep, send, dqkv, dmid, cback, x = work(
        quads,
        fine_gain.reshape(1, -1),
        merge_gain.reshape(1, -1),
        coarse_gain.reshape(1, -1),
        fine_qkv,
        fine_proj,
        jnp.asarray(MERGE, BF16),
        jnp.asarray(MERGE.transpose(0, 2, 1), BF16),
        merge_weight,
        coarse_qkv,
        coarse_proj,
        expand,
    )
    lat, lon = lax.axis_index("lat"), lax.axis_index("lon")
    pieces = local_grads(keep, send, lat)
    pieces, dqkv = lax.optimization_barrier((pieces, dqkv))
    back = token_grads(fine_gain, fine_qkv, dqkv, dmid, cback, x, expand)
    terms = spread(pieces, lambda a, b, d: (a ^ (2 * d), b)).astype(BF16)
    terms, _ = lax.optimization_barrier((terms, back))
    moved = (shift(back[1], -1, 0), shift(back[2], 0, -1), shift(back[3], -1, -1))
    terms = pieces_of(terms.reshape(4, 2, 128, 128), lon // 4)
    terms = spread(terms, lambda a, b, d: (a, b ^ (4 * d))).astype(BF16)
    terms, moved = lax.optimization_barrier((terms, moved))
    terms = pieces_of(terms.reshape(4, 64, 128), (lon // 2 % 2) * 2 + lat % 2)
    fine_grads = spread(terms, lambda a, b, d: (a ^ (d & 1), b ^ (d & 2)))
    grad, coarse = finish(pick, cpick, back[0], *moved)
    coarse = coarse.reshape(6, 12, 2, 1024).transpose(2, 0, 1, 3)
    return (coarse, grad.reshape(tokens.shape), fine_grads)


def solution(mesh):
    grid = P(None, "lat", "lon", None)
    placed = (grid, P("lat", "lon")) + (P(),) * 9 + (grid,)
    return jax.shard_map(
        local,
        mesh=mesh,
        in_specs=placed,
        out_specs=(grid, grid, P("lat", "lon")),
        check_vma=False,
    )
```
